32 devices in a mesh: cluster: 8 (over y, x, core), blk: 4 (over z).
Axes of the slice: x: 2, y: 2, z: 4, core: 2. Of those that a mesh axis runs over, the one named last changes fastest.
Arguments:
- codes: int32 [8, 4, 64, 512], P('cluster', 'blk'), may hold values from 0 to 255
- routes: int32 [8, 4, 512, 1], P('cluster', 'blk'), may hold values from 0 to 31; in each aligned block of 512 rows (0 to 511, 512 to 1023, ..., all dimensions but the last counted through in order) at most 32 rows name the same one
- codebook: bfloat16 [256, 1024], replicated, may hold values from -6 to 6
- centroids: bfloat16 [8, 1024], replicated, may hold values from -3 to 3
Outputs:
- nearest: float32 [8, 4, 1024], P('cluster', 'blk')
The draws below stay inside these ranges and needn't reach their ends.
Inputs may be any that keep to these rules, and one draw needn't show every extreme that they name: `routes`: within the rows of one device no destination is named more than 32 times, and in every draw some device names some destination exactly 32 times; every destination is named somewhere.
All inputs are finite; a program needn't handle non-finite values.
Results may differ from the reference program's by a relative error of at most 0.00043.
Values may be sent and summed in bfloat16 or wider, within the bound.
No kernel may reach another device: no remote copies, remote signals or barrier semaphores. Data moves between devices by JAX's collectives and lax.ppermute only.
A program may use at most 64 MiB of HBM per device.

```python
import math
import jax
import jax.numpy as jnp
import numpy as np
from jax import lax

D = 1024
SUB = 64
CW = 256
SUBDIM = 16
IN_DEV = 512
CAP = 32
SLOTS = 1024
ROWS = 4096
N_CLUSTER = 8
N_BLK = 4
DEVICES = 32


def touch_ends(array, stream_key, smallest, largest):
    index_at = [jax.random.randint(jax.random.fold_in(stream_key, axis), (), 0, length) for axis, length in enumerate(array.shape)]
    longest = array.shape.index(max(array.shape))
    next_to = index_at[:longest] + [(index_at[longest] + 1) % array.shape[longest]] + index_at[longest + 1:]
    return array.at[tuple(index_at)].set(smallest).at[tuple(next_to)].set(largest)


def rank_bounds(number_of, slope):
    weights = [(1 << 20) // math.isqrt(standing ** slope) + 1 for standing in range(1, number_of + 1)]
    width = 1 + sum(weights) // (1 << 30)
    return np.cumsum(np.array([max(1, weight // width) for weight in weights]))


def ranked(rng, shape, number_of, skew):
    listing = rank_bounds(number_of, skew)
    lot = jax.random.randint(jax.random.fold_in(rng, 1), shape, 0, int(listing[number_of - 1]))
    standing = jnp.searchsorted(jnp.asarray(listing, jnp.int32), lot, side="right")
    return jax.random.permutation(jax.random.fold_in(rng, 2), number_of)[standing].astype(jnp.int32)


def shared_out(own_key, own, number, rows, amount, top, reach, lean):
    ranking = jax.random.permutation(own_key, amount)
    packed, usual = shares(amount, rows * top, reach, lean, True), shares(amount, rows * top, reach, lean, False)
    places = jnp.arange(amount)

    def named(lengths, offset_by):
        used = int((lengths > 0).sum())
        fixed = max(1, used // 4)
        shifted = fixed + (places - fixed + offset_by * (used - fixed)) % max(1, amount - fixed)
        return jnp.zeros((amount,), jnp.int32).at[ranking[jnp.where(places < fixed, places, shifted)]].set(jnp.asarray(lengths, jnp.int32))

    lengths = jnp.where(number % 4 == 0, named(packed, number // 4), named(usual, number - number // 4 - 1))
    mixed = jax.random.permutation(jax.random.fold_in(own, 3), amount)
    source_of, receiver = mixed[0:amount // 2 * 2:2], mixed[1:amount // 2 * 2:2]
    room = jnp.minimum(lengths[source_of] - 1, reach - lengths[receiver]) // 2
    room = jnp.where((source_of == ranking[0]) | (receiver == ranking[0]) | (lengths[receiver] == 0), 0, jnp.maximum(room, 0))
    shifted = jax.random.randint(jax.random.fold_in(own, 4), (amount // 2,), 0, 1 << 20) % (room + 1)
    lengths = lengths.at[source_of].add(-shifted).at[receiver].add(shifted)
    members = jnp.searchsorted(jnp.cumsum(lengths), jnp.arange(rows * top), side="right").astype(jnp.int32)
    listing = members.reshape(top, rows).T
    listing = listing[jax.random.permutation(jax.random.fold_in(own, 1), rows)]
    offset_by = jax.random.randint(jax.random.fold_in(own, 2), (rows, 1), 0, top)
    return jnp.take_along_axis(listing, (jnp.arange(top)[None, :] + offset_by) % top, axis=1)


def shares(amount, total, bound, skew, full):
    weights = [(1 << 20) // math.isqrt(standing ** skew) + 1 for standing in range(1, amount + 1)]
    largest = bound if full else min(bound, max(-(-total // amount), total * weights[0] // sum(weights)))
    least = 1 if total - largest >= amount - 1 else 0
    given, surplus = [largest] + [least] * (amount - 1), total - largest - least * (amount - 1)
    while surplus > 0:
        movable = [i for i in range(1, amount) if given[i] < largest] or [i for i in range(1, amount) if given[i] < bound]
        pool, left = sum([weights[i] for i in movable]), surplus
        for i in movable:
            more = min(bound - given[i], max(1, left * weights[i] // pool), surplus)
            given[i] = given[i] + more
            surplus = surplus - more
    return np.array(given)


def gaussian(own_key, shape, width, reach, held_as=jnp.bfloat16):
    return jnp.clip(width * jax.random.normal(own_key, shape, jnp.float32), -reach, reach).astype(held_as)


def setup_inputs(seed: int = 0) -> dict:
    seeds = jax.random.split(jax.random.key(seed), 5)
    codes = touch_ends(ranked(seeds[0], (N_CLUSTER, N_BLK, SUB, IN_DEV), CW, 2), jax.random.fold_in(seeds[0], 3), 0, CW - 1).astype(jnp.int32)
    routes_keys = jax.random.split(jax.random.fold_in(seeds[1], 1), N_CLUSTER * N_BLK * IN_DEV // IN_DEV)
    routes_turns = jax.random.permutation(jax.random.fold_in(seeds[1], 3), N_CLUSTER * N_BLK * IN_DEV // IN_DEV)
    routes = jax.vmap(lambda own, number: shared_out(jax.random.fold_in(seeds[1], 2), own, number, IN_DEV, DEVICES, 1, CAP, 2))(routes_keys, routes_turns).reshape((N_CLUSTER, N_BLK, IN_DEV, 1))
    codebook = gaussian(seeds[2], (CW, D), 1.0, 6.0)
    centroids = gaussian(seeds[3], (N_CLUSTER, D), 0.5, 3.0)
    return dict(codes=codes, routes=routes, codebook=codebook, centroids=centroids)


def decode_device(codes_here, targets_here, codebook, centroids):
    onehot = (codes_here[:, :, None] == jnp.arange(CW, dtype=jnp.int32)[None, None, :]).astype(jnp.float32)
    table = codebook.astype(jnp.float32).reshape(CW, SUB, SUBDIM)
    residual = jnp.einsum('mrk,kmd->rmd', onehot, table, precision=lax.Precision.HIGHEST).reshape(IN_DEV, D)
    groups = targets_here // N_BLK
    select = (groups[:, None] == jnp.arange(N_CLUSTER, dtype=jnp.int32)[None, :]).astype(jnp.float32)
    centre = jnp.dot(select, centroids.astype(jnp.float32), precision=lax.Precision.HIGHEST)
    embed = centre + residual
    return (embed / jnp.sqrt(lax.optimization_barrier(jnp.sum(embed * embed, axis=1, keepdims=True)) + 1e-06)).astype(jnp.bfloat16)

def reference(codes, routes, codebook, centroids):
    codes_all = codes.reshape(DEVICES, SUB, IN_DEV)
    targets = routes.reshape(DEVICES, IN_DEV).astype(jnp.int32)
    units = lax.map(lambda pair: decode_device(pair[0], pair[1], codebook, centroids), (codes_all, targets))
    target_hot = (targets[:, :, None] == jnp.arange(DEVICES, dtype=jnp.int32)[None, None, :]).astype(jnp.int32)
    running = jnp.cumsum(target_hot, axis=1)
    position = lax.optimization_barrier(jnp.sum(target_hot * (running - 1), axis=2))
    source = jnp.arange(DEVICES, dtype=jnp.int32)[:, None] * CAP
    slot_ids = (source + position).astype(jnp.int32)
    regrouped = jnp.zeros((DEVICES, SLOTS, D), jnp.bfloat16).at[targets, slot_ids].set(units)
    filled = jnp.zeros((DEVICES, SLOTS), jnp.float32).at[targets, slot_ids].set(1.0)
    cluster_rows = regrouped.reshape(N_CLUSTER, ROWS, D)
    cluster_filled = filled.reshape(N_CLUSTER, ROWS)
    col_ids = jnp.arange(ROWS, dtype=jnp.int32)

    def block_best(index):
        group = index // N_BLK
        member = index % N_BLK
        rows_all = cluster_rows[group].astype(jnp.float32)
        marks_all = cluster_filled[group]
        start = (member * SLOTS).astype(jnp.int32)
        rows_here = lax.dynamic_slice_in_dim(rows_all, start, SLOTS, 0)
        marks_here = lax.dynamic_slice_in_dim(marks_all, start, SLOTS, 0)
        scores = jnp.dot(rows_here, rows_all.T, precision=lax.Precision.HIGHEST)
        row_ids = start + jnp.arange(SLOTS, dtype=jnp.int32)
        keep = (marks_all[None, :] > 0) & (col_ids[None, :] != row_ids[:, None])
        best = lax.optimization_barrier(jnp.max(jnp.where(keep, scores, -4.0), axis=1))
        return jnp.where(marks_here > 0, best, 0.0)
    nearest = lax.map(block_best, jnp.arange(DEVICES, dtype=jnp.int32))
    return nearest.reshape(N_CLUSTER, N_BLK, SLOTS)
```

```python
import functools

import jax
import jax.numpy as jnp
from jax import lax
from jax.experimental import pallas as pl
from jax.experimental.pallas import tpu as pltpu
from jax.sharding import PartitionSpec as P

LANES = 128
COLS = 256
LOW = -4.0
VMEM_LIMIT = 48 * 1024 * 1024


def take_lanes(table, index):
    return jnp.take_along_axis(table, index, axis=1, mode="promise_in_bounds")


def pack_kernel(devices, capacity, codes_ref, routes_ref, out_ref):
    subspaces, in_rows = codes_ref.shape
    half_rows = capacity // 2
    targets = routes_ref[...]
    hot = lax.broadcasted_iota(jnp.int32, (devices, in_rows), 0) == targets
    hot32 = jnp.where(hot, 1.0, 0.0)
    earlier = (
        lax.broadcasted_iota(jnp.int32, (in_rows, in_rows), 0)
        < lax.broadcasted_iota(jnp.int32, (in_rows, in_rows), 1)
    )
    running = jnp.dot(
        hot32.astype(jnp.bfloat16),
        jnp.where(earlier, 1.0, 0.0).astype(jnp.bfloat16),
        preferred_element_type=jnp.float32,
    )
    position = jnp.sum(hot32 * running, axis=0, keepdims=True).astype(jnp.int32)
    second = position >= half_rows
    key = targets * half_rows + jnp.where(second, position - half_rows, position)
    out_rows = devices * half_rows
    row_ids = lax.broadcasted_iota(jnp.int32, (out_rows, in_rows), 0)
    values = (codes_ref[...] + 1).astype(jnp.bfloat16)
    halves = []
    for wanted in (jnp.where(second, -1, key), jnp.where(second, key, -1)):
        move = jnp.where(row_ids == wanted, 1.0, 0.0).astype(jnp.bfloat16)
        halves.append(
            lax.dot_general(
                move, values, (((1,), (1,)), ((), ())), preferred_element_type=jnp.float32
            )
        )
    out_ref[...] = jnp.concatenate(halves, axis=1).astype(jnp.bfloat16)


def unpack_codes(block, lo_ref, hi_ref, mark_ref, tile):
    turned = jnp.transpose(block.astype(jnp.float32)).astype(jnp.int32)
    subspaces = turned.shape[0] // 2
    for half in range(2):
        part = turned[half * subspaces : (half + 1) * subspaces]
        index = jnp.maximum(part - 1, 0)
        lo_ref[tile + half] = index & (LANES - 1)
        hi_ref[tile + half] = index // LANES
        mark_ref[tile + half] = jnp.where(part[0:8] > 0, 1.0, 0.0)


def decode_tile(lo_ref, hi_ref, tile, table_ref, norms_ref, store):
    subspaces = norms_ref.shape[0]
    sub_width = table_ref.shape[0] // subspaces
    lo_all = lo_ref[tile]
    hi_all = hi_ref[tile] > 0
    squares = jnp.where(
        hi_all,
        take_lanes(norms_ref[:, LANES:], lo_all),
        take_lanes(norms_ref[:, :LANES], lo_all),
    )
    scale = lax.rsqrt(jnp.sum(squares, axis=0, keepdims=True) + 1e-06)
    for sub in range(subspaces):
        lo = jnp.broadcast_to(lo_ref[tile, sub : sub + 1, :], (sub_width, LANES))
        hi = jnp.broadcast_to(hi_ref[tile, sub : sub + 1, :], (sub_width, LANES)) > 0
        rows = slice(sub * sub_width, (sub + 1) * sub_width)
        word = jnp.where(
            hi,
            take_lanes(table_ref[rows, LANES:], lo),
            take_lanes(table_ref[rows, :LANES], lo),
        )
        store(rows, (word * scale).astype(jnp.bfloat16))


def own_kernel(
    codes_ref, codebook_ref, centroids_ref, group_ref,
    left_ref, best_ref, table_ref, norms_ref,
    units_ref, lo_ref, hi_ref, mark_ref,
):
    slots, width = left_ref.shape
    subspaces = norms_ref.shape[0]
    tiles = slots // LANES
    words = codebook_ref.shape[0]
    pick = lax.broadcasted_iota(jnp.int32, (centroids_ref.shape[0], 1), 0) == group_ref[0, 0]
    centre = jnp.sum(
        jnp.where(pick, centroids_ref[...].astype(jnp.float32), 0.0), axis=0, keepdims=True
    )
    embeds = codebook_ref[...].astype(jnp.float32) + centre
    table = jnp.transpose(embeds)
    table_ref[...] = table
    norms_ref[...] = jnp.sum((table * table).reshape(subspaces, width // subspaces, words), axis=1)
    for group in range(tiles // 2):
        unpack_codes(
            codes_ref[group * LANES : (group + 1) * LANES, :], lo_ref, hi_ref, mark_ref, 2 * group
        )

    def one_tile(tile, _):
        start = pl.multiple_of(tile * LANES, LANES)

        def store(rows, value):
            units_ref[rows, pl.ds(start, LANES)] = value

        decode_tile(lo_ref, hi_ref, tile, table_ref, norms_ref, store)
        left_ref[pl.ds(start, LANES), :] = jnp.transpose(units_ref[:, pl.ds(start, LANES)])
        return 0

    lax.fori_loop(0, tiles, one_tile, 0)

    best_ref[...] = jnp.full(best_ref.shape, LOW, jnp.float32)
    row_ids = lax.broadcasted_iota(jnp.int32, (slots, LANES), 0)
    lane_ids = lax.broadcasted_iota(jnp.int32, (slots, LANES), 1)

    def score(step, _):
        start = pl.multiple_of(step * COLS, COLS)
        scores = jnp.dot(
            left_ref[...], units_ref[:, pl.ds(start, COLS)], preferred_element_type=jnp.float32
        )
        best = best_ref[...]
        for part in range(COLS // LANES):
            filled = mark_ref[step * (COLS // LANES) + part][0:1, :] > 0
            keep = filled & (row_ids != lane_ids + (start + part * LANES))
            best = jnp.maximum(
                best, jnp.where(keep, scores[:, part * LANES : (part + 1) * LANES], LOW)
            )
        best_ref[...] = best
        return 0

    lax.fori_loop(0, slots // COLS, score, 0)


def rest_kernel(
    capacity, codes_ref, others_ref, left_ref, start_ref, table_ref, norms_ref,
    out_ref,
    units_ref, lo_ref, hi_ref, mark_ref, best_ref,
):
    slots, width = left_ref.shape
    tiles = slots // LANES
    columns = units_ref.shape[1]
    best_ref[...] = start_ref[...]

    def unpack(group, _):
        start = pl.multiple_of(group * LANES, LANES)
        unpack_codes(others_ref[pl.ds(start, LANES), :], lo_ref, hi_ref, mark_ref, 2 * group)
        return 0

    lax.fori_loop(0, others_ref.shape[0] // LANES, unpack, 0)

    def one_tile(tile, _):
        start = pl.multiple_of(tile * LANES, LANES)

        def store(rows, value):
            units_ref[rows, pl.ds(start, LANES)] = value

        decode_tile(lo_ref, hi_ref, tile, table_ref, norms_ref, store)
        return 0

    lax.fori_loop(0, columns // LANES, one_tile, 0)

    def score(step, _):
        start = pl.multiple_of(step * COLS, COLS)
        scores = jnp.dot(
            left_ref[...], units_ref[:, pl.ds(start, COLS)], preferred_element_type=jnp.float32
        )
        best = best_ref[...]
        for part in range(COLS // LANES):
            filled = mark_ref[step * (COLS // LANES) + part][0:1, :] > 0
            best = jnp.maximum(
                best, jnp.where(filled, scores[:, part * LANES : (part + 1) * LANES], LOW)
            )
        best_ref[...] = best
        return 0

    lax.fori_loop(0, columns // COLS, score, 0)

    half_rows = capacity // 2
    maxima = []
    for group in range(tiles // 2):
        turned = jnp.transpose(codes_ref[group * LANES : (group + 1) * LANES, :].astype(jnp.float32))
        subspaces = turned.shape[0] // 2
        for half in range(2):
            tile = 2 * group + half
            best = jnp.max(
                jnp.transpose(best_ref[tile * LANES : (tile + 1) * LANES, :]),
                axis=0, keepdims=True,
            )
            filled = turned[half * subspaces : half * subspaces + 1] > 0
            maxima.append(jnp.where(filled, best, 0.0))
    spread = [
        jnp.concatenate([maxima[2 * (row // 2) + half] for row in range(tiles)], axis=0)
        for half in range(2)
    ]
    lane = lax.broadcasted_iota(jnp.int32, (tiles, LANES), 1)
    row = lax.broadcasted_iota(jnp.int32, (tiles, LANES), 0)
    source = (LANES // 2) * (row % 2) + half_rows * (lane // capacity) + lane % half_rows
    upper = (lane % capacity) >= half_rows
    out_ref[...] = jnp.where(
        upper, take_lanes(spread[1], source), take_lanes(spread[0], source)
    )


def on_device(codes, routes, codebook, centroids):
    groups = lax.axis_size("cluster")
    members = lax.axis_size("blk")
    devices = groups * members
    subspaces, in_rows = codes.shape[2:]
    capacity = 2 * in_rows // devices
    slots = devices * capacity
    tiles = slots // LANES
    words, width = codebook.shape
    bf16, f32, i32 = jnp.bfloat16, jnp.float32, jnp.int32
    params = pltpu.CompilerParams(vmem_limit_bytes=VMEM_LIMIT)

    packed = pl.pallas_call(
        functools.partial(pack_kernel, devices, capacity),
        out_shape=jax.ShapeDtypeStruct((in_rows, 2 * subspaces), bf16),
        compiler_params=params,
        name="pack_rows",
    )(codes[0, 0], routes.reshape(1, in_rows))
    own = lax.all_to_all(packed, ("cluster", "blk"), split_axis=0, concat_axis=0, tiled=True)
    others = [
        lax.ppermute(own, "blk", [(i, (i + shift) % members) for i in range(members)])
        for shift in range(1, members)
    ]
    group = lax.axis_index("cluster").astype(i32).reshape(1, 1)
    left, best, table, norms = pl.pallas_call(
        own_kernel,
        out_shape=(
            jax.ShapeDtypeStruct((slots, width), bf16),
            jax.ShapeDtypeStruct((slots, LANES), f32),
            jax.ShapeDtypeStruct((width, words), f32),
            jax.ShapeDtypeStruct((subspaces, words), f32),
        ),
        in_specs=[pl.BlockSpec(memory_space=pltpu.VMEM)] * 3
        + [pl.BlockSpec(memory_space=pltpu.SMEM)],
        scratch_shapes=[
            pltpu.VMEM((width, slots), bf16),
            pltpu.VMEM((tiles, subspaces, LANES), i32),
            pltpu.VMEM((tiles, subspaces, LANES), i32),
            pltpu.VMEM((tiles, 8, LANES), f32),
        ],
        compiler_params=params,
        cost_estimate=pl.CostEstimate(
            flops=2 * slots * slots * width, bytes_accessed=8 * slots * width, transcendentals=0
        ),
        name="own_rows",
    )(own, codebook, centroids, group)
    columns = (members - 1) * slots
    nearest = pl.pallas_call(
        functools.partial(rest_kernel, capacity),
        out_shape=jax.ShapeDtypeStruct((tiles, LANES), f32),
        scratch_shapes=[
            pltpu.VMEM((width, columns), bf16),
            pltpu.VMEM((columns // LANES, subspaces, LANES), i32),
            pltpu.VMEM((columns // LANES, subspaces, LANES), i32),
            pltpu.VMEM((columns // LANES, 8, LANES), f32),
            pltpu.VMEM((slots, LANES), f32),
        ],
        compiler_params=params,
        cost_estimate=pl.CostEstimate(
            flops=2 * slots * columns * width, bytes_accessed=8 * slots * width, transcendentals=0
        ),
        name="rest_rows",
    )(own, jnp.concatenate(others, axis=0), left, best, table, norms)
    return nearest.reshape(1, 1, slots)


def solution(mesh):
    in_specs = (P("cluster", "blk", None, None), P("cluster", "blk", None, None), P(), P())
    out_specs = P("cluster", "blk", None)
    return jax.shard_map(
        on_device, mesh=mesh, in_specs=in_specs, out_specs=out_specs, check_vma=False
    )
```

```python
import functools

import jax
import jax.numpy as jnp
from jax import lax
from jax.experimental import pallas as pl
from jax.experimental.pallas import tpu as pltpu
from jax.sharding import PartitionSpec as P

LANES = 128
COLS = 256
LOW = -4.0
VMEM_LIMIT = 48 * 1024 * 1024
PARAMS = pltpu.CompilerParams(vmem_limit_bytes=VMEM_LIMIT)


def take_lanes(table, index):
    return jnp.take_along_axis(table, index, axis=1, mode="promise_in_bounds")


def pack_kernel(devices, capacity, codes_ref, routes_ref, out_ref):
    subspaces, in_rows = codes_ref.shape
    half_rows = capacity // 2
    targets = routes_ref[...]
    hot = lax.broadcasted_iota(jnp.int32, (devices, in_rows), 0) == targets
    hot32 = jnp.where(hot, 1.0, 0.0)
    earlier = (
        lax.broadcasted_iota(jnp.int32, (in_rows, in_rows), 0)
        < lax.broadcasted_iota(jnp.int32, (in_rows, in_rows), 1)
    )
    running = jnp.dot(
        hot32.astype(jnp.bfloat16),
        jnp.where(earlier, 1.0, 0.0).astype(jnp.bfloat16),
        preferred_element_type=jnp.float32,
    )
    position = jnp.sum(hot32 * running, axis=0, keepdims=True).astype(jnp.int32)
    second = position >= half_rows
    key = targets * half_rows + jnp.where(second, position - half_rows, position)
    out_rows = devices * half_rows
    row_ids = lax.broadcasted_iota(jnp.int32, (out_rows, in_rows), 0)
    values = (codes_ref[...] + 1).astype(jnp.bfloat16)
    halves = []
    for wanted in (jnp.where(second, -1, key), jnp.where(second, key, -1)):
        move = jnp.where(row_ids == wanted, 1.0, 0.0).astype(jnp.bfloat16)
        halves.append(
            lax.dot_general(
                move, values, (((1,), (1,)), ((), ())), preferred_element_type=jnp.float32
            )
        )
    out_ref[...] = jnp.concatenate(halves, axis=1).astype(jnp.bfloat16)


def table_kernel(group_ref, codebook_ref, centroids_ref, table_ref, norms_ref):
    words, width = codebook_ref.shape
    subspaces = norms_ref.shape[0]
    pick = lax.broadcasted_iota(jnp.int32, (centroids_ref.shape[0], 1), 0) == group_ref[0, 0]
    centre = jnp.sum(
        jnp.where(pick, centroids_ref[...].astype(jnp.float32), 0.0), axis=0, keepdims=True
    )
    table = jnp.transpose(codebook_ref[...].astype(jnp.float32) + centre)
    table_ref[...] = table
    norms_ref[...] = jnp.sum((table * table).reshape(subspaces, width // subspaces, words), axis=1)


def owner_block(codes_ref, owner, owners):
    parts = [
        codes_ref[pl.ds(pl.multiple_of((part * owners + owner) * 16, 16), 16), :]
        for part in range(LANES // 16)
    ]
    return jnp.concatenate(parts, axis=0)


def unpack_codes(block, lo_ref, hi_ref, mark_ref, group):
    turned = jnp.transpose(block.astype(jnp.float32)).astype(jnp.int32)
    subspaces = turned.shape[0] // 2
    for half in range(2):
        part = turned[half * subspaces : (half + 1) * subspaces]
        index = jnp.maximum(part - 1, 0)
        lo_ref[2 * group + half] = index & (LANES - 1)
        hi_ref[2 * group + half] = index // LANES
        mark_ref[2 * group + half] = jnp.where(part[0:8] > 0, 1.0, 0.0)


def tile_scale(lo, hi, norms_ref):
    squares = jnp.where(
        hi > 0,
        take_lanes(norms_ref[:, LANES:], lo),
        take_lanes(norms_ref[:, :LANES], lo),
    )
    return lax.rsqrt(jnp.sum(squares, axis=0, keepdims=True) + 1e-06)


def stage_tile(lo_ref, hi_ref, tile, now_ref, half, norms_ref):
    lo, hi = lo_ref[tile], hi_ref[tile]
    now_ref[half, 0] = lo
    now_ref[half, 1] = hi
    return tile_scale(lo, hi, norms_ref)


def decode_tile(lo_ref, hi_ref, tile, now_ref, table_ref, norms_ref, units_ref, start):
    subspaces = norms_ref.shape[0]
    sub_width = table_ref.shape[0] // subspaces
    start = pl.multiple_of(start, LANES)
    scale = stage_tile(lo_ref, hi_ref, tile, now_ref, 0, norms_ref)
    for sub in range(subspaces):
        lo = jnp.broadcast_to(now_ref[0, 0, sub : sub + 1, :], (sub_width, LANES))
        hi = jnp.broadcast_to(now_ref[0, 1, sub : sub + 1, :], (sub_width, LANES)) > 0
        rows = slice(sub * sub_width, (sub + 1) * sub_width)
        word = jnp.where(
            hi,
            take_lanes(table_ref[rows, LANES:], lo),
            take_lanes(table_ref[rows, :LANES], lo),
        )
        units_ref[rows, pl.ds(start, LANES)] = (word * scale).astype(jnp.bfloat16)


def near_kernel(
    place_ref, codes_ref, table_ref, norms_ref, units_ref, mark_ref,
    lo_ref, hi_ref, now_ref,
):
    owners = units_ref.shape[1] // COLS
    for turn in range(owners):
        owner = lax.rem(place_ref[0, 0] + turn, owners)
        unpack_codes(owner_block(codes_ref, owner, owners), lo_ref, hi_ref, mark_ref, turn)

    def one_tile(tile, _):
        decode_tile(lo_ref, hi_ref, tile, now_ref, table_ref, norms_ref, units_ref, tile * LANES)
        return 0

    lax.fori_loop(0, 2 * owners, one_tile, 0)


def last_kernel(sizes, place_ref, *refs):
    capacity, clusters, members = sizes
    more = len(refs) - 12
    codes_refs = refs[:more]
    (
        near_ref, near_mark_ref, table_ref, norms_ref, out_ref,
        left_ref, units_ref, best_ref, lo_ref, hi_ref, mark_ref, now_ref,
    ) = refs[more:]
    slots, width = left_ref.shape
    groups = more + 1
    owners = units_ref.shape[1] // slots
    place = place_ref[0, 0]

    for turn in range(owners):
        owner = lax.rem(place + turn, owners)
        for which in range(more):
            unpack_codes(
                owner_block(codes_refs[which], owner, owners),
                lo_ref, hi_ref, mark_ref, turn * groups + which + 1,
            )
        for half in range(2):
            mark_ref[2 * turn * groups + half] = near_mark_ref[2 * turn + half]
        units_ref[:, turn * slots : turn * slots + COLS] = near_ref[
            :, turn * COLS : (turn + 1) * COLS
        ]

    per_turn = slots // LANES
    for turn in range(owners):

        def one_tile(tile, _):
            tile = tile + turn * per_turn
            decode_tile(
                lo_ref, hi_ref, tile, now_ref, table_ref, norms_ref, units_ref, tile * LANES
            )
            return 0

        lax.fori_loop(2, per_turn, one_tile, 0)

    def turn_left(tile, _):
        start = pl.multiple_of(tile * LANES, LANES)
        left_ref[pl.ds(start, LANES), :] = jnp.transpose(units_ref[:, pl.ds(start, LANES)])
        return 0

    lax.fori_loop(0, per_turn, turn_left, 0)
    best_ref[...] = jnp.full(best_ref.shape, LOW, jnp.float32)

    def score(step, _):
        start = pl.multiple_of(step * COLS, COLS)
        scores = jnp.dot(
            left_ref[...], units_ref[:, pl.ds(start, COLS)], preferred_element_type=jnp.float32
        )
        best = best_ref[...]
        row_ids = lax.broadcasted_iota(jnp.int32, (slots, LANES), 0)
        lane_ids = lax.broadcasted_iota(jnp.int32, (slots, LANES), 1)
        for part in range(COLS // LANES):
            filled = mark_ref[step * (COLS // LANES) + part][0:1, :] > 0
            keep = filled & (row_ids != lane_ids + (start + part * LANES))
            best = jnp.maximum(
                best, jnp.where(keep, scores[:, part * LANES : (part + 1) * LANES], LOW)
            )
        best_ref[...] = best
        return 0

    lax.fori_loop(0, owners * groups, score, 0)

    half_rows = capacity // 2
    tiles = slots // LANES
    lane = lax.broadcasted_iota(jnp.int32, (tiles, LANES), 1)
    slot = lax.broadcasted_iota(jnp.int32, (tiles, LANES), 0) * LANES + lane
    source, within = slot // capacity, slot % capacity
    turn = lax.rem(place - source % members + members, members)
    own_row = (turn * clusters + source // members) * half_rows + within % half_rows
    tile_of = 2 * (own_row // LANES) + within // half_rows
    result = jnp.zeros((tiles, LANES), jnp.float32)
    for tile in range(tiles):
        best = jnp.max(
            jnp.transpose(best_ref[tile * LANES : (tile + 1) * LANES, :]), axis=0, keepdims=True
        )
        mark = mark_ref[tile]
        best = jnp.where(mark[0:1, :] > 0, best, 0.0)
        result = jnp.where(
            tile_of == tile,
            take_lanes(jnp.broadcast_to(best, (tiles, LANES)), own_row % LANES),
            result,
        )
    out_ref[...] = result


def on_device(codes, routes, codebook, centroids):
    clusters = lax.axis_size("cluster")
    members = lax.axis_size("blk")
    devices = clusters * members
    subspaces, in_rows = codes.shape[2:]
    capacity = 2 * in_rows // devices
    half_rows = capacity // 2
    slots = devices * capacity
    tiles = slots // LANES
    groups = slots // COLS
    words, width = codebook.shape
    bf16, f32, i32 = jnp.bfloat16, jnp.float32, jnp.int32
    smem = pl.BlockSpec(memory_space=pltpu.SMEM)
    vmem = pl.BlockSpec(memory_space=pltpu.VMEM)

    packed = pl.pallas_call(
        functools.partial(pack_kernel, devices, capacity),
        out_shape=jax.ShapeDtypeStruct((in_rows, 2 * subspaces), bf16),
        compiler_params=PARAMS,
        name="pack_rows",
    )(codes[0, 0], routes.reshape(1, in_rows))
    here = lax.all_to_all(packed, "cluster", split_axis=0, concat_axis=0, tiled=True)
    there = [
        lax.ppermute(here, "blk", [(i, (i + shift) % members) for i in range(members)])
        for shift in range(1, members)
    ]
    if half_rows == 16 and clusters * half_rows == LANES:
        blocks = [here, *there]
    else:
        every = jnp.stack([here, *there]).reshape(members, clusters, members, half_rows, LANES)
        every = every.transpose(2, 0, 1, 3, 4).reshape(members, groups, LANES // 16, 16, LANES)
        every = every.transpose(1, 2, 0, 3, 4).reshape(groups, members * LANES, LANES)
        blocks = list(every)

    place = lax.axis_index("blk").astype(i32).reshape(1, 1)
    group = lax.axis_index("cluster").astype(i32).reshape(1, 1)
    table, norms = pl.pallas_call(
        table_kernel,
        out_shape=(
            jax.ShapeDtypeStruct((width, words), f32),
            jax.ShapeDtypeStruct((subspaces, words), f32),
        ),
        in_specs=[smem, vmem, vmem],
        compiler_params=PARAMS,
        cost_estimate=pl.CostEstimate(
            flops=4 * words * width, bytes_accessed=6 * words * width, transcendentals=0
        ),
        name="word_table",
    )(group, codebook, centroids)
    near, near_mark = pl.pallas_call(
        near_kernel,
        out_shape=(
            jax.ShapeDtypeStruct((width, members * COLS), bf16),
            jax.ShapeDtypeStruct((2 * members, 8, LANES), f32),
        ),
        in_specs=[smem, vmem, vmem, vmem],
        scratch_shapes=[
            pltpu.VMEM((2 * members, subspaces, LANES), i32),
            pltpu.VMEM((2 * members, subspaces, LANES), i32),
            pltpu.VMEM((1, 2, subspaces, LANES), i32),
        ],
        compiler_params=PARAMS,
        cost_estimate=pl.CostEstimate(
            flops=4 * members * COLS * width,
            bytes_accessed=4 * members * COLS * width,
            transcendentals=0,
        ),
        name="near_rows",
    )(place, blocks[0], table, norms)
    more = groups - 1
    nearest = pl.pallas_call(
        functools.partial(last_kernel, (capacity, clusters, members)),
        out_shape=jax.ShapeDtypeStruct((tiles, LANES), f32),
        in_specs=[smem] + [vmem] * (more + 4),
        scratch_shapes=[
            pltpu.VMEM((slots, width), bf16),
            pltpu.VMEM((width, members * slots), bf16),
            pltpu.VMEM((slots, LANES), f32),
            pltpu.VMEM((2 * members * groups, subspaces, LANES), i32),
            pltpu.VMEM((2 * members * groups, subspaces, LANES), i32),
            pltpu.VMEM((2 * members * groups, 8, LANES), f32),
            pltpu.VMEM((1, 2, subspaces, LANES), i32),
        ],
        compiler_params=PARAMS,
        cost_estimate=pl.CostEstimate(
            flops=2 * slots * members * slots * width,
            bytes_accessed=8 * slots * width,
            transcendentals=0,
        ),
        name="all_rows",
    )(place, *blocks[1:], near, near_mark, table, norms)
    return nearest.reshape(1, 1, slots)


def solution(mesh):
    in_specs = (P("cluster", "blk", None, None), P("cluster", "blk", None, None), P(), P())
    out_specs = P("cluster", "blk", None)
    return jax.shard_map(
        on_device, mesh=mesh, in_specs=in_specs, out_specs=out_specs, check_vma=False
    )
```

```python
import functools

import jax
import jax.numpy as jnp
from jax import lax
from jax.experimental import pallas as pl
from jax.experimental.pallas import tpu as pltpu
from jax.sharding import PartitionSpec as P

LANES = 128
COLS = 256
STEP = 512
LOW = -4.0
VMEM_LIMIT = 48 * 1024 * 1024
PARAMS = pltpu.CompilerParams(vmem_limit_bytes=VMEM_LIMIT)


LANE_LOOKUP = lax.GatherDimensionNumbers(
    offset_dims=(),
    collapsed_slice_dims=(1,),
    start_index_map=(1,),
    operand_batching_dims=(0,),
    start_indices_batching_dims=(0,),
)


def take_lanes(table, index):
    return lax.gather(
        table, index[:, :, None], LANE_LOOKUP, (1, 1),
        mode=lax.GatherScatterMode.PROMISE_IN_BOUNDS,
    )


def pack_kernel(devices, capacity, codes_ref, routes_ref, out_ref):
    subspaces, in_rows = codes_ref.shape
    half_rows = capacity // 2
    targets = routes_ref[...]
    hot = lax.broadcasted_iota(jnp.int32, (devices, in_rows), 0) == targets
    hot32 = jnp.where(hot, 1.0, 0.0)
    earlier = (
        lax.broadcasted_iota(jnp.int32, (in_rows, in_rows), 0)
        < lax.broadcasted_iota(jnp.int32, (in_rows, in_rows), 1)
    )
    running = jnp.dot(
        hot32.astype(jnp.bfloat16),
        jnp.where(earlier, 1.0, 0.0).astype(jnp.bfloat16),
        preferred_element_type=jnp.float32,
    )
    position = jnp.sum(hot32 * running, axis=0, keepdims=True).astype(jnp.int32)
    second = position >= half_rows
    key = targets * half_rows + jnp.where(second, position - half_rows, position)
    out_rows = devices * half_rows
    row_ids = lax.broadcasted_iota(jnp.int32, (out_rows, in_rows), 0)
    values = (codes_ref[...] + 1).astype(jnp.bfloat16)
    halves = []
    for wanted in (jnp.where(second, -1, key), jnp.where(second, key, -1)):
        move = jnp.where(row_ids == wanted, 1.0, 0.0).astype(jnp.bfloat16)
        halves.append(
            lax.dot_general(
                move, values, (((1,), (1,)), ((), ())), preferred_element_type=jnp.float32
            )
        )
    out_ref[...] = jnp.concatenate(halves, axis=1).astype(jnp.bfloat16)


def table_kernel(group_ref, codebook_ref, centroids_ref, words_ref, centre_ref, norms_ref):
    words, width = codebook_ref.shape
    subspaces = norms_ref.shape[0]
    pick = lax.broadcasted_iota(jnp.int32, (centroids_ref.shape[0], 1), 0) == group_ref[0, 0]
    centre = jnp.sum(
        jnp.where(pick, centroids_ref[...].astype(jnp.float32), 0.0), axis=0, keepdims=True
    )
    centre = jnp.transpose(jnp.broadcast_to(centre, (LANES, width)))
    centre_ref[...] = centre
    turned = jnp.transpose(codebook_ref[...].astype(jnp.float32))
    words_ref[...] = turned.astype(jnp.bfloat16)
    for half in range(words // LANES):
        lanes = slice(half * LANES, (half + 1) * LANES)
        table = turned[:, lanes] + centre
        norms_ref[:, lanes] = jnp.sum(
            (table * table).reshape(subspaces, width // subspaces, LANES), axis=1
        )


def owner_block(codes_ref, owner, owners):
    parts = [
        codes_ref[pl.ds(pl.multiple_of((part * owners + owner) * 16, 16), 16), :]
        for part in range(LANES // 16)
    ]
    return jnp.concatenate(parts, axis=0)


def unpack_codes(block, lo_ref, hi_ref, mark_ref, group):
    turned = jnp.transpose(block.astype(jnp.float32)).astype(jnp.int32)
    subspaces = turned.shape[0] // 2
    for half in range(2):
        part = turned[half * subspaces : (half + 1) * subspaces]
        index = jnp.maximum(part - 1, 0)
        lo_ref[2 * group + half] = index & (LANES - 1)
        hi_ref[2 * group + half] = index // LANES
        mark_ref[2 * group + half] = jnp.where(part[0:8] > 0, 1.0, 0.0)


def tile_scale(lo, hi, norms_ref):
    squares = jnp.where(
        hi > 0,
        take_lanes(norms_ref[:, LANES:], lo),
        take_lanes(norms_ref[:, :LANES], lo),
    )
    return lax.rsqrt(jnp.sum(squares, axis=0, keepdims=True) + 1e-06)


def stage_tile(lo_ref, hi_ref, tile, now_ref, half, norms_ref):
    lo, hi = lo_ref[tile], hi_ref[tile]
    now_ref[half, 0] = lo
    now_ref[half, 1] = hi
    return tile_scale(lo, hi, norms_ref)


def decode_tile(
    lo_ref, hi_ref, tile, now_ref, words_ref, centre_ref, norms_ref, units_ref, start
):
    subspaces = norms_ref.shape[0]
    sub_width = words_ref.shape[0] // subspaces
    start = pl.multiple_of(start, LANES)
    scale = stage_tile(lo_ref, hi_ref, tile, now_ref, 0, norms_ref)
    for sub in range(subspaces):
        lo = jnp.broadcast_to(now_ref[0, 0, sub : sub + 1, :], (sub_width, LANES))
        hi = jnp.broadcast_to(now_ref[0, 1, sub : sub + 1, :], (sub_width, LANES)) > 0
        lo = lo.astype(jnp.int16)
        rows = slice(sub * sub_width, (sub + 1) * sub_width)
        lower = take_lanes(words_ref[rows, :LANES], lo).astype(jnp.float32)
        upper = take_lanes(words_ref[rows, LANES:], lo).astype(jnp.float32)
        embed = jnp.where(hi, upper, lower) + centre_ref[rows, :]
        units_ref[rows, pl.ds(start, LANES)] = (embed * scale).astype(jnp.bfloat16)


def near_kernel(
    place_ref, codes_ref, words_ref, centre_ref, norms_ref, units_ref, mark_ref,
    lo_ref, hi_ref, now_ref,
):
    owners = units_ref.shape[1] // COLS
    for turn in range(owners):
        owner = lax.rem(place_ref[0, 0] + turn, owners)
        unpack_codes(owner_block(codes_ref, owner, owners), lo_ref, hi_ref, mark_ref, turn)

    def one_tile(tile, _):
        decode_tile(
            lo_ref, hi_ref, tile, now_ref, words_ref, centre_ref, norms_ref, units_ref,
            tile * LANES,
        )
        return 0

    lax.fori_loop(0, 2 * owners, one_tile, 0)


def last_kernel(sizes, place_ref, *refs):
    capacity, clusters, members = sizes
    more = len(refs) - 13
    codes_refs = refs[:more]
    (
        near_ref, near_mark_ref, words_ref, centre_ref, norms_ref, out_ref,
        left_ref, units_ref, best_ref, lo_ref, hi_ref, mark_ref, now_ref,
    ) = refs[more:]
    slots, width = left_ref.shape
    groups = more + 1
    owners = units_ref.shape[1] // slots
    place = place_ref[0, 0]

    for turn in range(owners):
        owner = lax.rem(place + turn, owners)
        for which in range(more):
            unpack_codes(
                owner_block(codes_refs[which], owner, owners),
                lo_ref, hi_ref, mark_ref, turn * groups + which + 1,
            )
        for half in range(2):
            mark_ref[2 * turn * groups + half] = near_mark_ref[2 * turn + half]
        units_ref[:, turn * slots : turn * slots + COLS] = near_ref[
            :, turn * COLS : (turn + 1) * COLS
        ]

    per_turn = slots // LANES
    for turn in range(owners):

        def one_tile(tile, _):
            tile = tile + turn * per_turn
            decode_tile(
                lo_ref, hi_ref, tile, now_ref, words_ref, centre_ref, norms_ref, units_ref,
                tile * LANES,
            )
            return 0

        lax.fori_loop(2, per_turn, one_tile, 0)

    def turn_left(tile, _):
        start = pl.multiple_of(tile * LANES, LANES)
        left_ref[pl.ds(start, LANES), :] = jnp.transpose(units_ref[:, pl.ds(start, LANES)])
        return 0

    lax.fori_loop(0, per_turn, turn_left, 0)
    best_ref[...] = jnp.full(best_ref.shape, LOW, jnp.float32)

    def score(step, _, own):
        start = pl.multiple_of(step * STEP, STEP)
        scores = jnp.dot(
            left_ref[...], units_ref[:, pl.ds(start, STEP)], preferred_element_type=jnp.float32
        )
        best = best_ref[...]
        for part in range(STEP // LANES):
            keep = mark_ref[step * (STEP // LANES) + part][0:1, :] > 0
            if own:
                row_ids = lax.broadcasted_iota(jnp.int32, (slots, LANES), 0)
                lane_ids = lax.broadcasted_iota(jnp.int32, (slots, LANES), 1)
                keep = keep & (row_ids != lane_ids + (start + part * LANES))
            best = jnp.maximum(
                best, jnp.where(keep, scores[:, part * LANES : (part + 1) * LANES], LOW)
            )
        best_ref[...] = best
        return 0

    own_steps = slots // STEP
    lax.fori_loop(0, own_steps, functools.partial(score, own=True), 0)
    lax.fori_loop(own_steps, owners * own_steps, functools.partial(score, own=False), 0)

    half_rows = capacity // 2
    tiles = slots // LANES
    lane = lax.broadcasted_iota(jnp.int32, (tiles, LANES), 1)
    slot = lax.broadcasted_iota(jnp.int32, (tiles, LANES), 0) * LANES + lane
    source, within = slot // capacity, slot % capacity
    turn = lax.rem(place - source % members + members, members)
    own_row = (turn * clusters + source // members) * half_rows + within % half_rows
    tile_of = 2 * (own_row // LANES) + within // half_rows
    result = jnp.zeros((tiles, LANES), jnp.float32)
    for tile in range(tiles):
        best = jnp.max(
            jnp.transpose(best_ref[tile * LANES : (tile + 1) * LANES, :]), axis=0, keepdims=True
        )
        mark = mark_ref[tile]
        best = jnp.where(mark[0:1, :] > 0, best, 0.0)
        result = jnp.where(
            tile_of == tile,
            take_lanes(jnp.broadcast_to(best, (tiles, LANES)), own_row % LANES),
            result,
        )
    out_ref[...] = result


def on_device(codes, routes, codebook, centroids):
    clusters = lax.axis_size("cluster")
    members = lax.axis_size("blk")
    devices = clusters * members
    subspaces, in_rows = codes.shape[2:]
    capacity = 2 * in_rows // devices
    half_rows = capacity // 2
    slots = devices * capacity
    tiles = slots // LANES
    groups = slots // COLS
    words, width = codebook.shape
    bf16, f32, i32 = jnp.bfloat16, jnp.float32, jnp.int32
    smem = pl.BlockSpec(memory_space=pltpu.SMEM)
    vmem = pl.BlockSpec(memory_space=pltpu.VMEM)

    packed = pl.pallas_call(
        functools.partial(pack_kernel, devices, capacity),
        out_shape=jax.ShapeDtypeStruct((in_rows, 2 * subspaces), bf16),
        compiler_params=PARAMS,
        name="pack_rows",
    )(codes[0, 0], routes.reshape(1, in_rows))
    here = lax.all_to_all(packed, "cluster", split_axis=0, concat_axis=0, tiled=True)
    there = [
        lax.ppermute(here, "blk", [(i, (i + shift) % members) for i in range(members)])
        for shift in range(1, members)
    ]
    if half_rows == 16 and clusters * half_rows == LANES:
        blocks = [here, *there]
    else:
        every = jnp.stack([here, *there]).reshape(members, clusters, members, half_rows, LANES)
        every = every.transpose(2, 0, 1, 3, 4).reshape(members, groups, LANES // 16, 16, LANES)
        every = every.transpose(1, 2, 0, 3, 4).reshape(groups, members * LANES, LANES)
        blocks = list(every)

    place = lax.axis_index("blk").astype(i32).reshape(1, 1)
    group = lax.axis_index("cluster").astype(i32).reshape(1, 1)
    table = pl.pallas_call(
        table_kernel,
        out_shape=(
            jax.ShapeDtypeStruct((width, words), bf16),
            jax.ShapeDtypeStruct((width, LANES), f32),
            jax.ShapeDtypeStruct((subspaces, words), f32),
        ),
        in_specs=[smem, vmem, vmem],
        compiler_params=PARAMS,
        cost_estimate=pl.CostEstimate(
            flops=4 * words * width, bytes_accessed=6 * words * width, transcendentals=0
        ),
        name="word_table",
    )(group, codebook, centroids)
    near, near_mark = pl.pallas_call(
        near_kernel,
        out_shape=(
            jax.ShapeDtypeStruct((width, members * COLS), bf16),
            jax.ShapeDtypeStruct((2 * members, 8, LANES), f32),
        ),
        in_specs=[smem] + [vmem] * 4,
        scratch_shapes=[
            pltpu.VMEM((2 * members, subspaces, LANES), i32),
            pltpu.VMEM((2 * members, subspaces, LANES), i32),
            pltpu.VMEM((1, 2, subspaces, LANES), i32),
        ],
        compiler_params=PARAMS,
        cost_estimate=pl.CostEstimate(
            flops=4 * members * COLS * width,
            bytes_accessed=4 * members * COLS * width,
            transcendentals=0,
        ),
        name="near_rows",
    )(place, blocks[0], *table)
    more = groups - 1
    nearest = pl.pallas_call(
        functools.partial(last_kernel, (capacity, clusters, members)),
        out_shape=jax.ShapeDtypeStruct((tiles, LANES), f32),
        in_specs=[smem] + [vmem] * (more + 5),
        scratch_shapes=[
            pltpu.VMEM((slots, width), bf16),
            pltpu.VMEM((width, members * slots), bf16),
            pltpu.VMEM((slots, LANES), f32),
            pltpu.VMEM((2 * members * groups, subspaces, LANES), i32),
            pltpu.VMEM((2 * members * groups, subspaces, LANES), i32),
            pltpu.VMEM((2 * members * groups, 8, LANES), f32),
            pltpu.VMEM((1, 2, subspaces, LANES), i32),
        ],
        compiler_params=PARAMS,
        cost_estimate=pl.CostEstimate(
            flops=2 * slots * members * slots * width,
            bytes_accessed=8 * slots * width,
            transcendentals=0,
        ),
        name="all_rows",
    )(place, *blocks[1:], near, near_mark, *table)
    return nearest.reshape(1, 1, slots)


def solution(mesh):
    in_specs = (P("cluster", "blk", None, None), P("cluster", "blk", None, None), P(), P())
    out_specs = P("cluster", "blk", None)
    return jax.shard_map(
        on_device, mesh=mesh, in_specs=in_specs, out_specs=out_specs, check_vma=False
    )
```

```python
import functools

import jax
import jax.numpy as jnp
from jax import lax
from jax.experimental import pallas as pl
from jax.experimental.pallas import tpu as pltpu
from jax.sharding import PartitionSpec as P

LANES = 128
COLS = 256
STEP = 512
LOW = -4.0
VMEM_LIMIT = 40 * 1024 * 1024
PARAMS = pltpu.CompilerParams(vmem_limit_bytes=VMEM_LIMIT)


LANE_LOOKUP = lax.GatherDimensionNumbers(
    offset_dims=(),
    collapsed_slice_dims=(1,),
    start_index_map=(1,),
    operand_batching_dims=(0,),
    start_indices_batching_dims=(0,),
)


def take_lanes(table, index):
    return lax.gather(
        table, index[:, :, None], LANE_LOOKUP, (1, 1),
        mode=lax.GatherScatterMode.PROMISE_IN_BOUNDS,
    )


def pack_kernel(devices, capacity, rows_ref, out_ref):
    subspaces = rows_ref.shape[0] - 1
    in_rows = rows_ref.shape[1]
    half_rows = capacity // 2
    targets = rows_ref[subspaces:, :]
    hot = lax.broadcasted_iota(jnp.int32, (devices, in_rows), 0) == targets
    hot32 = jnp.where(hot, 1.0, 0.0)
    earlier = (
        lax.broadcasted_iota(jnp.int32, (in_rows, in_rows), 0)
        < lax.broadcasted_iota(jnp.int32, (in_rows, in_rows), 1)
    )
    running = jnp.dot(
        hot32.astype(jnp.bfloat16),
        jnp.where(earlier, 1.0, 0.0).astype(jnp.bfloat16),
        preferred_element_type=jnp.float32,
    )
    position = jnp.sum(hot32 * running, axis=0, keepdims=True).astype(jnp.int32)
    second = position >= half_rows
    key = targets * half_rows + jnp.where(second, position - half_rows, position)
    out_rows = devices * half_rows
    row_ids = lax.broadcasted_iota(jnp.int32, (out_rows, in_rows), 0)
    values = (rows_ref[:subspaces, :] + 1).astype(jnp.bfloat16)
    halves = []
    for wanted in (jnp.where(second, -1, key), jnp.where(second, key, -1)):
        move = jnp.where(row_ids == wanted, 1.0, 0.0).astype(jnp.bfloat16)
        halves.append(
            lax.dot_general(
                move, values, (((1,), (1,)), ((), ())), preferred_element_type=jnp.float32
            )
        )
    out_ref[...] = jnp.concatenate(halves, axis=1).astype(jnp.bfloat16)


def table_kernel(group_ref, book_ref, words_ref, centre_ref, norms_ref):
    width, words = words_ref.shape
    subspaces = norms_ref.shape[0]
    centres = book_ref[words:, :].astype(jnp.float32)
    pick = lax.broadcasted_iota(jnp.int32, (centres.shape[0], 1), 0) == group_ref[0, 0]
    centre = jnp.sum(jnp.where(pick, centres, 0.0), axis=0, keepdims=True)
    centre = jnp.transpose(jnp.broadcast_to(centre, (LANES, width)))
    centre_ref[...] = centre
    turned = jnp.transpose(book_ref[:words, :].astype(jnp.float32))
    words_ref[...] = turned.astype(jnp.bfloat16)
    for half in range(words // LANES):
        lanes = slice(half * LANES, (half + 1) * LANES)
        table = turned[:, lanes] + centre
        norms_ref[:, lanes] = jnp.sum(
            (table * table).reshape(subspaces, width // subspaces, LANES), axis=1
        )


def owner_block(codes_ref, owner, owners):
    parts = [
        codes_ref[pl.ds(pl.multiple_of((part * owners + owner) * 16, 16), 16), :]
        for part in range(LANES // 16)
    ]
    return jnp.concatenate(parts, axis=0)


def unpack_codes(block, norms_ref, code_ref, scale_ref, mark_ref, group, place):
    turned = jnp.transpose(block.astype(jnp.float32)).astype(jnp.int32)
    subspaces = turned.shape[0] // 2
    for half in range(2):
        part = turned[half * subspaces : (half + 1) * subspaces]
        code = jnp.maximum(part - 1, 0)
        code_ref[2 * group + half] = code
        mark_ref[2 * place + half] = jnp.where(part[0:8] > 0, 1.0, 0.0)
        low = code & (LANES - 1)
        squares = jnp.where(
            code >= LANES,
            take_lanes(norms_ref[:, LANES:], low),
            take_lanes(norms_ref[:, :LANES], low),
        )
        scale = lax.rsqrt(jnp.sum(squares, axis=0, keepdims=True) + 1e-06)
        scale_ref[2 * group + half] = jnp.broadcast_to(scale, (8, LANES))


def decode_groups(
    place, first, codes_refs, words_ref, centre_ref, norms_ref,
    units_ref, left_ref, mark_ref, code_ref, scale_ref, now_ref,
):
    slots = left_ref.shape[0]
    owners = units_ref.shape[1] // slots
    groups = slots // COLS
    subspaces = norms_ref.shape[0]
    sub_width = words_ref.shape[0] // subspaces
    for which, codes_ref in enumerate(codes_refs):
        for turn in range(owners):
            owner = lax.rem(place + turn, owners)
            unpack_codes(
                owner_block(codes_ref, owner, owners), norms_ref, code_ref, scale_ref, mark_ref,
                which * owners + turn, turn * groups + first + which,
            )

    for which in range(len(codes_refs)):

        def one_group(turn, _):
            start = pl.multiple_of(turn * slots + (first + which) * COLS, COLS)
            scales = []
            for half in range(2):
                tile = 2 * (which * owners + turn) + half
                now_ref[half] = code_ref[tile]
                scales.append(scale_ref[tile])
            for sub in range(subspaces):
                rows = slice(sub * sub_width, (sub + 1) * sub_width)
                for half in range(2):
                    code = jnp.broadcast_to(
                        now_ref[half, sub : sub + 1, :], (sub_width, LANES)
                    ).astype(jnp.int16)
                    low = code & (LANES - 1)
                    word = jnp.where(
                        code > LANES - 1,
                        take_lanes(words_ref[rows, LANES:], low),
                        take_lanes(words_ref[rows, :LANES], low),
                    )
                    embed = word.astype(jnp.float32) + centre_ref[rows, :]
                    unit = embed * jnp.concatenate([scales[half]] * (sub_width // 8), axis=0)
                    units_ref[rows, pl.ds(start + half * LANES, LANES)] = unit.astype(jnp.bfloat16)
            return 0

        lax.fori_loop(0, owners, one_group, 0)
        for half in range(2):
            start = (first + which) * COLS + half * LANES
            left_ref[start : start + LANES, :] = jnp.transpose(units_ref[:, start : start + LANES])


def first_kernel(place_ref, codes_ref, words_ref, centre_ref, norms_ref, *refs):
    decode_groups(place_ref[0, 0], 0, [codes_ref], words_ref, centre_ref, norms_ref, *refs)


def middle_kernel(count, place_ref, *refs):
    codes_refs, refs = refs[:count], refs[count:]
    decode_groups(place_ref[0, 0], 1, codes_refs, *refs[:3], *refs[6:])


def last_kernel(sizes, place_ref, *refs):
    capacity, clusters, members, count = sizes
    place = place_ref[0, 0]
    codes_refs, refs = refs[:count], refs[count:]
    table_refs, refs = refs[:3], refs[6:]
    out_ref, units_ref, left_ref, mark_ref, best_ref, code_ref, scale_ref, now_ref = refs
    slots = left_ref.shape[0]
    owners = units_ref.shape[1] // slots
    decode_groups(
        place, slots // COLS - count, codes_refs, *table_refs,
        units_ref, left_ref, mark_ref, code_ref, scale_ref, now_ref,
    )
    best_ref[...] = jnp.full(best_ref.shape, LOW, jnp.float32)

    def score(step, _, own):
        start = pl.multiple_of(step * STEP, STEP)
        scores = jnp.dot(
            left_ref[...], units_ref[:, pl.ds(start, STEP)], preferred_element_type=jnp.float32
        )
        best = best_ref[...]
        for part in range(STEP // LANES):
            keep = mark_ref[step * (STEP // LANES) + part][0:1, :] > 0
            if own:
                row_ids = lax.broadcasted_iota(jnp.int32, (slots, LANES), 0)
                lane_ids = lax.broadcasted_iota(jnp.int32, (slots, LANES), 1)
                keep = keep & (row_ids != lane_ids + (start + part * LANES))
            best = jnp.maximum(
                best, jnp.where(keep, scores[:, part * LANES : (part + 1) * LANES], LOW)
            )
        best_ref[...] = best
        return 0

    own_steps = slots // STEP
    lax.fori_loop(0, own_steps, functools.partial(score, own=True), 0)
    lax.fori_loop(own_steps, owners * own_steps, functools.partial(score, own=False), 0)

    half_rows = capacity // 2
    tiles = slots // LANES
    lane = lax.broadcasted_iota(jnp.int32, (tiles, LANES), 1)
    slot = lax.broadcasted_iota(jnp.int32, (tiles, LANES), 0) * LANES + lane
    source, within = slot // capacity, slot % capacity
    turn = place ^ (source % members)
    own_row = (turn * clusters + source // members) * half_rows + within % half_rows
    tile_of = 2 * (own_row // LANES) + within // half_rows
    result = jnp.zeros((tiles, LANES), jnp.float32)
    for tile in range(tiles):
        best = jnp.max(
            jnp.transpose(best_ref[tile * LANES : (tile + 1) * LANES, :]), axis=0, keepdims=True
        )
        mark = mark_ref[tile]
        best = jnp.where(mark[0:1, :] > 0, best, 0.0)
        result = jnp.where(
            tile_of == tile,
            take_lanes(jnp.broadcast_to(best, (tiles, LANES)), own_row % LANES),
            result,
        )
    out_ref[...] = result


def on_device(codes, routes, codebook, centroids):
    clusters = lax.axis_size("cluster")
    members = lax.axis_size("blk")
    devices = clusters * members
    subspaces, in_rows = codes.shape[2:]
    capacity = 2 * in_rows // devices
    half_rows = capacity // 2
    slots = devices * capacity
    tiles = slots // LANES
    groups = slots // COLS
    words, width = codebook.shape
    bf16, f32, i32 = jnp.bfloat16, jnp.float32, jnp.int32
    smem = pl.BlockSpec(memory_space=pltpu.SMEM)
    vmem = pl.BlockSpec(memory_space=pltpu.VMEM)

    packed = pl.pallas_call(
        functools.partial(pack_kernel, devices, capacity),
        out_shape=jax.ShapeDtypeStruct((in_rows, 2 * subspaces), bf16),
        compiler_params=PARAMS,
        name="pack_rows",
    )(jnp.concatenate([codes[0, 0], routes.reshape(1, in_rows)], axis=0))
    here = lax.all_to_all(packed, "cluster", split_axis=0, concat_axis=0, tiled=True)
    def from_member(block, mask):
        return lax.ppermute(block, "blk", [(i, i ^ mask) for i in range(members)])

    masks = range(1, members)
    blocks = {0: here}
    for mask in masks:
        if mask & (mask - 1) == 0:
            blocks[mask] = from_member(here, mask)

    place = lax.axis_index("blk").astype(i32).reshape(1, 1)
    group = lax.axis_index("cluster").astype(i32).reshape(1, 1)
    table = pl.pallas_call(
        table_kernel,
        out_shape=(
            jax.ShapeDtypeStruct((width, words), bf16),
            jax.ShapeDtypeStruct((width, LANES), f32),
            jax.ShapeDtypeStruct((subspaces, words), f32),
        ),
        in_specs=[smem, vmem],
        compiler_params=PARAMS,
        cost_estimate=pl.CostEstimate(
            flops=4 * words * width, bytes_accessed=6 * words * width, transcendentals=0
        ),
        name="word_table",
    )(group, jnp.concatenate([codebook, centroids], axis=0))

    state_shape = (
        jax.ShapeDtypeStruct((width, members * slots), bf16),
        jax.ShapeDtypeStruct((slots, width), bf16),
        jax.ShapeDtypeStruct((2 * members * groups, 8, LANES), f32),
    )

    def code_scratch(count):
        return [
            pltpu.VMEM((2 * members * count, subspaces, LANES), i32),
            pltpu.VMEM((2 * members * count, 8, LANES), f32),
            pltpu.VMEM((2, subspaces, LANES), i32),
        ]

    def decode_cost(count):
        return pl.CostEstimate(
            flops=100 * count * members * COLS * width,
            bytes_accessed=4 * count * members * COLS * width,
            transcendentals=0,
        )

    first = pl.pallas_call(
        first_kernel,
        out_shape=state_shape,
        in_specs=[smem] + [vmem] * 4,
        out_specs=(vmem,) * 3,
        scratch_shapes=code_scratch(1),
        compiler_params=PARAMS,
        cost_estimate=decode_cost(1),
        name="first_rows",
    )
    whole_groups = half_rows == 16 and clusters * half_rows == LANES
    if whole_groups:
        units, left, marks = first(place, here, *table)
    for mask in masks:
        if mask not in blocks:
            low = mask & -mask
            block = blocks[mask - low]
            if whole_groups:
                block, marks = lax.optimization_barrier((block, marks))
            blocks[mask] = from_member(block, low)
    blocks = [here] + [blocks[mask] for mask in masks]
    if not whole_groups:
        every = jnp.stack(blocks).reshape(members, clusters, members, half_rows, LANES)
        every = every.transpose(2, 0, 1, 3, 4).reshape(members, groups, LANES // 16, 16, LANES)
        every = every.transpose(1, 2, 0, 3, 4).reshape(groups, members * LANES, LANES)
        blocks = list(every)
        units, left, marks = first(place, blocks[0], *table)
    state = (units, left, marks)
    count = groups - 2
    state = pl.pallas_call(
        functools.partial(middle_kernel, count),
        out_shape=state_shape,
        in_specs=[smem] + [vmem] * (count + 6),
        out_specs=(vmem,) * 3,
        scratch_shapes=code_scratch(count),
        input_output_aliases={count + 4 + which: which for which in range(3)},
        compiler_params=PARAMS,
        cost_estimate=decode_cost(count),
        name="middle_rows",
    )(place, *blocks[1 : 1 + count], *table, *state)
    nearest, *_ = pl.pallas_call(
        functools.partial(last_kernel, (capacity, clusters, members, 1)),
        out_shape=(jax.ShapeDtypeStruct((tiles, LANES), f32), *state_shape),
        in_specs=[smem] + [vmem] * 7,
        out_specs=(vmem,) * 4,
        scratch_shapes=[pltpu.VMEM((slots, LANES), f32)] + code_scratch(1),
        input_output_aliases={5 + which: 1 + which for which in range(3)},
        compiler_params=PARAMS,
        cost_estimate=pl.CostEstimate(
            flops=2 * slots * members * slots * width,
            bytes_accessed=8 * slots * width,
            transcendentals=0,
        ),
        name="last_rows",
    )(place, blocks[groups - 1], *table, *state)
    return nearest.reshape(1, 1, slots)


def solution(mesh):
    in_specs = (P("cluster", "blk", None, None), P("cluster", "blk", None, None), P(), P())
    out_specs = P("cluster", "blk", None)
    return jax.shard_map(
        on_device, mesh=mesh, in_specs=in_specs, out_specs=out_specs, check_vma=False
    )
```

```python
import functools

import jax
import jax.numpy as jnp
from jax import lax
from jax.experimental import pallas as pl
from jax.experimental.pallas import tpu as pltpu
from jax.sharding import PartitionSpec as P

LANES = 128
COLS = 256
STEP = 1024
ROWS = 16
LOW = -4.0
VMEM_LIMIT = 40 * 1024 * 1024
PARAMS = pltpu.CompilerParams(vmem_limit_bytes=VMEM_LIMIT)


LANE_LOOKUP = lax.GatherDimensionNumbers(
    offset_dims=(),
    collapsed_slice_dims=(1,),
    start_index_map=(1,),
    operand_batching_dims=(0,),
    start_indices_batching_dims=(0,),
)


def take_lanes(table, index):
    return lax.gather(
        table, index[:, :, None], LANE_LOOKUP, (1, 1),
        mode=lax.GatherScatterMode.PROMISE_IN_BOUNDS,
    )


def pack_kernel(devices, capacity, rows_ref, out_ref):
    subspaces = rows_ref.shape[0] - 1
    in_rows = rows_ref.shape[1]
    half_rows = capacity // 2
    targets = rows_ref[subspaces:, :]
    hot = lax.broadcasted_iota(jnp.int32, (devices, in_rows), 0) == targets
    hot32 = jnp.where(hot, 1.0, 0.0)
    earlier = (
        lax.broadcasted_iota(jnp.int32, (in_rows, in_rows), 0)
        < lax.broadcasted_iota(jnp.int32, (in_rows, in_rows), 1)
    )
    running = jnp.dot(
        hot32.astype(jnp.bfloat16),
        jnp.where(earlier, 1.0, 0.0).astype(jnp.bfloat16),
        preferred_element_type=jnp.float32,
    )
    position = jnp.sum(hot32 * running, axis=0, keepdims=True).astype(jnp.int32)
    second = position >= half_rows
    key = targets * half_rows + jnp.where(second, position - half_rows, position)
    out_rows = devices * half_rows
    row_ids = lax.broadcasted_iota(jnp.int32, (out_rows, in_rows), 0)
    values = (rows_ref[:subspaces, :] + 1).astype(jnp.bfloat16)
    halves = []
    for wanted in (jnp.where(second, -1, key), jnp.where(second, key, -1)):
        move = jnp.where(row_ids == wanted, 1.0, 0.0).astype(jnp.bfloat16)
        halves.append(
            lax.dot_general(
                move, values, (((1,), (1,)), ((), ())), preferred_element_type=jnp.float32
            )
        )
    out_ref[...] = jnp.concatenate(halves, axis=1).astype(jnp.bfloat16)


def table_kernel(group_ref, book_ref, words_ref, centre_ref, norms_ref):
    width, words = words_ref.shape
    subspaces = norms_ref.shape[0]
    sub_width = width // subspaces
    block = ROWS * sub_width
    new = lax.broadcasted_iota(jnp.int32, (block, block), 0)
    old = lax.broadcasted_iota(jnp.int32, (block, block), 1)
    order = jnp.where(old == (new % ROWS) * sub_width + new // ROWS, 1.0, 0.0).astype(jnp.bfloat16)
    clusters = book_ref.shape[0] - words
    pick = lax.broadcasted_iota(jnp.int32, (1, clusters), 1) == group_ref[0, 0]
    for part in range(width // block):
        rows = slice(part * block, (part + 1) * block)
        turned = lax.dot_general(
            order, book_ref[:, rows], (((1,), (1,)), ((), ())), preferred_element_type=jnp.float32
        )
        centre = jnp.sum(jnp.where(pick, turned[:, words:], 0.0), axis=1, keepdims=True)
        words_ref[rows, :] = turned[:, :words].astype(jnp.bfloat16)
        centre_ref[rows, :] = jnp.broadcast_to(centre, (block, LANES))
        table = turned[:, :words] + centre
        norms_ref[part * ROWS : (part + 1) * ROWS, :] = jnp.sum(
            (table * table).reshape(sub_width, ROWS, words), axis=0
        )


def owner_block(codes_ref, owner, owners):
    parts = [
        codes_ref[pl.ds(pl.multiple_of((part * owners + owner) * 16, 16), 16), :]
        for part in range(LANES // 16)
    ]
    return jnp.concatenate(parts, axis=0)


def unpack_codes(block, norms_ref, code_ref, scale_ref, mark_ref, group, place):
    turned = jnp.transpose(block.astype(jnp.float32)).astype(jnp.int32)
    subspaces = turned.shape[0] // 2
    for half in range(2):
        part = turned[half * subspaces : (half + 1) * subspaces]
        code = jnp.maximum(part - 1, 0)
        code_ref[2 * group + half] = code
        mark_ref[2 * place + half] = jnp.where(part[0:8] > 0, 1.0, 0.0)
        low = code & (LANES - 1)
        squares = jnp.where(
            code >= LANES,
            take_lanes(norms_ref[:, LANES:], low),
            take_lanes(norms_ref[:, :LANES], low),
        )
        scale = lax.rsqrt(jnp.sum(squares, axis=0, keepdims=True) + 1e-06)
        scale_ref[2 * group + half] = jnp.broadcast_to(scale, (8, LANES))


def decode_groups(
    place, first, codes_refs, words_ref, centre_ref, norms_ref,
    units_ref, left_ref, mark_ref, code_ref, scale_ref,
):
    slots = left_ref.shape[0]
    owners = units_ref.shape[1] // slots
    groups = slots // COLS
    subspaces = norms_ref.shape[0]
    sub_width = words_ref.shape[0] // subspaces
    for which, codes_ref in enumerate(codes_refs):
        for turn in range(owners):
            owner = lax.rem(place + turn, owners)
            unpack_codes(
                owner_block(codes_ref, owner, owners), norms_ref, code_ref, scale_ref, mark_ref,
                which * owners + turn, turn * groups + first + which,
            )

    for which in range(len(codes_refs)):

        def one_group(turn, _):
            start = pl.multiple_of(turn * slots + (first + which) * COLS, COLS)
            for half in range(2):
                tile = 2 * (which * owners + turn) + half
                codes = code_ref[tile].astype(jnp.int16)
                scale = jnp.concatenate([scale_ref[tile]] * (ROWS // 8), axis=0)
                for part in range(subspaces // ROWS):
                    code = codes[part * ROWS : (part + 1) * ROWS]
                    low = code & (LANES - 1)
                    high = code > LANES - 1
                    for entry in range(sub_width):
                        row = (part * sub_width + entry) * ROWS
                        rows = slice(row, row + ROWS)
                        word = jnp.where(
                            high,
                            take_lanes(words_ref[rows, LANES:], low),
                            take_lanes(words_ref[rows, :LANES], low),
                        )
                        unit = (word.astype(jnp.float32) + centre_ref[rows, :]) * scale
                        units_ref[rows, pl.ds(start + half * LANES, LANES)] = unit.astype(
                            jnp.bfloat16
                        )
            return 0

        lax.fori_loop(0, owners, one_group, 0)
        for half in range(2):
            start = (first + which) * COLS + half * LANES
            left_ref[start : start + LANES, :] = jnp.transpose(units_ref[:, start : start + LANES])


def first_kernel(place_ref, codes_ref, words_ref, centre_ref, norms_ref, *refs):
    decode_groups(place_ref[0, 0], 0, [codes_ref], words_ref, centre_ref, norms_ref, *refs)


def middle_kernel(count, place_ref, *refs):
    codes_refs, refs = refs[:count], refs[count:]
    decode_groups(place_ref[0, 0], 1, codes_refs, *refs[:3], *refs[6:])


def last_kernel(sizes, place_ref, *refs):
    capacity, clusters, members, count = sizes
    place = place_ref[0, 0]
    codes_refs, refs = refs[:count], refs[count:]
    table_refs, refs = refs[:3], refs[6:]
    out_ref, units_ref, left_ref, mark_ref, best_ref, code_ref, scale_ref = refs
    slots = left_ref.shape[0]
    owners = units_ref.shape[1] // slots
    decode_groups(
        place, slots // COLS - count, codes_refs, *table_refs,
        units_ref, left_ref, mark_ref, code_ref, scale_ref,
    )
    best_ref[...] = jnp.full(best_ref.shape, LOW, jnp.float32)

    def score(step, _, own):
        start = pl.multiple_of(step * STEP, STEP)
        scores = jnp.dot(
            left_ref[...], units_ref[:, pl.ds(start, STEP)], preferred_element_type=jnp.float32
        )
        best = best_ref[...]
        for part in range(STEP // LANES):
            keep = mark_ref[step * (STEP // LANES) + part][0:1, :] > 0
            if own:
                row_ids = lax.broadcasted_iota(jnp.int32, (slots, LANES), 0)
                lane_ids = lax.broadcasted_iota(jnp.int32, (slots, LANES), 1)
                keep = keep & (row_ids != lane_ids + (start + part * LANES))
            best = jnp.maximum(
                best, jnp.where(keep, scores[:, part * LANES : (part + 1) * LANES], LOW)
            )
        best_ref[...] = best
        return 0

    own_steps = slots // STEP
    lax.fori_loop(0, own_steps, functools.partial(score, own=True), 0)
    lax.fori_loop(own_steps, owners * own_steps, functools.partial(score, own=False), 0)

    half_rows = capacity // 2
    tiles = slots // LANES
    lane = lax.broadcasted_iota(jnp.int32, (tiles, LANES), 1)
    slot = lax.broadcasted_iota(jnp.int32, (tiles, LANES), 0) * LANES + lane
    source, within = slot // capacity, slot % capacity
    turn = place ^ (source % members)
    own_row = (turn * clusters + source // members) * half_rows + within % half_rows
    tile_of = 2 * (own_row // LANES) + within // half_rows
    result = jnp.zeros((tiles, LANES), jnp.float32)
    for tile in range(tiles):
        best = jnp.max(
            jnp.transpose(best_ref[tile * LANES : (tile + 1) * LANES, :]), axis=0, keepdims=True
        )
        mark = mark_ref[tile]
        best = jnp.where(mark[0:1, :] > 0, best, 0.0)
        result = jnp.where(
            tile_of == tile,
            take_lanes(jnp.broadcast_to(best, (tiles, LANES)), own_row % LANES),
            result,
        )
    out_ref[...] = result


def on_device(codes, routes, codebook, centroids):
    clusters = lax.axis_size("cluster")
    members = lax.axis_size("blk")
    devices = clusters * members
    subspaces, in_rows = codes.shape[2:]
    capacity = 2 * in_rows // devices
    half_rows = capacity // 2
    slots = devices * capacity
    tiles = slots // LANES
    groups = slots // COLS
    words, width = codebook.shape
    bf16, f32, i32 = jnp.bfloat16, jnp.float32, jnp.int32
    smem = pl.BlockSpec(memory_space=pltpu.SMEM)
    vmem = pl.BlockSpec(memory_space=pltpu.VMEM)

    packed = pl.pallas_call(
        functools.partial(pack_kernel, devices, capacity),
        out_shape=jax.ShapeDtypeStruct((in_rows, 2 * subspaces), bf16),
        compiler_params=PARAMS,
        name="pack_rows",
    )(jnp.concatenate([codes[0, 0], routes.reshape(1, in_rows)], axis=0))
    here = lax.all_to_all(packed, "cluster", split_axis=0, concat_axis=0, tiled=True)
    def from_member(block, mask):
        return lax.ppermute(block, "blk", [(i, i ^ mask) for i in range(members)])

    masks = range(1, members)
    blocks = {0: here}
    for mask in masks:
        if mask & (mask - 1) == 0:
            blocks[mask] = from_member(here, mask)

    place = lax.axis_index("blk").astype(i32).reshape(1, 1)
    group = lax.axis_index("cluster").astype(i32).reshape(1, 1)
    table = pl.pallas_call(
        table_kernel,
        out_shape=(
            jax.ShapeDtypeStruct((width, words), bf16),
            jax.ShapeDtypeStruct((width, LANES), f32),
            jax.ShapeDtypeStruct((subspaces, words), f32),
        ),
        in_specs=[smem, vmem],
        compiler_params=PARAMS,
        cost_estimate=pl.CostEstimate(
            flops=4 * words * width, bytes_accessed=6 * words * width, transcendentals=0
        ),
        name="word_table",
    )(group, jnp.concatenate([codebook, centroids], axis=0))

    state_shape = (
        jax.ShapeDtypeStruct((width, members * slots), bf16),
        jax.ShapeDtypeStruct((slots, width), bf16),
        jax.ShapeDtypeStruct((2 * members * groups, 8, LANES), f32),
    )

    def code_scratch(count):
        return [
            pltpu.VMEM((2 * members * count, subspaces, LANES), i32),
            pltpu.VMEM((2 * members * count, 8, LANES), f32),
        ]

    def decode_cost(count):
        return pl.CostEstimate(
            flops=100 * count * members * COLS * width,
            bytes_accessed=4 * count * members * COLS * width,
            transcendentals=0,
        )

    first = pl.pallas_call(
        first_kernel,
        out_shape=state_shape,
        in_specs=[smem] + [vmem] * 4,
        out_specs=(vmem,) * 3,
        scratch_shapes=code_scratch(1),
        compiler_params=PARAMS,
        cost_estimate=decode_cost(1),
        name="first_rows",
    )
    whole_groups = half_rows == 16 and clusters * half_rows == LANES
    if whole_groups:
        units, left, marks = first(place, here, *table)
    for mask in masks:
        if mask not in blocks:
            low = mask & -mask
            block = blocks[mask - low]
            if whole_groups:
                block, marks = lax.optimization_barrier((block, marks))
            blocks[mask] = from_member(block, low)
    blocks = [here] + [blocks[mask] for mask in masks]
    if not whole_groups:
        every = jnp.stack(blocks).reshape(members, clusters, members, half_rows, LANES)
        every = every.transpose(2, 0, 1, 3, 4).reshape(members, groups, LANES // 16, 16, LANES)
        every = every.transpose(1, 2, 0, 3, 4).reshape(groups, members * LANES, LANES)
        blocks = list(every)
        units, left, marks = first(place, blocks[0], *table)
    state = (units, left, marks)
    count = groups - 2
    state = pl.pallas_call(
        functools.partial(middle_kernel, count),
        out_shape=state_shape,
        in_specs=[smem] + [vmem] * (count + 6),
        out_specs=(vmem,) * 3,
        scratch_shapes=code_scratch(count),
        input_output_aliases={count + 4 + which: which for which in range(3)},
        compiler_params=PARAMS,
        cost_estimate=decode_cost(count),
        name="middle_rows",
    )(place, *blocks[1 : 1 + count], *table, *state)
    nearest, *_ = pl.pallas_call(
        functools.partial(last_kernel, (capacity, clusters, members, 1)),
        out_shape=(jax.ShapeDtypeStruct((tiles, LANES), f32), *state_shape),
        in_specs=[smem] + [vmem] * 7,
        out_specs=(vmem,) * 4,
        scratch_shapes=[pltpu.VMEM((slots, LANES), f32)] + code_scratch(1),
        input_output_aliases={5 + which: 1 + which for which in range(3)},
        compiler_params=PARAMS,
        cost_estimate=pl.CostEstimate(
            flops=2 * slots * members * slots * width,
            bytes_accessed=8 * slots * width,
            transcendentals=0,
        ),
        name="last_rows",
    )(place, blocks[groups - 1], *table, *state)
    return nearest.reshape(1, 1, slots)


def solution(mesh):
    in_specs = (P("cluster", "blk", None, None), P("cluster", "blk", None, None), P(), P())
    out_specs = P("cluster", "blk", None)
    return jax.shard_map(
        on_device, mesh=mesh, in_specs=in_specs, out_specs=out_specs, check_vma=False
    )
```

```python
import functools

import jax
import jax.numpy as jnp
from jax import lax
from jax.experimental import pallas as pl
from jax.experimental.pallas import tpu as pltpu
from jax.sharding import PartitionSpec as P

LANES = 128
COLS = 256
ROWS = 16
LOW = -4.0
VMEM_LIMIT = 40 * 1024 * 1024
PARAMS = pltpu.CompilerParams(vmem_limit_bytes=VMEM_LIMIT)


LANE_LOOKUP = lax.GatherDimensionNumbers(
    offset_dims=(),
    collapsed_slice_dims=(1,),
    start_index_map=(1,),
    operand_batching_dims=(0,),
    start_indices_batching_dims=(0,),
)


def take_lanes(table, index):
    return lax.gather(
        table, index[:, :, None], LANE_LOOKUP, (1, 1),
        mode=lax.GatherScatterMode.PROMISE_IN_BOUNDS,
    )


def pack_kernel(devices, capacity, rows_ref, out_ref):
    subspaces = rows_ref.shape[0] - 1
    in_rows = rows_ref.shape[1]
    half_rows = capacity // 2
    targets = rows_ref[subspaces:, :]
    hot = lax.broadcasted_iota(jnp.int32, (devices, in_rows), 0) == targets
    hot32 = jnp.where(hot, 1.0, 0.0)
    earlier = (
        lax.broadcasted_iota(jnp.int32, (in_rows, in_rows), 0)
        < lax.broadcasted_iota(jnp.int32, (in_rows, in_rows), 1)
    )
    running = jnp.dot(
        hot32.astype(jnp.bfloat16),
        jnp.where(earlier, 1.0, 0.0).astype(jnp.bfloat16),
        preferred_element_type=jnp.float32,
    )
    position = jnp.sum(hot32 * running, axis=0, keepdims=True).astype(jnp.int32)
    second = position >= half_rows
    key = targets * half_rows + jnp.where(second, position - half_rows, position)
    out_rows = devices * half_rows
    row_ids = lax.broadcasted_iota(jnp.int32, (out_rows, in_rows), 0)
    values = (rows_ref[:subspaces, :] + 1).astype(jnp.bfloat16)
    halves = []
    for wanted in (jnp.where(second, -1, key), jnp.where(second, key, -1)):
        move = jnp.where(row_ids == wanted, 1.0, 0.0).astype(jnp.bfloat16)
        halves.append(
            lax.dot_general(
                move, values, (((1,), (1,)), ((), ())), preferred_element_type=jnp.float32
            )
        )
    out_ref[...] = jnp.concatenate(halves, axis=1).astype(jnp.bfloat16)


def table_kernel(group_ref, book_ref, words_ref, centre_ref, norms_ref):
    width, words = words_ref.shape
    subspaces = norms_ref.shape[0]
    sub_width = width // subspaces
    block = ROWS * sub_width
    new = lax.broadcasted_iota(jnp.int32, (block, block), 0)
    old = lax.broadcasted_iota(jnp.int32, (block, block), 1)
    order = jnp.where(old == (new % ROWS) * sub_width + new // ROWS, 1.0, 0.0).astype(jnp.bfloat16)
    clusters = book_ref.shape[0] - words
    pick = lax.broadcasted_iota(jnp.int32, (1, clusters), 1) == group_ref[0, 0]
    for part in range(width // block):
        rows = slice(part * block, (part + 1) * block)
        turned = lax.dot_general(
            order, book_ref[:, rows], (((1,), (1,)), ((), ())), preferred_element_type=jnp.float32
        )
        centre = jnp.sum(jnp.where(pick, turned[:, words:], 0.0), axis=1, keepdims=True)
        words_ref[rows, :] = turned[:, :words].astype(jnp.bfloat16)
        centre_ref[rows, :] = jnp.broadcast_to(centre, (block, LANES))
        table = turned[:, :words] + centre
        norms_ref[part * ROWS : (part + 1) * ROWS, :] = jnp.sum(
            (table * table).reshape(sub_width, ROWS, words), axis=0
        )


def owner_block(codes_ref, owner, owners):
    parts = [
        codes_ref[pl.ds(pl.multiple_of((part * owners + owner) * 16, 16), 16), :]
        for part in range(LANES // 16)
    ]
    return jnp.concatenate(parts, axis=0)


def unpack_codes(block, norms_ref, code_ref, scale_ref, mark_ref, group, place):
    turned = jnp.transpose(block.astype(jnp.float32)).astype(jnp.int32)
    subspaces = turned.shape[0] // 2
    for half in range(2):
        part = turned[half * subspaces : (half + 1) * subspaces]
        code = jnp.maximum(part - 1, 0)
        code_ref[2 * group + half] = code
        mark_ref[2 * place + half] = jnp.where(part[0:8] > 0, 1.0, 0.0)
        low = code & (LANES - 1)
        squares = jnp.where(
            code >= LANES,
            take_lanes(norms_ref[:, LANES:], low),
            take_lanes(norms_ref[:, :LANES], low),
        )
        scale = lax.rsqrt(jnp.sum(squares, axis=0, keepdims=True) + 1e-06)
        scale_ref[2 * group + half] = jnp.broadcast_to(scale, (8, LANES))


def unpack_block(
    place, first, which, codes_ref, norms_ref, code_ref, scale_ref, mark_ref, owners, groups
):
    for turn in range(owners):
        owner = lax.rem(place + turn, owners)
        unpack_codes(
            owner_block(codes_ref, owner, owners), norms_ref, code_ref, scale_ref, mark_ref,
            which * owners + turn, turn * groups + first + which,
        )


def decode_half(code_ref, scale_ref, tile, words_ref, centre_ref, units_ref, start):
    subspaces = code_ref.shape[1]
    sub_width = words_ref.shape[0] // subspaces
    codes = code_ref[tile].astype(jnp.int16)
    scale = jnp.concatenate([scale_ref[tile]] * (ROWS // 8), axis=0)
    for part in range(subspaces // ROWS):
        code = codes[part * ROWS : (part + 1) * ROWS]
        low = code & (LANES - 1)
        high = code > LANES - 1
        for entry in range(sub_width):
            row = (part * sub_width + entry) * ROWS
            rows = slice(row, row + ROWS)
            word = jnp.where(
                high,
                take_lanes(words_ref[rows, LANES:], low),
                take_lanes(words_ref[rows, :LANES], low),
            )
            unit = (word.astype(jnp.float32) + centre_ref[rows, :]) * scale
            units_ref[rows, pl.ds(start, LANES)] = unit.astype(jnp.bfloat16)


def turn_own(units_ref, left_ref, block):
    for half in range(2):
        start = block * COLS + half * LANES
        left_ref[start : start + LANES, :] = jnp.transpose(
            units_ref[:, half * LANES : (half + 1) * LANES]
        )


def score(left_ref, rows, units_ref, start, marks, best_ref):
    scores = jnp.dot(
        left_ref[rows, :], units_ref[:, pl.ds(start, COLS)], preferred_element_type=jnp.float32
    )
    best = best_ref[rows, :]
    for part in range(COLS // LANES):
        best = jnp.maximum(
            best, jnp.where(marks[part], scores[:, part * LANES : (part + 1) * LANES], LOW)
        )
    best_ref[rows, :] = best


def own_score(left_ref, units_ref, mark_ref, block, best_ref, mirror_ref):
    above, count = block * COLS, (block + 1) * COLS
    scores = jnp.dot(
        left_ref[:count, :], units_ref[:, :COLS], preferred_element_type=jnp.float32
    )
    row_ids = lax.broadcasted_iota(jnp.int32, (COLS, LANES), 0)
    lane_ids = lax.broadcasted_iota(jnp.int32, (COLS, LANES), 1)
    for part in range(COLS // LANES):
        tile = block * (COLS // LANES) + part
        lanes = slice(part * LANES, (part + 1) * LANES)
        filled = mark_ref[tile][0:1, :] > 0
        keep = filled & (row_ids != lane_ids + part * LANES)
        best_ref[above:count, :] = jnp.maximum(
            best_ref[above:count, :], jnp.where(keep, scores[above:count, lanes], LOW)
        )
        mirror = jnp.full((1, LANES), LOW, jnp.float32)
        for other in range(above // LANES):
            rows = slice(other * LANES, (other + 1) * LANES)
            piece = scores[rows, lanes]
            best_ref[rows, :] = jnp.maximum(best_ref[rows, :], jnp.where(filled, piece, LOW))
            row_filled = jnp.transpose(
                jnp.broadcast_to(mark_ref[other][0:1, :], (LANES, LANES))
            )
            mirror = jnp.maximum(
                mirror,
                jnp.max(jnp.where(row_filled > 0, piece, LOW), axis=0, keepdims=True),
            )
        mirror_ref[tile] = jnp.broadcast_to(mirror, (8, LANES))


def marks_of(mark_ref, group):
    return [mark_ref[2 * group + part][0:1, :] > 0 for part in range(COLS // LANES)]


def first_kernel(
    place_ref, codes_ref, words_ref, centre_ref, norms_ref,
    units_ref, left_ref, mark_ref, code_ref, scale_ref,
):
    owners = units_ref.shape[1] // COLS
    groups = left_ref.shape[0] // COLS
    unpack_block(
        place_ref[0, 0], 0, 0, codes_ref, norms_ref, code_ref, scale_ref, mark_ref, owners, groups
    )

    def one_group(turn, _):
        for half in range(2):
            start = pl.multiple_of(turn * COLS + half * LANES, LANES)
            decode_half(
                code_ref, scale_ref, 2 * turn + half, words_ref, centre_ref, units_ref, start
            )
        return 0

    lax.fori_loop(0, owners, one_group, 0)
    turn_own(units_ref, left_ref, 0)


def blocks_kernel(first, done_rows, place, codes_refs, table_refs, units_refs, state):
    left_ref, mark_ref, best_ref, mirror_ref, code_ref, scale_ref = state
    words_ref, centre_ref, norms_ref = table_refs
    owners = units_refs[0].shape[1] // COLS
    groups = left_ref.shape[0] // COLS
    for which, codes_ref in enumerate(codes_refs):
        unpack_block(
            place, first, which, codes_ref, norms_ref, code_ref, scale_ref, mark_ref,
            owners, groups,
        )
        for half in range(2):
            decode_half(
                code_ref, scale_ref, 2 * which * owners + half, words_ref, centre_ref,
                units_refs[which + 1], half * LANES,
            )
        turn_own(units_refs[which + 1], left_ref, first + which)
    for which in range(len(codes_refs)):
        own_score(left_ref, units_refs[which + 1], mark_ref, first + which, best_ref, mirror_ref)

    halves = [slice(0, done_rows // 2), slice(done_rows // 2, done_rows)]
    for which in range(len(codes_refs)):

        def both(turn, _):
            column = pl.multiple_of(turn * COLS, LANES)
            marks = marks_of(mark_ref, turn * groups + first + which - 1)
            for half in range(2):
                score(left_ref, halves[half], units_refs[which], column, marks, best_ref)
                decode_half(
                    code_ref, scale_ref, 2 * (which * owners + turn) + half,
                    words_ref, centre_ref, units_refs[which + 1],
                    pl.multiple_of(turn * COLS + half * LANES, LANES),
                )
            return 0

        lax.fori_loop(1, owners, both, 0)


def middle_kernel(count, place_ref, *refs):
    codes_refs, refs = refs[:count], refs[count:]
    table_refs, refs = refs[:3], refs[3:]
    near_ref, refs = refs[0], refs[3:]
    units_refs, refs = refs[:count], refs[count:]
    left_ref, mark_ref, best_ref, mirror_ref, code_ref, scale_ref = refs
    best_ref[...] = jnp.full(best_ref.shape, LOW, jnp.float32)
    own_score(left_ref, near_ref, mark_ref, 0, best_ref, mirror_ref)
    blocks_kernel(
        1, (count + 1) * COLS, place_ref[0, 0], codes_refs, table_refs,
        [near_ref, *units_refs], refs,
    )


def last_kernel(sizes, place_ref, codes_ref, *refs):
    capacity, clusters, members = sizes
    place = place_ref[0, 0]
    table_refs, refs = refs[:3], refs[3:]
    units_refs, refs = refs[:-12], refs[-8:]
    out_ref, left_ref, mark_ref, best_ref, mirror_ref, units_ref, code_ref, scale_ref = refs
    slots = left_ref.shape[0]
    groups = slots // COLS
    owners = units_ref.shape[1] // COLS
    blocks_kernel(
        groups - 1, slots, place, [codes_ref], table_refs, [units_refs[-1], units_ref],
        (left_ref, mark_ref, best_ref, mirror_ref, code_ref, scale_ref),
    )

    def rest(turn, _):
        column = pl.multiple_of(turn * COLS, LANES)
        score(
            left_ref, slice(0, slots), units_ref, column,
            marks_of(mark_ref, turn * groups + groups - 1), best_ref,
        )
        for which in range(groups - 2):
            score(
                left_ref, slice(slots - COLS, slots), units_refs[which], column,
                marks_of(mark_ref, turn * groups + which), best_ref,
            )
        return 0

    lax.fori_loop(1, owners, rest, 0)

    half_rows = capacity // 2
    tiles = slots // LANES
    lane = lax.broadcasted_iota(jnp.int32, (tiles, LANES), 1)
    slot = lax.broadcasted_iota(jnp.int32, (tiles, LANES), 0) * LANES + lane
    source, within = slot // capacity, slot % capacity
    turn = place ^ (source % members)
    own_row = (turn * clusters + source // members) * half_rows + within % half_rows
    tile_of = 2 * (own_row // LANES) + within // half_rows
    result = jnp.zeros((tiles, LANES), jnp.float32)
    for tile in range(tiles):
        best = jnp.max(
            jnp.transpose(best_ref[tile * LANES : (tile + 1) * LANES, :]), axis=0, keepdims=True
        )
        best = jnp.maximum(best, mirror_ref[tile][0:1, :])
        mark = mark_ref[tile]
        best = jnp.where(mark[0:1, :] > 0, best, 0.0)
        result = jnp.where(
            tile_of == tile,
            take_lanes(jnp.broadcast_to(best, (tiles, LANES)), own_row % LANES),
            result,
        )
    out_ref[...] = result


def on_device(codes, routes, codebook, centroids):
    clusters = lax.axis_size("cluster")
    members = lax.axis_size("blk")
    devices = clusters * members
    subspaces, in_rows = codes.shape[2:]
    capacity = 2 * in_rows // devices
    half_rows = capacity // 2
    slots = devices * capacity
    tiles = slots // LANES
    groups = slots // COLS
    words, width = codebook.shape
    bf16, f32, i32 = jnp.bfloat16, jnp.float32, jnp.int32
    smem = pl.BlockSpec(memory_space=pltpu.SMEM)
    vmem = pl.BlockSpec(memory_space=pltpu.VMEM)

    packed = pl.pallas_call(
        functools.partial(pack_kernel, devices, capacity),
        out_shape=jax.ShapeDtypeStruct((in_rows, 2 * subspaces), bf16),
        compiler_params=PARAMS,
        name="pack_rows",
    )(jnp.concatenate([codes[0, 0], routes.reshape(1, in_rows)], axis=0))
    here = lax.all_to_all(packed, "cluster", split_axis=0, concat_axis=0, tiled=True)
    def from_member(block, mask):
        return lax.ppermute(block, "blk", [(i, i ^ mask) for i in range(members)])

    masks = range(1, members)
    blocks = {0: here}
    for mask in masks:
        if mask & (mask - 1) == 0:
            blocks[mask] = from_member(here, mask)

    place = lax.axis_index("blk").astype(i32).reshape(1, 1)
    group = lax.axis_index("cluster").astype(i32).reshape(1, 1)
    table = pl.pallas_call(
        table_kernel,
        out_shape=(
            jax.ShapeDtypeStruct((width, words), bf16),
            jax.ShapeDtypeStruct((width, LANES), f32),
            jax.ShapeDtypeStruct((subspaces, words), f32),
        ),
        in_specs=[smem, vmem],
        compiler_params=PARAMS,
        cost_estimate=pl.CostEstimate(
            flops=4 * words * width, bytes_accessed=6 * words * width, transcendentals=0
        ),
        name="word_table",
    )(group, jnp.concatenate([codebook, centroids], axis=0))

    units_shape = jax.ShapeDtypeStruct((width, members * COLS), bf16)
    state_shape = (
        jax.ShapeDtypeStruct((slots, width), bf16),
        jax.ShapeDtypeStruct((2 * members * groups, 8, LANES), f32),
        jax.ShapeDtypeStruct((slots, LANES), f32),
        jax.ShapeDtypeStruct((tiles, 8, LANES), f32),
    )

    def code_scratch(count):
        return [
            pltpu.VMEM((2 * members * count, subspaces, LANES), i32),
            pltpu.VMEM((2 * members * count, 8, LANES), f32),
        ]

    def cost(flops):
        return pl.CostEstimate(
            flops=flops, bytes_accessed=16 * slots * width, transcendentals=0
        )

    scores_flops = 2 * slots * members * slots * width
    first = pl.pallas_call(
        first_kernel,
        out_shape=(units_shape, *state_shape[:2]),
        in_specs=[smem] + [vmem] * 4,
        out_specs=(vmem,) * 3,
        scratch_shapes=code_scratch(1),
        compiler_params=PARAMS,
        cost_estimate=cost(scores_flops // 4),
        name="first_rows",
    )
    whole_groups = half_rows == 16 and clusters * half_rows == LANES
    if whole_groups:
        units, left, marks = first(place, here, *table)
    for mask in masks:
        if mask not in blocks:
            low = mask & -mask
            block = blocks[mask - low]
            if whole_groups:
                block, marks = lax.optimization_barrier((block, marks))
            blocks[mask] = from_member(block, low)
    blocks = [here] + [blocks[mask] for mask in masks]
    if not whole_groups:
        every = jnp.stack(blocks).reshape(members, clusters, members, half_rows, LANES)
        every = every.transpose(2, 0, 1, 3, 4).reshape(members, groups, LANES // 16, 16, LANES)
        every = every.transpose(1, 2, 0, 3, 4).reshape(groups, members * LANES, LANES)
        blocks = list(every)
        units, left, marks = first(place, blocks[0], *table)
    count = groups - 2
    *more, left, marks, best, mirror = pl.pallas_call(
        functools.partial(middle_kernel, count),
        out_shape=(*[units_shape] * count, *state_shape),
        in_specs=[smem] + [vmem] * (count + 6),
        out_specs=(vmem,) * (count + 4),
        scratch_shapes=code_scratch(count),
        input_output_aliases={count + 5 + which: count + which for which in range(2)},
        compiler_params=PARAMS,
        cost_estimate=cost(scores_flops // 2),
        name="middle_rows",
    )(place, *blocks[1 : 1 + count], *table, units, left, marks)
    nearest, *_ = pl.pallas_call(
        functools.partial(last_kernel, (capacity, clusters, members)),
        out_shape=(jax.ShapeDtypeStruct((tiles, LANES), f32), *state_shape),
        in_specs=[smem] + [vmem] * (groups + 7),
        out_specs=(vmem,) * 5,
        scratch_shapes=[pltpu.VMEM((width, members * COLS), bf16)] + code_scratch(1),
        input_output_aliases={groups + 4 + which: 1 + which for which in range(4)},
        compiler_params=PARAMS,
        cost_estimate=cost(scores_flops),
        name="last_rows",
    )(place, blocks[groups - 1], *table, units, *more, left, marks, best, mirror)
    return nearest.reshape(1, 1, slots)


def solution(mesh):
    in_specs = (P("cluster", "blk", None, None), P("cluster", "blk", None, None), P(), P())
    out_specs = P("cluster", "blk", None)
    return jax.shard_map(
        on_device, mesh=mesh, in_specs=in_specs, out_specs=out_specs, check_vma=False
    )
```

```python
import functools

import jax
import jax.numpy as jnp
from jax import lax
from jax.experimental import pallas as pl
from jax.experimental.pallas import tpu as pltpu
from jax.sharding import PartitionSpec as P

LANES = 128
COLS = 256
ROWS = 16
LOW = -4.0
VMEM_LIMIT = 40 * 1024 * 1024
PARAMS = pltpu.CompilerParams(vmem_limit_bytes=VMEM_LIMIT)


LANE_LOOKUP = lax.GatherDimensionNumbers(
    offset_dims=(),
    collapsed_slice_dims=(1,),
    start_index_map=(1,),
    operand_batching_dims=(0,),
    start_indices_batching_dims=(0,),
)


def take_lanes(table, index):
    return lax.gather(
        table, index[:, :, None], LANE_LOOKUP, (1, 1),
        mode=lax.GatherScatterMode.PROMISE_IN_BOUNDS,
    )


def pack_kernel(devices, capacity, rows_ref, out_ref):
    subspaces = rows_ref.shape[0] - 1
    in_rows = rows_ref.shape[1]
    half_rows = capacity // 2
    targets = rows_ref[subspaces:, :]
    hot = lax.broadcasted_iota(jnp.int32, (devices, in_rows), 0) == targets
    hot32 = jnp.where(hot, 1.0, 0.0)
    earlier = (
        lax.broadcasted_iota(jnp.int32, (in_rows, in_rows), 0)
        < lax.broadcasted_iota(jnp.int32, (in_rows, in_rows), 1)
    )
    running = jnp.dot(
        hot32.astype(jnp.bfloat16),
        jnp.where(earlier, 1.0, 0.0).astype(jnp.bfloat16),
        preferred_element_type=jnp.float32,
    )
    position = jnp.sum(hot32 * running, axis=0, keepdims=True).astype(jnp.int32)
    second = position >= half_rows
    key = targets * half_rows + jnp.where(second, position - half_rows, position)
    out_rows = devices * half_rows
    row_ids = lax.broadcasted_iota(jnp.int32, (out_rows, in_rows), 0)
    values = (rows_ref[:subspaces, :] + 1).astype(jnp.bfloat16)
    halves = []
    for wanted in (jnp.where(second, -1, key), jnp.where(second, key, -1)):
        move = jnp.where(row_ids == wanted, 1.0, 0.0).astype(jnp.bfloat16)
        halves.append(
            lax.dot_general(
                move, values, (((1,), (1,)), ((), ())), preferred_element_type=jnp.float32
            )
        )
    out_ref[...] = jnp.concatenate(halves, axis=1).astype(jnp.bfloat16)


def table_kernel(group_ref, book_ref, words_ref, centre_ref, norms_ref):
    width, words = words_ref.shape
    subspaces = norms_ref.shape[0]
    sub_width = width // subspaces
    block = ROWS * sub_width
    new = lax.broadcasted_iota(jnp.int32, (block, block), 0)
    old = lax.broadcasted_iota(jnp.int32, (block, block), 1)
    order = jnp.where(old == (new % ROWS) * sub_width + new // ROWS, 1.0, 0.0).astype(jnp.bfloat16)
    clusters = book_ref.shape[0] - words
    pick = lax.broadcasted_iota(jnp.int32, (1, clusters), 1) == group_ref[0, 0]
    for part in range(width // block):
        rows = slice(part * block, (part + 1) * block)
        turned = lax.dot_general(
            order, book_ref[:, rows], (((1,), (1,)), ((), ())), preferred_element_type=jnp.float32
        )
        centre = jnp.sum(jnp.where(pick, turned[:, words:], 0.0), axis=1, keepdims=True)
        words_ref[rows, :] = turned[:, :words].astype(jnp.bfloat16)
        centre_ref[rows, :] = jnp.broadcast_to(centre, (block, LANES))
        table = turned[:, :words] + centre
        norms_ref[part * ROWS : (part + 1) * ROWS, :] = jnp.sum(
            (table * table).reshape(sub_width, ROWS, words), axis=0
        )


def owner_block(codes_ref, owner, owners):
    parts = [
        codes_ref[pl.ds(pl.multiple_of((part * owners + owner) * 16, 16), 16), :]
        for part in range(LANES // 16)
    ]
    return jnp.concatenate(parts, axis=0)


def unpack_codes(block, norms_ref, code_ref, scale_ref, mark_ref, group, place):
    turned = jnp.transpose(block.astype(jnp.float32)).astype(jnp.int32)
    subspaces = turned.shape[0] // 2
    for half in range(2):
        part = turned[half * subspaces : (half + 1) * subspaces]
        code = jnp.maximum(part - 1, 0)
        code_ref[2 * group + half] = code
        mark_ref[2 * place + half] = jnp.where(part[0:8] > 0, 1.0, 0.0)
        low = code & (LANES - 1)
        squares = jnp.where(
            code >= LANES,
            take_lanes(norms_ref[:, LANES:], low),
            take_lanes(norms_ref[:, :LANES], low),
        )
        scale = lax.rsqrt(jnp.sum(squares, axis=0, keepdims=True) + 1e-06)
        scale_ref[2 * group + half] = jnp.broadcast_to(scale, (8, LANES))


def unpack_block(
    place, first, which, codes_ref, norms_ref, code_ref, scale_ref, mark_ref, owners, groups
):
    for turn in range(owners):
        owner = lax.rem(place + turn, owners)
        unpack_codes(
            owner_block(codes_ref, owner, owners), norms_ref, code_ref, scale_ref, mark_ref,
            which * owners + turn, turn * groups + first + which,
        )


def decode_steps(code_ref, scale_ref, tile, words_ref, centre_ref, units_ref, start):
    subspaces = code_ref.shape[1]
    sub_width = words_ref.shape[0] // subspaces

    def step(part):
        code = code_ref[tile, part * ROWS : (part + 1) * ROWS, :].astype(jnp.int16)
        scale = jnp.concatenate([scale_ref[tile]] * (ROWS // 8), axis=0)
        low = code & (LANES - 1)
        high = code > LANES - 1
        for entry in range(sub_width):
            row = (part * sub_width + entry) * ROWS
            rows = slice(row, row + ROWS)
            word = jnp.where(
                high,
                take_lanes(words_ref[rows, LANES:], low),
                take_lanes(words_ref[rows, :LANES], low),
            )
            unit = (word.astype(jnp.float32) + centre_ref[rows, :]) * scale
            units_ref[rows, pl.ds(start, LANES)] = unit.astype(jnp.bfloat16)

    return [functools.partial(step, part) for part in range(subspaces // ROWS)]


def run(steps):
    for step in steps:
        step()


def mix(some, others):
    done = 0
    for place, step in enumerate(some):
        step()
        upto = (place + 1) * len(others) // len(some)
        run(others[done:upto])
        done = upto


def turn_own(units_ref, left_ref, block):
    for half in range(2):
        start = block * COLS + half * LANES
        left_ref[start : start + LANES, :] = jnp.transpose(
            units_ref[:, half * LANES : (half + 1) * LANES]
        )


def score(left_ref, rows, units_ref, start, marks, best_ref):
    scores = jnp.dot(
        left_ref[rows, :], units_ref[:, pl.ds(start, COLS)], preferred_element_type=jnp.float32
    )
    best = best_ref[rows, :]
    for part in range(COLS // LANES):
        best = jnp.maximum(
            best, jnp.where(marks[part], scores[:, part * LANES : (part + 1) * LANES], LOW)
        )
    best_ref[rows, :] = best


def own_score(left_ref, units_ref, mark_ref, block, best_ref, mirror_ref):
    above, count = block * COLS, (block + 1) * COLS
    scores = jnp.dot(
        left_ref[:count, :], units_ref[:, :COLS], preferred_element_type=jnp.float32
    )
    row_ids = lax.broadcasted_iota(jnp.int32, (COLS, LANES), 0)
    lane_ids = lax.broadcasted_iota(jnp.int32, (COLS, LANES), 1)
    for part in range(COLS // LANES):
        tile = block * (COLS // LANES) + part
        lanes = slice(part * LANES, (part + 1) * LANES)
        filled = mark_ref[tile][0:1, :] > 0
        keep = filled & (row_ids != lane_ids + part * LANES)
        best_ref[above:count, :] = jnp.maximum(
            best_ref[above:count, :], jnp.where(keep, scores[above:count, lanes], LOW)
        )
        mirror = jnp.full((1, LANES), LOW, jnp.float32)
        for other in range(above // LANES):
            rows = slice(other * LANES, (other + 1) * LANES)
            piece = scores[rows, lanes]
            best_ref[rows, :] = jnp.maximum(best_ref[rows, :], jnp.where(filled, piece, LOW))
            row_filled = jnp.transpose(
                jnp.broadcast_to(mark_ref[other][0:1, :], (LANES, LANES))
            )
            mirror = jnp.maximum(
                mirror,
                jnp.max(jnp.where(row_filled > 0, piece, LOW), axis=0, keepdims=True),
            )
        mirror_ref[tile] = jnp.broadcast_to(mirror, (8, LANES))


def marks_of(mark_ref, group):
    return [mark_ref[2 * group + part][0:1, :] > 0 for part in range(COLS // LANES)]


def first_kernel(
    place_ref, codes_ref, words_ref, centre_ref, norms_ref,
    units_ref, left_ref, mark_ref, code_ref, scale_ref,
):
    owners = units_ref.shape[1] // COLS
    groups = left_ref.shape[0] // COLS
    unpack_block(
        place_ref[0, 0], 0, 0, codes_ref, norms_ref, code_ref, scale_ref, mark_ref, owners, groups
    )

    def one_group(turn, _):
        for half in range(2):
            start = pl.multiple_of(turn * COLS + half * LANES, LANES)
            run(
                decode_steps(
                    code_ref, scale_ref, 2 * turn + half, words_ref, centre_ref, units_ref, start
                )
            )
        return 0

    lax.fori_loop(0, owners, one_group, 0)
    turn_own(units_ref, left_ref, 0)


def block_kernel(block, place, codes_ref, table_refs, units_refs, state):
    left_ref, mark_ref, best_ref, mirror_ref, code_ref, scale_ref = state
    words_ref, centre_ref, norms_ref = table_refs
    units_ref = units_refs[block]
    owners = units_ref.shape[1] // COLS
    groups = left_ref.shape[0] // COLS
    unpack_block(
        place, block, 0, codes_ref, norms_ref, code_ref, scale_ref, mark_ref, owners, groups
    )

    def decoding(turn):
        steps = []
        for half in range(2):
            start = turn * COLS + half * LANES
            if not isinstance(turn, int):
                start = pl.multiple_of(start, LANES)
            steps += decode_steps(
                code_ref, scale_ref, 2 * turn + half, words_ref, centre_ref, units_ref, start
            )
        return steps

    run(decoding(0))
    turn_own(units_ref, left_ref, block)
    own_score(left_ref, units_ref, mark_ref, block, best_ref, mirror_ref)

    def both(turn, _):
        column = pl.multiple_of(turn * COLS, LANES)
        pairs = [(block - 1, chunk) for chunk in range(block + 1)]
        pairs += [(earlier, block) for earlier in range(block - 1)]
        scoring = [
            functools.partial(
                score, left_ref, slice(chunk * COLS, (chunk + 1) * COLS), units_refs[which],
                column, marks_of(mark_ref, turn * groups + which), best_ref,
            )
            for which, chunk in pairs
        ]
        mix(scoring, decoding(turn))
        return 0

    lax.fori_loop(1, owners, both, 0)


def next_kernel(block, place_ref, codes_ref, *refs):
    table_refs, refs = refs[:3], refs[3:]
    units_refs, refs = refs[:block], refs[block:]
    units_ref, left_ref, mark_ref, best_ref, mirror_ref, code_ref, scale_ref = refs[-7:]
    if block == 1:
        best_ref[...] = jnp.full(best_ref.shape, LOW, jnp.float32)
        own_score(left_ref, units_refs[0], mark_ref, 0, best_ref, mirror_ref)
    block_kernel(
        block, place_ref[0, 0], codes_ref, table_refs, [*units_refs, units_ref],
        (left_ref, mark_ref, best_ref, mirror_ref, code_ref, scale_ref),
    )


def last_kernel(sizes, place_ref, codes_ref, *refs):
    capacity, clusters, members = sizes
    place = place_ref[0, 0]
    table_refs, refs = refs[:3], refs[3:]
    units_refs, refs = refs[:-12], refs[-8:]
    out_ref, left_ref, mark_ref, best_ref, mirror_ref, units_ref, code_ref, scale_ref = refs
    slots = left_ref.shape[0]
    groups = slots // COLS
    owners = units_ref.shape[1] // COLS
    block_kernel(
        groups - 1, place, codes_ref, table_refs, [*units_refs, units_ref],
        (left_ref, mark_ref, best_ref, mirror_ref, code_ref, scale_ref),
    )

    def rest(turn, _):
        column = pl.multiple_of(turn * COLS, LANES)
        score(
            left_ref, slice(0, slots), units_ref, column,
            marks_of(mark_ref, turn * groups + groups - 1), best_ref,
        )
        return 0

    lax.fori_loop(1, owners, rest, 0)

    half_rows = capacity // 2
    tiles = slots // LANES
    lane = lax.broadcasted_iota(jnp.int32, (tiles, LANES), 1)
    slot = lax.broadcasted_iota(jnp.int32, (tiles, LANES), 0) * LANES + lane
    source, within = slot // capacity, slot % capacity
    turn = place ^ (source % members)
    own_row = (turn * clusters + source // members) * half_rows + within % half_rows
    tile_of = 2 * (own_row // LANES) + within // half_rows
    result = jnp.zeros((tiles, LANES), jnp.float32)
    for tile in range(tiles):
        best = jnp.max(
            jnp.transpose(best_ref[tile * LANES : (tile + 1) * LANES, :]), axis=0, keepdims=True
        )
        best = jnp.maximum(best, mirror_ref[tile][0:1, :])
        mark = mark_ref[tile]
        best = jnp.where(mark[0:1, :] > 0, best, 0.0)
        result = jnp.where(
            tile_of == tile,
            take_lanes(jnp.broadcast_to(best, (tiles, LANES)), own_row % LANES),
            result,
        )
    out_ref[...] = result


def on_device(codes, routes, codebook, centroids):
    clusters = lax.axis_size("cluster")
    members = lax.axis_size("blk")
    devices = clusters * members
    subspaces, in_rows = codes.shape[2:]
    capacity = 2 * in_rows // devices
    half_rows = capacity // 2
    slots = devices * capacity
    tiles = slots // LANES
    groups = slots // COLS
    words, width = codebook.shape
    bf16, f32, i32 = jnp.bfloat16, jnp.float32, jnp.int32
    smem = pl.BlockSpec(memory_space=pltpu.SMEM)
    vmem = pl.BlockSpec(memory_space=pltpu.VMEM)

    packed = pl.pallas_call(
        functools.partial(pack_kernel, devices, capacity),
        out_shape=jax.ShapeDtypeStruct((in_rows, 2 * subspaces), bf16),
        compiler_params=PARAMS,
        name="pack_rows",
    )(jnp.concatenate([codes[0, 0], routes.reshape(1, in_rows)], axis=0))
    here = lax.all_to_all(packed, "cluster", split_axis=0, concat_axis=0, tiled=True)
    def from_member(block, mask):
        return lax.ppermute(block, "blk", [(i, i ^ mask) for i in range(members)])

    masks = range(1, members)
    blocks = {0: here}
    for mask in masks:
        if mask & (mask - 1) == 0:
            blocks[mask] = from_member(here, mask)

    place = lax.axis_index("blk").astype(i32).reshape(1, 1)
    group = lax.axis_index("cluster").astype(i32).reshape(1, 1)
    table = pl.pallas_call(
        table_kernel,
        out_shape=(
            jax.ShapeDtypeStruct((width, words), bf16),
            jax.ShapeDtypeStruct((width, LANES), f32),
            jax.ShapeDtypeStruct((subspaces, words), f32),
        ),
        in_specs=[smem, vmem],
        compiler_params=PARAMS,
        cost_estimate=pl.CostEstimate(
            flops=4 * words * width, bytes_accessed=6 * words * width, transcendentals=0
        ),
        name="word_table",
    )(group, jnp.concatenate([codebook, centroids], axis=0))

    units_shape = jax.ShapeDtypeStruct((width, members * COLS), bf16)
    state_shape = (
        jax.ShapeDtypeStruct((slots, width), bf16),
        jax.ShapeDtypeStruct((2 * members * groups, 8, LANES), f32),
        jax.ShapeDtypeStruct((slots, LANES), f32),
        jax.ShapeDtypeStruct((tiles, 8, LANES), f32),
    )

    def code_scratch(count):
        return [
            pltpu.VMEM((2 * members * count, subspaces, LANES), i32),
            pltpu.VMEM((2 * members * count, 8, LANES), f32),
        ]

    def cost(flops):
        return pl.CostEstimate(
            flops=flops, bytes_accessed=16 * slots * width, transcendentals=0
        )

    scores_flops = 2 * slots * members * slots * width
    first = pl.pallas_call(
        first_kernel,
        out_shape=(units_shape, *state_shape[:2]),
        in_specs=[smem] + [vmem] * 4,
        out_specs=(vmem,) * 3,
        scratch_shapes=code_scratch(1),
        compiler_params=PARAMS,
        cost_estimate=cost(scores_flops // 4),
        name="first_rows",
    )
    def take_in(block, codes_in, units, state):
        kept = len(state)
        outs = pl.pallas_call(
            functools.partial(next_kernel, block),
            out_shape=(units_shape, *state_shape),
            in_specs=[smem] + [vmem] * (4 + block + kept),
            out_specs=(vmem,) * 5,
            scratch_shapes=code_scratch(1),
            input_output_aliases={5 + block + which: 1 + which for which in range(kept)},
            compiler_params=PARAMS,
            cost_estimate=cost(scores_flops // 4),
            name="next_rows",
        )(place, codes_in, *table, *units, *state)
        return [*units, outs[0]], outs[1:]

    whole_groups = half_rows == 16 and clusters * half_rows == LANES
    if whole_groups:
        near, *state = first(place, here, *table)
        units, state = take_in(1, blocks[1], [near], state)
    for mask in masks:
        if mask not in blocks:
            low = mask & -mask
            block = blocks[mask - low]
            if whole_groups:
                left, marks, best, mirror = state
                block, marks = lax.optimization_barrier((block, marks))
                state = (left, marks, best, mirror)
            blocks[mask] = from_member(block, low)
    blocks = [here] + [blocks[mask] for mask in masks]
    if not whole_groups:
        every = jnp.stack(blocks).reshape(members, clusters, members, half_rows, LANES)
        every = every.transpose(2, 0, 1, 3, 4).reshape(members, groups, LANES // 16, 16, LANES)
        every = every.transpose(1, 2, 0, 3, 4).reshape(groups, members * LANES, LANES)
        blocks = list(every)
        near, *state = first(place, blocks[0], *table)
        units, state = take_in(1, blocks[1], [near], state)
    for block in range(2, groups - 1):
        units, state = take_in(block, blocks[block], units, state)
    nearest, *_ = pl.pallas_call(
        functools.partial(last_kernel, (capacity, clusters, members)),
        out_shape=(jax.ShapeDtypeStruct((tiles, LANES), f32), *state_shape),
        in_specs=[smem] + [vmem] * (groups + 7),
        out_specs=(vmem,) * 5,
        scratch_shapes=[pltpu.VMEM((width, members * COLS), bf16)] + code_scratch(1),
        input_output_aliases={groups + 4 + which: 1 + which for which in range(4)},
        compiler_params=PARAMS,
        cost_estimate=cost(scores_flops),
        name="last_rows",
    )(place, blocks[groups - 1], *table, *units, *state)
    return nearest.reshape(1, 1, slots)


def solution(mesh):
    in_specs = (P("cluster", "blk", None, None), P("cluster", "blk", None, None), P(), P())
    out_specs = P("cluster", "blk", None)
    return jax.shard_map(
        on_device, mesh=mesh, in_specs=in_specs, out_specs=out_specs, check_vma=False
    )
```

```python
import functools

import jax
import jax.numpy as jnp
from jax import lax
from jax.experimental import pallas as pl
from jax.experimental.pallas import tpu as pltpu
from jax.sharding import PartitionSpec as P

LANES = 128
COLS = 256
ROWS = 16
HELD = 3
LOW = -4.0
VMEM_LIMIT = 40 * 1024 * 1024
PARAMS = pltpu.CompilerParams(vmem_limit_bytes=VMEM_LIMIT)


LANE_LOOKUP = lax.GatherDimensionNumbers(
    offset_dims=(),
    collapsed_slice_dims=(1,),
    start_index_map=(1,),
    operand_batching_dims=(0,),
    start_indices_batching_dims=(0,),
)


def take_lanes(table, index):
    return lax.gather(
        table, index[:, :, None], LANE_LOOKUP, (1, 1),
        mode=lax.GatherScatterMode.PROMISE_IN_BOUNDS,
    )


def pack_kernel(devices, capacity, rows_ref, out_ref):
    subspaces = rows_ref.shape[0] - 1
    in_rows = rows_ref.shape[1]
    half_rows = capacity // 2
    targets = rows_ref[subspaces:, :]
    hot = lax.broadcasted_iota(jnp.int32, (devices, in_rows), 0) == targets
    hot32 = jnp.where(hot, 1.0, 0.0)
    earlier = (
        lax.broadcasted_iota(jnp.int32, (in_rows, in_rows), 0)
        < lax.broadcasted_iota(jnp.int32, (in_rows, in_rows), 1)
    )
    running = jnp.dot(
        hot32.astype(jnp.bfloat16),
        jnp.where(earlier, 1.0, 0.0).astype(jnp.bfloat16),
        preferred_element_type=jnp.float32,
    )
    position = jnp.sum(hot32 * running, axis=0, keepdims=True).astype(jnp.int32)
    second = position >= half_rows
    key = targets * half_rows + jnp.where(second, position - half_rows, position)
    out_rows = devices * half_rows
    row_ids = lax.broadcasted_iota(jnp.int32, (out_rows, in_rows), 0)
    values = (rows_ref[:subspaces, :] + 1).astype(jnp.bfloat16)
    halves = []
    for wanted in (jnp.where(second, -1, key), jnp.where(second, key, -1)):
        move = jnp.where(row_ids == wanted, 1.0, 0.0).astype(jnp.bfloat16)
        halves.append(
            lax.dot_general(
                move, values, (((1,), (1,)), ((), ())), preferred_element_type=jnp.float32
            )
        )
    out_ref[...] = jnp.concatenate(halves, axis=1).astype(jnp.bfloat16)


def table_kernel(group_ref, book_ref, words_ref, centre_ref, norms_ref):
    width, words = words_ref.shape
    subspaces = norms_ref.shape[0]
    sub_width = width // subspaces
    block = ROWS * sub_width
    new = lax.broadcasted_iota(jnp.int32, (block, block), 0)
    old = lax.broadcasted_iota(jnp.int32, (block, block), 1)
    order = jnp.where(old == (new % ROWS) * sub_width + new // ROWS, 1.0, 0.0).astype(jnp.bfloat16)
    clusters = book_ref.shape[0] - words
    pick = lax.broadcasted_iota(jnp.int32, (1, clusters), 1) == group_ref[0, 0]
    for part in range(width // block):
        rows = slice(part * block, (part + 1) * block)
        turned = lax.dot_general(
            order, book_ref[:, rows], (((1,), (1,)), ((), ())), preferred_element_type=jnp.float32
        )
        centre = jnp.sum(jnp.where(pick, turned[:, words:], 0.0), axis=1, keepdims=True)
        words_ref[rows, :] = turned[:, :words].astype(jnp.bfloat16)
        centre_ref[rows, :] = jnp.broadcast_to(centre, (block, LANES))
        table = turned[:, :words] + centre
        norms_ref[part * ROWS : (part + 1) * ROWS, :] = jnp.sum(
            (table * table).reshape(sub_width, ROWS, words), axis=0
        )


def owner_block(codes_ref, owner, owners):
    parts = [
        codes_ref[pl.ds(pl.multiple_of((part * owners + owner) * 16, 16), 16), :]
        for part in range(LANES // 16)
    ]
    return jnp.concatenate(parts, axis=0)


def unpack_codes(block, norms_ref, code_ref, scale_ref, mark_ref, group, place):
    turned = jnp.transpose(block.astype(jnp.float32)).astype(jnp.int32)
    subspaces = turned.shape[0] // 2
    for half in range(2):
        part = turned[half * subspaces : (half + 1) * subspaces]
        code = jnp.maximum(part - 1, 0)
        code_ref[2 * group + half] = code
        mark_ref[2 * place + half] = jnp.where(part[0:8] > 0, 1.0, 0.0)
        low = code & (LANES - 1)
        squares = jnp.where(
            code >= LANES,
            take_lanes(norms_ref[:, LANES:], low),
            take_lanes(norms_ref[:, :LANES], low),
        )
        scale = lax.rsqrt(jnp.sum(squares, axis=0, keepdims=True) + 1e-06)
        scale_ref[2 * group + half] = jnp.broadcast_to(scale, (8, LANES))


def unpack_block(
    place, first, which, codes_ref, norms_ref, code_ref, scale_ref, mark_ref, owners, groups
):
    for turn in range(owners):
        owner = lax.rem(place + turn, owners)
        unpack_codes(
            owner_block(codes_ref, owner, owners), norms_ref, code_ref, scale_ref, mark_ref,
            which * owners + turn, turn * groups + first + which,
        )


def decode_steps(code_ref, scale_ref, tile, words_ref, centre_ref, units_ref, start):
    subspaces = code_ref.shape[1]
    sub_width = words_ref.shape[0] // subspaces

    def step(part):
        code = code_ref[tile, part * ROWS : (part + 1) * ROWS, :].astype(jnp.int16)
        scale = jnp.concatenate([scale_ref[tile]] * (ROWS // 8), axis=0)
        low = code & (LANES - 1)
        high = code > LANES - 1
        values = []
        for entry in range(sub_width):
            row = (part * sub_width + entry) * ROWS
            rows = slice(row, row + ROWS)
            word = jnp.where(
                high,
                take_lanes(words_ref[rows, LANES:], low),
                take_lanes(words_ref[rows, :LANES], low),
            )
            unit = (word.astype(jnp.float32) + centre_ref[rows, :]) * scale
            values.append((rows, unit.astype(jnp.bfloat16)))
        return values

    def put(values):
        for rows, value in values:
            units_ref[rows, pl.ds(start, LANES)] = value

    return [(functools.partial(step, part), put) for part in range(subspaces // ROWS)]


def run(decoding):
    for step, put in decoding:
        put(step())


def mix(scoring, decoding):
    done = 0
    for place, score_chunk in enumerate(scoring):
        upto = (place + 1) * len(decoding) // len(scoring)
        beside = decoding[done : min(upto, done + HELD)]
        held = [(step(), put) for step, put in beside]
        score_chunk()
        for values, put in held:
            put(values)
        run(decoding[done + len(beside) : upto])
        done = upto


def turn_own(units_ref, left_ref, block):
    for half in range(2):
        start = block * COLS + half * LANES
        left_ref[start : start + LANES, :] = jnp.transpose(
            units_ref[:, half * LANES : (half + 1) * LANES]
        )


def score(left_ref, rows, units_ref, start, marks, best_ref):
    scores = jnp.dot(
        left_ref[rows, :], units_ref[:, pl.ds(start, COLS)], preferred_element_type=jnp.float32
    )
    best = best_ref[rows, :]
    for part in range(COLS // LANES):
        best = jnp.maximum(
            best, jnp.where(marks[part], scores[:, part * LANES : (part + 1) * LANES], LOW)
        )
    best_ref[rows, :] = best


def own_score(left_ref, chunk, units_ref, block, mark_ref, best_ref, mirror_ref):
    start = chunk * COLS
    scores = jnp.dot(
        left_ref[start : start + COLS, :], units_ref[:, :COLS],
        preferred_element_type=jnp.float32,
    )
    row_ids = lax.broadcasted_iota(jnp.int32, (COLS, LANES), 0)
    lane_ids = lax.broadcasted_iota(jnp.int32, (COLS, LANES), 1)
    best = best_ref[start : start + COLS, :]
    for part in range(COLS // LANES):
        tile = block * (COLS // LANES) + part
        piece = scores[:, part * LANES : (part + 1) * LANES]
        keep = mark_ref[tile][0:1, :] > 0
        if chunk == block:
            keep = keep & (row_ids != lane_ids + part * LANES)
        best = jnp.maximum(best, jnp.where(keep, piece, LOW))
        if chunk == 0:
            mirror = jnp.full((8, LANES), LOW, jnp.float32)
        else:
            mirror = mirror_ref[tile]
        if chunk < block:
            for other in range(COLS // LANES):
                row_marks = mark_ref[chunk * (COLS // LANES) + other][0:1, :]
                row_filled = jnp.transpose(jnp.broadcast_to(row_marks, (LANES, LANES))) > 0
                across = jnp.where(
                    row_filled, piece[other * LANES : (other + 1) * LANES], LOW
                )
                mirror = jnp.maximum(mirror, jnp.max(across, axis=0, keepdims=True))
        mirror_ref[tile] = mirror
    best_ref[start : start + COLS, :] = best


def marks_of(mark_ref, group):
    return [mark_ref[2 * group + part][0:1, :] > 0 for part in range(COLS // LANES)]


def block_kernel(block, place, codes_ref, table_refs, units_refs, state):
    left_ref, mark_ref, best_ref, mirror_ref, code_ref, scale_ref = state
    words_ref, centre_ref, norms_ref = table_refs
    units_ref = units_refs[block]
    owners = units_ref.shape[1] // COLS
    groups = left_ref.shape[0] // COLS
    unpack_block(
        place, block, 0, codes_ref, norms_ref, code_ref, scale_ref, mark_ref, owners, groups
    )

    def column_of(turn, offset=0):
        column = turn * COLS + offset
        return column if isinstance(turn, int) else pl.multiple_of(column, LANES)

    def decoding(turn):
        steps = []
        for half in range(2):
            steps += decode_steps(
                code_ref, scale_ref, 2 * turn + half, words_ref, centre_ref, units_ref,
                column_of(turn, half * LANES),
            )
        return steps

    def scoring(which, turn, chunks):
        return [
            functools.partial(
                score, left_ref, slice(chunk * COLS, (chunk + 1) * COLS), units_refs[which],
                column_of(turn), marks_of(mark_ref, turn * groups + which), best_ref,
            )
            for chunk in chunks
        ]

    if block == 0:
        best_ref[...] = jnp.full(best_ref.shape, LOW, jnp.float32)
        run(decoding(0))
    else:
        mix(scoring(block - 1, owners - 1, range(block)), decoding(0))
    turn_own(units_ref, left_ref, block)

    steps = [
        functools.partial(
            own_score, left_ref, chunk, units_ref, block, mark_ref, best_ref, mirror_ref
        )
        for chunk in range(block + 1)
    ]
    for which in range(block):
        steps += scoring(which, 1, [block])
    mix(steps, decoding(1))

    def both(turn, _):
        steps = scoring(block, turn - 1, range(block + 1))
        for which in range(block):
            steps += scoring(which, turn, [block])
        mix(steps, decoding(turn))
        return 0

    lax.fori_loop(2, owners, both, 0)


def next_kernel(block, place_ref, codes_ref, *refs):
    table_refs, refs = refs[:3], refs[3:]
    units_refs, refs = refs[:block], refs[block:]
    units_ref, left_ref, mark_ref, best_ref, mirror_ref, code_ref, scale_ref = refs[-7:]
    block_kernel(
        block, place_ref[0, 0], codes_ref, table_refs, [*units_refs, units_ref],
        (left_ref, mark_ref, best_ref, mirror_ref, code_ref, scale_ref),
    )


def last_kernel(sizes, place_ref, codes_ref, *refs):
    capacity, clusters, members = sizes
    place = place_ref[0, 0]
    table_refs, refs = refs[:3], refs[3:]
    units_refs, refs = refs[:-12], refs[-8:]
    out_ref, left_ref, mark_ref, best_ref, mirror_ref, units_ref, code_ref, scale_ref = refs
    slots = left_ref.shape[0]
    groups = slots // COLS
    owners = units_ref.shape[1] // COLS
    block_kernel(
        groups - 1, place, codes_ref, table_refs, [*units_refs, units_ref],
        (left_ref, mark_ref, best_ref, mirror_ref, code_ref, scale_ref),
    )

    final = (owners - 1) * groups + groups - 1
    score(
        left_ref, slice(0, slots), units_ref, (owners - 1) * COLS, marks_of(mark_ref, final),
        best_ref,
    )

    half_rows = capacity // 2
    tiles = slots // LANES
    lane = lax.broadcasted_iota(jnp.int32, (tiles, LANES), 1)
    slot = lax.broadcasted_iota(jnp.int32, (tiles, LANES), 0) * LANES + lane
    source, within = slot // capacity, slot % capacity
    turn = place ^ (source % members)
    own_row = (turn * clusters + source // members) * half_rows + within % half_rows
    tile_of = 2 * (own_row // LANES) + within // half_rows
    result = jnp.zeros((tiles, LANES), jnp.float32)
    for tile in range(tiles):
        best = jnp.max(
            jnp.transpose(best_ref[tile * LANES : (tile + 1) * LANES, :]), axis=0, keepdims=True
        )
        best = jnp.maximum(best, mirror_ref[tile][0:1, :])
        mark = mark_ref[tile]
        best = jnp.where(mark[0:1, :] > 0, best, 0.0)
        result = jnp.where(
            tile_of == tile,
            take_lanes(jnp.broadcast_to(best, (tiles, LANES)), own_row % LANES),
            result,
        )
    out_ref[...] = result


def on_device(codes, routes, codebook, centroids):
    clusters = lax.axis_size("cluster")
    members = lax.axis_size("blk")
    devices = clusters * members
    subspaces, in_rows = codes.shape[2:]
    capacity = 2 * in_rows // devices
    half_rows = capacity // 2
    slots = devices * capacity
    tiles = slots // LANES
    groups = slots // COLS
    words, width = codebook.shape
    bf16, f32, i32 = jnp.bfloat16, jnp.float32, jnp.int32
    smem = pl.BlockSpec(memory_space=pltpu.SMEM)
    vmem = pl.BlockSpec(memory_space=pltpu.VMEM)

    packed = pl.pallas_call(
        functools.partial(pack_kernel, devices, capacity),
        out_shape=jax.ShapeDtypeStruct((in_rows, 2 * subspaces), bf16),
        compiler_params=PARAMS,
        name="pack_rows",
    )(jnp.concatenate([codes[0, 0], routes.reshape(1, in_rows)], axis=0))
    here = lax.all_to_all(packed, "cluster", split_axis=0, concat_axis=0, tiled=True)
    def from_member(block, mask):
        return lax.ppermute(block, "blk", [(i, i ^ mask) for i in range(members)])

    masks = range(1, members)
    blocks = {0: here}
    for mask in masks:
        if mask & (mask - 1) == 0:
            blocks[mask] = from_member(here, mask)

    place = lax.axis_index("blk").astype(i32).reshape(1, 1)
    group = lax.axis_index("cluster").astype(i32).reshape(1, 1)
    table = pl.pallas_call(
        table_kernel,
        out_shape=(
            jax.ShapeDtypeStruct((width, words), bf16),
            jax.ShapeDtypeStruct((width, LANES), f32),
            jax.ShapeDtypeStruct((subspaces, words), f32),
        ),
        in_specs=[smem, vmem],
        compiler_params=PARAMS,
        cost_estimate=pl.CostEstimate(
            flops=4 * words * width, bytes_accessed=6 * words * width, transcendentals=0
        ),
        name="word_table",
    )(group, jnp.concatenate([codebook, centroids], axis=0))

    units_shape = jax.ShapeDtypeStruct((width, members * COLS), bf16)
    state_shape = (
        jax.ShapeDtypeStruct((slots, width), bf16),
        jax.ShapeDtypeStruct((2 * members * groups, 8, LANES), f32),
        jax.ShapeDtypeStruct((slots, LANES), f32),
        jax.ShapeDtypeStruct((tiles, 8, LANES), f32),
    )

    def code_scratch(count):
        return [
            pltpu.VMEM((2 * members * count, subspaces, LANES), i32),
            pltpu.VMEM((2 * members * count, 8, LANES), f32),
        ]

    def cost(flops):
        return pl.CostEstimate(
            flops=flops, bytes_accessed=16 * slots * width, transcendentals=0
        )

    scores_flops = 2 * slots * members * slots * width
    def take_in(block, codes_in, units, state):
        kept = len(state)
        outs = pl.pallas_call(
            functools.partial(next_kernel, block),
            out_shape=(units_shape, *state_shape),
            in_specs=[smem] + [vmem] * (4 + block + kept),
            out_specs=(vmem,) * 5,
            scratch_shapes=code_scratch(1),
            input_output_aliases={5 + block + which: 1 + which for which in range(kept)},
            compiler_params=PARAMS,
            cost_estimate=cost(scores_flops // 4),
            name=f"rows_{block}",
        )(place, codes_in, *table, *units, *state)
        return [*units, outs[0]], outs[1:]

    whole_groups = half_rows == 16 and clusters * half_rows == LANES
    if whole_groups:
        units, state = take_in(0, here, [], ())
        units, state = take_in(1, blocks[1], units, state)
    for mask in masks:
        if mask not in blocks:
            low = mask & -mask
            block = blocks[mask - low]
            if whole_groups:
                left, marks, best, mirror = state
                block, marks = lax.optimization_barrier((block, marks))
                state = (left, marks, best, mirror)
            blocks[mask] = from_member(block, low)
    blocks = [here] + [blocks[mask] for mask in masks]
    if not whole_groups:
        every = jnp.stack(blocks).reshape(members, clusters, members, half_rows, LANES)
        every = every.transpose(2, 0, 1, 3, 4).reshape(members, groups, LANES // 16, 16, LANES)
        every = every.transpose(1, 2, 0, 3, 4).reshape(groups, members * LANES, LANES)
        blocks = list(every)
        units, state = take_in(0, blocks[0], [], ())
        units, state = take_in(1, blocks[1], units, state)
    for block in range(2, groups - 1):
        units, state = take_in(block, blocks[block], units, state)
    nearest, *_ = pl.pallas_call(
        functools.partial(last_kernel, (capacity, clusters, members)),
        out_shape=(jax.ShapeDtypeStruct((tiles, LANES), f32), *state_shape),
        in_specs=[smem] + [vmem] * (groups + 7),
        out_specs=(vmem,) * 5,
        scratch_shapes=[pltpu.VMEM((width, members * COLS), bf16)] + code_scratch(1),
        input_output_aliases={groups + 4 + which: 1 + which for which in range(4)},
        compiler_params=PARAMS,
        cost_estimate=cost(scores_flops),
        name="last_rows",
    )(place, blocks[groups - 1], *table, *units, *state)
    return nearest.reshape(1, 1, slots)


def solution(mesh):
    in_specs = (P("cluster", "blk", None, None), P("cluster", "blk", None, None), P(), P())
    out_specs = P("cluster", "blk", None)
    return jax.shard_map(
        on_device, mesh=mesh, in_specs=in_specs, out_specs=out_specs, check_vma=False
    )
```

```python
import functools

import jax
import jax.numpy as jnp
from jax import lax
from jax.experimental import pallas as pl
from jax.experimental.pallas import tpu as pltpu
from jax.sharding import PartitionSpec as P

LANES = 128
COLS = 256
ROWS = 16
HELD = 3
DEPTH = 256
LOW = -4.0
VMEM_LIMIT = 40 * 1024 * 1024
PARAMS = pltpu.CompilerParams(vmem_limit_bytes=VMEM_LIMIT)


LANE_LOOKUP = lax.GatherDimensionNumbers(
    offset_dims=(),
    collapsed_slice_dims=(1,),
    start_index_map=(1,),
    operand_batching_dims=(0,),
    start_indices_batching_dims=(0,),
)


def take_lanes(table, index):
    return lax.gather(
        table, index[:, :, None], LANE_LOOKUP, (1, 1),
        mode=lax.GatherScatterMode.PROMISE_IN_BOUNDS,
    )


def pack_kernel(devices, capacity, rows_ref, out_ref):
    subspaces = rows_ref.shape[0] - 1
    in_rows = rows_ref.shape[1]
    half_rows = capacity // 2
    targets = rows_ref[subspaces:, :]
    hot = lax.broadcasted_iota(jnp.int32, (devices, in_rows), 0) == targets
    hot32 = jnp.where(hot, 1.0, 0.0)
    earlier = (
        lax.broadcasted_iota(jnp.int32, (in_rows, in_rows), 0)
        < lax.broadcasted_iota(jnp.int32, (in_rows, in_rows), 1)
    )
    running = jnp.dot(
        hot32.astype(jnp.bfloat16),
        jnp.where(earlier, 1.0, 0.0).astype(jnp.bfloat16),
        preferred_element_type=jnp.float32,
    )
    position = jnp.sum(hot32 * running, axis=0, keepdims=True).astype(jnp.int32)
    second = position >= half_rows
    key = targets * half_rows + jnp.where(second, position - half_rows, position)
    out_rows = devices * half_rows
    row_ids = lax.broadcasted_iota(jnp.int32, (out_rows, in_rows), 0)
    values = (rows_ref[:subspaces, :] + 1).astype(jnp.bfloat16)
    halves = []
    for wanted in (jnp.where(second, -1, key), jnp.where(second, key, -1)):
        move = jnp.where(row_ids == wanted, 1.0, 0.0).astype(jnp.bfloat16)
        halves.append(
            lax.dot_general(
                move, values, (((1,), (1,)), ((), ())), preferred_element_type=jnp.float32
            )
        )
    out_ref[...] = jnp.concatenate(halves, axis=1).astype(jnp.bfloat16)


def table_kernel(group_ref, book_ref, words_ref, centre_ref, norms_ref):
    width, words = words_ref.shape
    subspaces = norms_ref.shape[0]
    sub_width = width // subspaces
    block = ROWS * sub_width
    new = lax.broadcasted_iota(jnp.int32, (block, block), 0)
    old = lax.broadcasted_iota(jnp.int32, (block, block), 1)
    order = jnp.where(old == (new % ROWS) * sub_width + new // ROWS, 1.0, 0.0).astype(jnp.bfloat16)
    clusters = book_ref.shape[0] - words
    pick = lax.broadcasted_iota(jnp.int32, (1, clusters), 1) == group_ref[0, 0]
    for part in range(width // block):
        rows = slice(part * block, (part + 1) * block)
        turned = lax.dot_general(
            order, book_ref[:, rows], (((1,), (1,)), ((), ())), preferred_element_type=jnp.float32
        )
        centre = jnp.sum(jnp.where(pick, turned[:, words:], 0.0), axis=1, keepdims=True)
        words_ref[rows, :] = turned[:, :words].astype(jnp.bfloat16)
        centre_ref[rows, :] = jnp.broadcast_to(centre, (block, LANES))
        table = turned[:, :words] + centre
        norms_ref[part * ROWS : (part + 1) * ROWS, :] = jnp.sum(
            (table * table).reshape(sub_width, ROWS, words), axis=0
        )


def owner_block(codes_ref, owner, owners):
    parts = [
        codes_ref[pl.ds(pl.multiple_of((part * owners + owner) * 16, 16), 16), :]
        for part in range(LANES // 16)
    ]
    return jnp.concatenate(parts, axis=0)


def unpack_codes(block, norms_ref, code_ref, scale_ref, mark_ref, group, place):
    turned = jnp.transpose(block.astype(jnp.float32)).astype(jnp.int32)
    subspaces = turned.shape[0] // 2
    for half in range(2):
        part = turned[half * subspaces : (half + 1) * subspaces]
        code = jnp.maximum(part - 1, 0)
        code_ref[2 * group + half] = code
        mark_ref[2 * place + half] = jnp.where(part[0:8] > 0, 1.0, 0.0)
        low = code & (LANES - 1)
        squares = jnp.where(
            code >= LANES,
            take_lanes(norms_ref[:, LANES:], low),
            take_lanes(norms_ref[:, :LANES], low),
        )
        scale = lax.rsqrt(jnp.sum(squares, axis=0, keepdims=True) + 1e-06)
        scale_ref[2 * group + half] = jnp.broadcast_to(scale, (8, LANES))


def unpack_block(
    place, first, which, codes_ref, norms_ref, code_ref, scale_ref, mark_ref, owners, groups
):
    for turn in range(owners):
        owner = lax.rem(place + turn, owners)
        unpack_codes(
            owner_block(codes_ref, owner, owners), norms_ref, code_ref, scale_ref, mark_ref,
            which * owners + turn, turn * groups + first + which,
        )


def decode_steps(code_ref, scale_ref, tile, words_ref, centre_ref, units_ref, start):
    subspaces = code_ref.shape[1]
    sub_width = words_ref.shape[0] // subspaces

    def step(part):
        code = code_ref[tile, part * ROWS : (part + 1) * ROWS, :].astype(jnp.int16)
        scale = jnp.concatenate([scale_ref[tile]] * (ROWS // 8), axis=0)
        low = code & (LANES - 1)
        high = code > LANES - 1
        values = []
        for entry in range(sub_width):
            row = (part * sub_width + entry) * ROWS
            rows = slice(row, row + ROWS)
            word = jnp.where(
                high,
                take_lanes(words_ref[rows, LANES:], low),
                take_lanes(words_ref[rows, :LANES], low),
            )
            unit = (word.astype(jnp.float32) + centre_ref[rows, :]) * scale
            values.append((rows, unit.astype(jnp.bfloat16)))
        return values

    def put(values):
        for rows, value in values:
            units_ref[rows, pl.ds(start, LANES)] = value

    return [(functools.partial(step, part), put) for part in range(subspaces // ROWS)]


def run(decoding):
    for step, put in decoding:
        put(step())


def mix(scoring, decoding):
    done = 0
    for place, score_chunk in enumerate(scoring):
        upto = (place + 1) * len(decoding) // len(scoring)
        beside = decoding[done : min(upto, done + HELD)]
        held = [(step(), put) for step, put in beside]
        score_chunk()
        for values, put in held:
            put(values)
        run(decoding[done + len(beside) : upto])
        done = upto


def turn_own(units_ref, left_ref, block):
    for half in range(2):
        start = block * COLS + half * LANES
        left_ref[start : start + LANES, :] = jnp.transpose(
            units_ref[:, half * LANES : (half + 1) * LANES]
        )


def products(left_ref, rows, units_ref, columns):
    total = None
    for start in range(0, left_ref.shape[1], DEPTH):
        depth = slice(start, start + DEPTH)
        piece = jnp.dot(
            left_ref[rows, depth], units_ref[depth, columns], preferred_element_type=jnp.float32
        )
        total = piece if total is None else total + piece
    return total


def score(left_ref, rows, units_ref, start, marks, best_ref):
    scores = products(left_ref, rows, units_ref, pl.ds(start, COLS))
    best = best_ref[rows, :]
    for part in range(COLS // LANES):
        best = jnp.maximum(
            best, jnp.where(marks[part], scores[:, part * LANES : (part + 1) * LANES], LOW)
        )
    best_ref[rows, :] = best


def own_score(left_ref, chunk, units_ref, block, mark_ref, best_ref, mirror_ref):
    start = chunk * COLS
    scores = products(left_ref, slice(start, start + COLS), units_ref, slice(0, COLS))
    row_ids = lax.broadcasted_iota(jnp.int32, (COLS, LANES), 0)
    lane_ids = lax.broadcasted_iota(jnp.int32, (COLS, LANES), 1)
    best = best_ref[start : start + COLS, :]
    for part in range(COLS // LANES):
        tile = block * (COLS // LANES) + part
        piece = scores[:, part * LANES : (part + 1) * LANES]
        keep = mark_ref[tile][0:1, :] > 0
        if chunk == block:
            keep = keep & (row_ids != lane_ids + part * LANES)
        best = jnp.maximum(best, jnp.where(keep, piece, LOW))
        if chunk == 0:
            mirror = jnp.full((8, LANES), LOW, jnp.float32)
        else:
            mirror = mirror_ref[tile]
        if chunk < block:
            for other in range(COLS // LANES):
                row_marks = mark_ref[chunk * (COLS // LANES) + other][0:1, :]
                row_filled = jnp.transpose(jnp.broadcast_to(row_marks, (LANES, LANES))) > 0
                across = jnp.where(
                    row_filled, piece[other * LANES : (other + 1) * LANES], LOW
                )
                mirror = jnp.maximum(mirror, jnp.max(across, axis=0, keepdims=True))
        mirror_ref[tile] = mirror
    best_ref[start : start + COLS, :] = best


def marks_of(mark_ref, group):
    return [mark_ref[2 * group + part][0:1, :] > 0 for part in range(COLS // LANES)]


def block_kernel(block, place, codes_ref, table_refs, units_refs, state):
    left_ref, mark_ref, best_ref, mirror_ref, code_ref, scale_ref = state
    words_ref, centre_ref, norms_ref = table_refs
    units_ref = units_refs[block]
    owners = units_ref.shape[1] // COLS
    groups = left_ref.shape[0] // COLS
    unpack_block(
        place, block, 0, codes_ref, norms_ref, code_ref, scale_ref, mark_ref, owners, groups
    )

    def column_of(turn, offset=0):
        column = turn * COLS + offset
        return column if isinstance(turn, int) else pl.multiple_of(column, LANES)

    def decoding(turn):
        steps = []
        for half in range(2):
            steps += decode_steps(
                code_ref, scale_ref, 2 * turn + half, words_ref, centre_ref, units_ref,
                column_of(turn, half * LANES),
            )
        return steps

    def scoring(which, turn, chunks):
        return [
            functools.partial(
                score, left_ref, slice(chunk * COLS, (chunk + 1) * COLS), units_refs[which],
                column_of(turn), marks_of(mark_ref, turn * groups + which), best_ref,
            )
            for chunk in chunks
        ]

    if block == 0:
        best_ref[...] = jnp.full(best_ref.shape, LOW, jnp.float32)
        run(decoding(0))
    else:
        mix(scoring(block - 1, owners - 1, range(block)), decoding(0))
    turn_own(units_ref, left_ref, block)

    steps = [
        functools.partial(
            own_score, left_ref, chunk, units_ref, block, mark_ref, best_ref, mirror_ref
        )
        for chunk in range(block + 1)
    ]
    for which in range(block):
        steps += scoring(which, 1, [block])
    mix(steps, decoding(1))

    def both(turn, _):
        steps = scoring(block, turn - 1, range(block + 1))
        for which in range(block):
            steps += scoring(which, turn, [block])
        mix(steps, decoding(turn))
        return 0

    lax.fori_loop(2, owners, both, 0)


def next_kernel(block, place_ref, codes_ref, *refs):
    table_refs, refs = refs[:3], refs[3:]
    units_refs, refs = refs[:block], refs[block:]
    units_ref, left_ref, mark_ref, best_ref, mirror_ref, code_ref, scale_ref = refs[-7:]
    block_kernel(
        block, place_ref[0, 0], codes_ref, table_refs, [*units_refs, units_ref],
        (left_ref, mark_ref, best_ref, mirror_ref, code_ref, scale_ref),
    )


def last_kernel(sizes, place_ref, codes_ref, *refs):
    capacity, clusters, members = sizes
    place = place_ref[0, 0]
    table_refs, refs = refs[:3], refs[3:]
    units_refs, refs = refs[:-12], refs[-8:]
    out_ref, left_ref, mark_ref, best_ref, mirror_ref, units_ref, code_ref, scale_ref = refs
    slots = left_ref.shape[0]
    groups = slots // COLS
    owners = units_ref.shape[1] // COLS
    block_kernel(
        groups - 1, place, codes_ref, table_refs, [*units_refs, units_ref],
        (left_ref, mark_ref, best_ref, mirror_ref, code_ref, scale_ref),
    )

    final = (owners - 1) * groups + groups - 1
    score(
        left_ref, slice(0, slots), units_ref, (owners - 1) * COLS, marks_of(mark_ref, final),
        best_ref,
    )

    half_rows = capacity // 2
    tiles = slots // LANES
    lane = lax.broadcasted_iota(jnp.int32, (tiles, LANES), 1)
    slot = lax.broadcasted_iota(jnp.int32, (tiles, LANES), 0) * LANES + lane
    source, within = slot // capacity, slot % capacity
    turn = place ^ (source % members)
    own_row = (turn * clusters + source // members) * half_rows + within % half_rows
    tile_of = 2 * (own_row // LANES) + within // half_rows
    result = jnp.zeros((tiles, LANES), jnp.float32)
    for tile in range(tiles):
        best = jnp.max(
            jnp.transpose(best_ref[tile * LANES : (tile + 1) * LANES, :]), axis=0, keepdims=True
        )
        best = jnp.maximum(best, mirror_ref[tile][0:1, :])
        mark = mark_ref[tile]
        best = jnp.where(mark[0:1, :] > 0, best, 0.0)
        result = jnp.where(
            tile_of == tile,
            take_lanes(jnp.broadcast_to(best, (tiles, LANES)), own_row % LANES),
            result,
        )
    out_ref[...] = result


def on_device(codes, routes, codebook, centroids):
    clusters = lax.axis_size("cluster")
    members = lax.axis_size("blk")
    devices = clusters * members
    subspaces, in_rows = codes.shape[2:]
    capacity = 2 * in_rows // devices
    half_rows = capacity // 2
    slots = devices * capacity
    tiles = slots // LANES
    groups = slots // COLS
    words, width = codebook.shape
    bf16, f32, i32 = jnp.bfloat16, jnp.float32, jnp.int32
    smem = pl.BlockSpec(memory_space=pltpu.SMEM)
    vmem = pl.BlockSpec(memory_space=pltpu.VMEM)

    packed = pl.pallas_call(
        functools.partial(pack_kernel, devices, capacity),
        out_shape=jax.ShapeDtypeStruct((in_rows, 2 * subspaces), bf16),
        compiler_params=PARAMS,
        name="pack_rows",
    )(jnp.concatenate([codes[0, 0], routes.reshape(1, in_rows)], axis=0))
    here = lax.all_to_all(packed, "cluster", split_axis=0, concat_axis=0, tiled=True)
    def from_member(block, mask):
        return lax.ppermute(block, "blk", [(i, i ^ mask) for i in range(members)])

    masks = range(1, members)
    blocks = {0: here}
    for mask in masks:
        if mask & (mask - 1) == 0:
            blocks[mask] = from_member(here, mask)

    place = lax.axis_index("blk").astype(i32).reshape(1, 1)
    group = lax.axis_index("cluster").astype(i32).reshape(1, 1)
    table = pl.pallas_call(
        table_kernel,
        out_shape=(
            jax.ShapeDtypeStruct((width, words), bf16),
            jax.ShapeDtypeStruct((width, LANES), f32),
            jax.ShapeDtypeStruct((subspaces, words), f32),
        ),
        in_specs=[smem, vmem],
        compiler_params=PARAMS,
        cost_estimate=pl.CostEstimate(
            flops=4 * words * width, bytes_accessed=6 * words * width, transcendentals=0
        ),
        name="word_table",
    )(group, jnp.concatenate([codebook, centroids], axis=0))

    units_shape = jax.ShapeDtypeStruct((width, members * COLS), bf16)
    state_shape = (
        jax.ShapeDtypeStruct((slots, width), bf16),
        jax.ShapeDtypeStruct((2 * members * groups, 8, LANES), f32),
        jax.ShapeDtypeStruct((slots, LANES), f32),
        jax.ShapeDtypeStruct((tiles, 8, LANES), f32),
    )

    def code_scratch(count):
        return [
            pltpu.VMEM((2 * members * count, subspaces, LANES), i32),
            pltpu.VMEM((2 * members * count, 8, LANES), f32),
        ]

    def cost(flops):
        return pl.CostEstimate(
            flops=flops, bytes_accessed=16 * slots * width, transcendentals=0
        )

    scores_flops = 2 * slots * members * slots * width
    def take_in(block, codes_in, units, state):
        kept = len(state)
        outs = pl.pallas_call(
            functools.partial(next_kernel, block),
            out_shape=(units_shape, *state_shape),
            in_specs=[smem] + [vmem] * (4 + block + kept),
            out_specs=(vmem,) * 5,
            scratch_shapes=code_scratch(1),
            input_output_aliases={5 + block + which: 1 + which for which in range(kept)},
            compiler_params=PARAMS,
            cost_estimate=cost(scores_flops // 4),
            name=f"rows_{block}",
        )(place, codes_in, *table, *units, *state)
        return [*units, outs[0]], outs[1:]

    whole_groups = half_rows == 16 and clusters * half_rows == LANES
    if whole_groups:
        units, state = take_in(0, here, [], ())
        units, state = take_in(1, blocks[1], units, state)
    for mask in masks:
        if mask not in blocks:
            low = mask & -mask
            block = blocks[mask - low]
            if whole_groups:
                left, marks, best, mirror = state
                block, marks = lax.optimization_barrier((block, marks))
                state = (left, marks, best, mirror)
            blocks[mask] = from_member(block, low)
    blocks = [here] + [blocks[mask] for mask in masks]
    if not whole_groups:
        every = jnp.stack(blocks).reshape(members, clusters, members, half_rows, LANES)
        every = every.transpose(2, 0, 1, 3, 4).reshape(members, groups, LANES // 16, 16, LANES)
        every = every.transpose(1, 2, 0, 3, 4).reshape(groups, members * LANES, LANES)
        blocks = list(every)
        units, state = take_in(0, blocks[0], [], ())
        units, state = take_in(1, blocks[1], units, state)
    for block in range(2, groups - 1):
        units, state = take_in(block, blocks[block], units, state)
    nearest, *_ = pl.pallas_call(
        functools.partial(last_kernel, (capacity, clusters, members)),
        out_shape=(jax.ShapeDtypeStruct((tiles, LANES), f32), *state_shape),
        in_specs=[smem] + [vmem] * (groups + 7),
        out_specs=(vmem,) * 5,
        scratch_shapes=[pltpu.VMEM((width, members * COLS), bf16)] + code_scratch(1),
        input_output_aliases={groups + 4 + which: 1 + which for which in range(4)},
        compiler_params=PARAMS,
        cost_estimate=cost(scores_flops),
        name="last_rows",
    )(place, blocks[groups - 1], *table, *units, *state)
    return nearest.reshape(1, 1, slots)


def solution(mesh):
    in_specs = (P("cluster", "blk", None, None), P("cluster", "blk", None, None), P(), P())
    out_specs = P("cluster", "blk", None)
    return jax.shard_map(
        on_device, mesh=mesh, in_specs=in_specs, out_specs=out_specs, check_vma=False
    )
```

```python
import functools

import jax
import jax.numpy as jnp
from jax import lax
from jax.experimental import pallas as pl
from jax.experimental.pallas import tpu as pltpu
from jax.sharding import PartitionSpec as P

LANES = 128
COLS = 256
ROWS = 16
HELD = 3
CHUNK = 128
LOW = -4.0
VMEM_LIMIT = 40 * 1024 * 1024
PARAMS = pltpu.CompilerParams(vmem_limit_bytes=VMEM_LIMIT)
PACK_PARAMS = pltpu.CompilerParams(vmem_limit_bytes=60 * 1024 * 1024)


LANE_LOOKUP = lax.GatherDimensionNumbers(
    offset_dims=(),
    collapsed_slice_dims=(1,),
    start_index_map=(1,),
    operand_batching_dims=(0,),
    start_indices_batching_dims=(0,),
)


def take_lanes(table, index):
    return lax.gather(
        table, index[:, :, None], LANE_LOOKUP, (1, 1),
        mode=lax.GatherScatterMode.PROMISE_IN_BOUNDS,
    )


def pack_kernel(
    devices, capacity, codes_any, routes_any, out_any, codes_ref, routes_ref, out_ref, semaphores
):
    routes_in = pltpu.make_async_copy(routes_any, routes_ref, semaphores.at[0])
    codes_in = pltpu.make_async_copy(codes_any, codes_ref, semaphores.at[1])
    routes_in.start()
    codes_in.start()
    in_rows = codes_ref.shape[1]
    half_rows = capacity // 2
    earlier = (
        lax.broadcasted_iota(jnp.int32, (in_rows, in_rows), 0)
        < lax.broadcasted_iota(jnp.int32, (in_rows, in_rows), 1)
    )
    earlier = jnp.where(earlier, 1.0, 0.0).astype(jnp.bfloat16)
    routes_in.wait()
    targets = routes_ref[...]
    hot = lax.broadcasted_iota(jnp.int32, (devices, in_rows), 0) == targets
    hot32 = jnp.where(hot, 1.0, 0.0)
    running = jnp.dot(
        hot32.astype(jnp.bfloat16), earlier, preferred_element_type=jnp.float32
    )
    position = jnp.sum(hot32 * running, axis=0, keepdims=True).astype(jnp.int32)
    second = position >= half_rows
    key = targets * half_rows + jnp.where(second, position - half_rows, position)
    codes_in.wait()
    values = (codes_ref[...] + 1).astype(jnp.bfloat16)
    out_rows = out_ref.shape[0] // 2
    copies = []
    for part in range(2):
        rows = slice(part * out_rows, (part + 1) * out_rows)
        row_ids = lax.broadcasted_iota(jnp.int32, (out_rows, in_rows), 0) + part * out_rows
        halves = []
        for wanted in (jnp.where(second, -1, key), jnp.where(second, key, -1)):
            move = jnp.where(row_ids == wanted, 1.0, 0.0).astype(jnp.bfloat16)
            halves.append(
                lax.dot_general(
                    move, values, (((1,), (1,)), ((), ())), preferred_element_type=jnp.float32
                )
            )
        out_ref[rows, :] = jnp.concatenate(halves, axis=1).astype(jnp.bfloat16)
        copies.append(
            pltpu.make_async_copy(out_ref.at[rows], out_any.at[rows], semaphores.at[2 + part])
        )
        copies[part].start()
    for copy in copies:
        copy.wait()


def table_kernel(group_ref, book_ref, words_ref, centre_ref, norms_ref):
    width, words = words_ref.shape
    subspaces = norms_ref.shape[0]
    sub_width = width // subspaces
    block = ROWS * sub_width
    new = lax.broadcasted_iota(jnp.int32, (block, block), 0)
    old = lax.broadcasted_iota(jnp.int32, (block, block), 1)
    order = jnp.where(old == (new % ROWS) * sub_width + new // ROWS, 1.0, 0.0).astype(jnp.bfloat16)
    clusters = book_ref.shape[0] - words
    pick = lax.broadcasted_iota(jnp.int32, (1, clusters), 1) == group_ref[0, 0]
    for part in range(width // block):
        rows = slice(part * block, (part + 1) * block)
        turned = lax.dot_general(
            order, book_ref[:, rows], (((1,), (1,)), ((), ())), preferred_element_type=jnp.float32
        )
        centre = jnp.sum(jnp.where(pick, turned[:, words:], 0.0), axis=1, keepdims=True)
        words_ref[rows, :] = turned[:, :words].astype(jnp.bfloat16)
        centre_ref[rows, :] = jnp.broadcast_to(centre, (block, LANES))
        table = turned[:, :words] + centre
        norms_ref[part * ROWS : (part + 1) * ROWS, :] = jnp.sum(
            (table * table).reshape(sub_width, ROWS, words), axis=0
        )


def owner_block(codes_ref, owner, owners):
    parts = [
        codes_ref[pl.ds(pl.multiple_of((part * owners + owner) * 16, 16), 16), :]
        for part in range(LANES // 16)
    ]
    return jnp.concatenate(parts, axis=0)


def unpack_codes(block, norms_ref, code_ref, scale_ref, mark_ref, group, place):
    turned = jnp.transpose(block.astype(jnp.float32)).astype(jnp.int32)
    subspaces = turned.shape[0] // 2
    for half in range(2):
        part = turned[half * subspaces : (half + 1) * subspaces]
        code = jnp.maximum(part - 1, 0)
        code_ref[2 * group + half] = code
        mark_ref[2 * place + half] = jnp.where(part[0:8] > 0, 1.0, 0.0)
        low = code & (LANES - 1)
        squares = jnp.where(
            code >= LANES,
            take_lanes(norms_ref[:, LANES:], low),
            take_lanes(norms_ref[:, :LANES], low),
        )
        scale = lax.rsqrt(jnp.sum(squares, axis=0, keepdims=True) + 1e-06)
        scale_ref[2 * group + half] = jnp.broadcast_to(scale, (8, LANES))


def unpack_block(
    place, first, which, codes_ref, norms_ref, code_ref, scale_ref, mark_ref, owners, groups
):
    for turn in range(owners):
        owner = lax.rem(place + turn, owners)
        unpack_codes(
            owner_block(codes_ref, owner, owners), norms_ref, code_ref, scale_ref, mark_ref,
            which * owners + turn, turn * groups + first + which,
        )


def decode_steps(code_ref, scale_ref, tile, words_ref, centre_ref, units_ref, start):
    subspaces = code_ref.shape[1]
    sub_width = words_ref.shape[0] // subspaces

    def step(part):
        code = code_ref[tile, part * ROWS : (part + 1) * ROWS, :].astype(jnp.int16)
        scale = jnp.concatenate([scale_ref[tile]] * (ROWS // 8), axis=0)
        low = code & (LANES - 1)
        high = code > LANES - 1
        values = []
        for entry in range(sub_width):
            row = (part * sub_width + entry) * ROWS
            rows = slice(row, row + ROWS)
            word = jnp.where(
                high,
                take_lanes(words_ref[rows, LANES:], low),
                take_lanes(words_ref[rows, :LANES], low),
            )
            unit = (word.astype(jnp.float32) + centre_ref[rows, :]) * scale
            values.append((rows, unit.astype(jnp.bfloat16)))
        return values

    def put(values):
        for rows, value in values:
            units_ref[rows, pl.ds(start, LANES)] = value

    return [(functools.partial(step, part), put) for part in range(subspaces // ROWS)]


def run(decoding):
    for step, put in decoding:
        put(step())


def mix(scoring, decoding):
    done = 0
    for place, score_chunk in enumerate(scoring):
        upto = (place + 1) * len(decoding) // len(scoring)
        beside = decoding[done : min(upto, done + HELD)]
        held = [(step(), put) for step, put in beside]
        score_chunk()
        for values, put in held:
            put(values)
        run(decoding[done + len(beside) : upto])
        done = upto


def turn_own(units_ref, left_ref, block):
    for half in range(2):
        start = block * COLS + half * LANES
        left_ref[start : start + LANES, :] = jnp.transpose(
            units_ref[:, half * LANES : (half + 1) * LANES]
        )


def score(left_ref, rows, units_ref, start, marks, best_ref):
    scores = jnp.dot(
        left_ref[rows, :], units_ref[:, pl.ds(start, COLS)], preferred_element_type=jnp.float32
    )
    best = best_ref[rows, :]
    for part in range(COLS // LANES):
        best = jnp.maximum(
            best, jnp.where(marks[part], scores[:, part * LANES : (part + 1) * LANES], LOW)
        )
    best_ref[rows, :] = best


def own_score(left_ref, chunk, units_ref, block, mark_ref, best_ref, mirror_ref):
    start = chunk * COLS
    scores = jnp.dot(
        left_ref[start : start + COLS, :], units_ref[:, :COLS],
        preferred_element_type=jnp.float32,
    )
    row_ids = lax.broadcasted_iota(jnp.int32, (COLS, LANES), 0)
    lane_ids = lax.broadcasted_iota(jnp.int32, (COLS, LANES), 1)
    best = best_ref[start : start + COLS, :]
    for part in range(COLS // LANES):
        tile = block * (COLS // LANES) + part
        piece = scores[:, part * LANES : (part + 1) * LANES]
        keep = mark_ref[tile][0:1, :] > 0
        if chunk == block:
            keep = keep & (row_ids != lane_ids + part * LANES)
        best = jnp.maximum(best, jnp.where(keep, piece, LOW))
        if chunk == 0:
            mirror = jnp.full((8, LANES), LOW, jnp.float32)
        else:
            mirror = mirror_ref[tile]
        if chunk < block:
            for other in range(COLS // LANES):
                row_marks = mark_ref[chunk * (COLS // LANES) + other][0:1, :]
                row_filled = jnp.transpose(jnp.broadcast_to(row_marks, (LANES, LANES))) > 0
                across = jnp.where(
                    row_filled, piece[other * LANES : (other + 1) * LANES], LOW
                )
                mirror = jnp.maximum(mirror, jnp.max(across, axis=0, keepdims=True))
        mirror_ref[tile] = mirror
    best_ref[start : start + COLS, :] = best


def marks_of(mark_ref, group):
    return [mark_ref[2 * group + part][0:1, :] > 0 for part in range(COLS // LANES)]


def block_kernel(block, place, codes_ref, table_refs, units_refs, state):
    left_ref, mark_ref, best_ref, mirror_ref, code_ref, scale_ref = state
    words_ref, centre_ref, norms_ref = table_refs
    units_ref = units_refs[block]
    owners = units_ref.shape[1] // COLS
    groups = left_ref.shape[0] // COLS
    unpack_block(
        place, block, 0, codes_ref, norms_ref, code_ref, scale_ref, mark_ref, owners, groups
    )

    def column_of(turn, offset=0):
        column = turn * COLS + offset
        return column if isinstance(turn, int) else pl.multiple_of(column, LANES)

    def decoding(turn):
        steps = []
        for half in range(2):
            steps += decode_steps(
                code_ref, scale_ref, 2 * turn + half, words_ref, centre_ref, units_ref,
                column_of(turn, half * LANES),
            )
        return steps

    def scoring(which, turn, chunks):
        return [
            functools.partial(
                score, left_ref, slice(start, start + CHUNK), units_refs[which],
                column_of(turn), marks_of(mark_ref, turn * groups + which), best_ref,
            )
            for chunk in chunks
            for start in range(chunk * COLS, (chunk + 1) * COLS, CHUNK)
        ]

    if block == 0:
        best_ref[...] = jnp.full(best_ref.shape, LOW, jnp.float32)
        run(decoding(0))
    else:
        mix(scoring(block - 1, owners - 1, range(block)), decoding(0))
    turn_own(units_ref, left_ref, block)

    steps = [
        functools.partial(
            own_score, left_ref, chunk, units_ref, block, mark_ref, best_ref, mirror_ref
        )
        for chunk in range(block + 1)
    ]
    for which in range(block):
        steps += scoring(which, 1, [block])
    mix(steps, decoding(1))

    def both(turn, _):
        steps = scoring(block, turn - 1, range(block + 1))
        for which in range(block):
            steps += scoring(which, turn, [block])
        mix(steps, decoding(turn))
        return 0

    lax.fori_loop(2, owners, both, 0)


def next_kernel(block, place_ref, codes_ref, *refs):
    table_refs, refs = refs[:3], refs[3:]
    units_refs, refs = refs[:block], refs[block:]
    units_ref, left_ref, mark_ref, best_ref, mirror_ref, code_ref, scale_ref = refs[-7:]
    block_kernel(
        block, place_ref[0, 0], codes_ref, table_refs, [*units_refs, units_ref],
        (left_ref, mark_ref, best_ref, mirror_ref, code_ref, scale_ref),
    )


def last_kernel(sizes, place_ref, codes_ref, *refs):
    capacity, clusters, members = sizes
    place = place_ref[0, 0]
    table_refs, refs = refs[:3], refs[3:]
    units_refs, refs = refs[:-12], refs[-8:]
    out_ref, left_ref, mark_ref, best_ref, mirror_ref, units_ref, code_ref, scale_ref = refs
    slots = left_ref.shape[0]
    groups = slots // COLS
    owners = units_ref.shape[1] // COLS
    block_kernel(
        groups - 1, place, codes_ref, table_refs, [*units_refs, units_ref],
        (left_ref, mark_ref, best_ref, mirror_ref, code_ref, scale_ref),
    )

    final = (owners - 1) * groups + groups - 1
    score(
        left_ref, slice(0, slots), units_ref, (owners - 1) * COLS, marks_of(mark_ref, final),
        best_ref,
    )

    half_rows = capacity // 2
    tiles = slots // LANES
    lane = lax.broadcasted_iota(jnp.int32, (tiles, LANES), 1)
    slot = lax.broadcasted_iota(jnp.int32, (tiles, LANES), 0) * LANES + lane
    source, within = slot // capacity, slot % capacity
    turn = place ^ (source % members)
    own_row = (turn * clusters + source // members) * half_rows + within % half_rows
    tile_of = 2 * (own_row // LANES) + within // half_rows
    result = jnp.zeros((tiles, LANES), jnp.float32)
    for tile in range(tiles):
        best = jnp.max(
            jnp.transpose(best_ref[tile * LANES : (tile + 1) * LANES, :]), axis=0, keepdims=True
        )
        best = jnp.maximum(best, mirror_ref[tile][0:1, :])
        mark = mark_ref[tile]
        best = jnp.where(mark[0:1, :] > 0, best, 0.0)
        result = jnp.where(
            tile_of == tile,
            take_lanes(jnp.broadcast_to(best, (tiles, LANES)), own_row % LANES),
            result,
        )
    out_ref[...] = result


def on_device(codes, routes, codebook, centroids):
    clusters = lax.axis_size("cluster")
    members = lax.axis_size("blk")
    devices = clusters * members
    subspaces, in_rows = codes.shape[2:]
    capacity = 2 * in_rows // devices
    half_rows = capacity // 2
    slots = devices * capacity
    tiles = slots // LANES
    groups = slots // COLS
    words, width = codebook.shape
    bf16, f32, i32 = jnp.bfloat16, jnp.float32, jnp.int32
    smem = pl.BlockSpec(memory_space=pltpu.SMEM)
    vmem = pl.BlockSpec(memory_space=pltpu.VMEM)

    anywhere = pl.BlockSpec(memory_space=pl.ANY)
    packed = pl.pallas_call(
        functools.partial(pack_kernel, devices, capacity),
        out_shape=jax.ShapeDtypeStruct((in_rows, 2 * subspaces), bf16),
        in_specs=[anywhere] * 2,
        out_specs=anywhere,
        scratch_shapes=[
            pltpu.VMEM((subspaces, in_rows), i32),
            pltpu.VMEM((1, in_rows), i32),
            pltpu.VMEM((in_rows, 2 * subspaces), bf16),
            pltpu.SemaphoreType.DMA((4,)),
        ],
        compiler_params=PACK_PARAMS,
        name="pack_rows",
    )(codes[0, 0], routes.reshape(1, in_rows))
    here = lax.all_to_all(packed, "cluster", split_axis=0, concat_axis=0, tiled=True)
    def from_member(block, mask):
        return lax.ppermute(block, "blk", [(i, i ^ mask) for i in range(members)])

    masks = range(1, members)
    blocks = {0: here}
    for mask in masks:
        if mask & (mask - 1) == 0:
            blocks[mask] = from_member(here, mask)

    place = lax.axis_index("blk").astype(i32).reshape(1, 1)
    group = lax.axis_index("cluster").astype(i32).reshape(1, 1)
    table = pl.pallas_call(
        table_kernel,
        out_shape=(
            jax.ShapeDtypeStruct((width, words), bf16),
            jax.ShapeDtypeStruct((width, LANES), f32),
            jax.ShapeDtypeStruct((subspaces, words), f32),
        ),
        in_specs=[smem, vmem],
        compiler_params=PARAMS,
        cost_estimate=pl.CostEstimate(
            flops=4 * words * width, bytes_accessed=6 * words * width, transcendentals=0
        ),
        name="word_table",
    )(group, jnp.concatenate([codebook, centroids], axis=0))

    units_shape = jax.ShapeDtypeStruct((width, members * COLS), bf16)
    state_shape = (
        jax.ShapeDtypeStruct((slots, width), bf16),
        jax.ShapeDtypeStruct((2 * members * groups, 8, LANES), f32),
        jax.ShapeDtypeStruct((slots, LANES), f32),
        jax.ShapeDtypeStruct((tiles, 8, LANES), f32),
    )

    def code_scratch(count):
        return [
            pltpu.VMEM((2 * members * count, subspaces, LANES), i32),
            pltpu.VMEM((2 * members * count, 8, LANES), f32),
        ]

    def cost(flops):
        return pl.CostEstimate(
            flops=flops, bytes_accessed=16 * slots * width, transcendentals=0
        )

    scores_flops = 2 * slots * members * slots * width
    def take_in(block, codes_in, units, state):
        kept = len(state)
        outs = pl.pallas_call(
            functools.partial(next_kernel, block),
            out_shape=(units_shape, *state_shape),
            in_specs=[smem] + [vmem] * (4 + block + kept),
            out_specs=(vmem,) * 5,
            scratch_shapes=code_scratch(1),
            input_output_aliases={5 + block + which: 1 + which for which in range(kept)},
            compiler_params=PARAMS,
            cost_estimate=cost(scores_flops // 4),
            name=f"rows_{block}",
        )(place, codes_in, *table, *units, *state)
        return [*units, outs[0]], outs[1:]

    whole_groups = half_rows == 16 and clusters * half_rows == LANES
    if whole_groups:
        units, state = take_in(0, here, [], ())
        units, state = take_in(1, blocks[1], units, state)
    for mask in masks:
        if mask not in blocks:
            low = mask & -mask
            block = blocks[mask - low]
            if whole_groups:
                left, marks, best, mirror = state
                block, marks = lax.optimization_barrier((block, marks))
                state = (left, marks, best, mirror)
            blocks[mask] = from_member(block, low)
    blocks = [here] + [blocks[mask] for mask in masks]
    if not whole_groups:
        every = jnp.stack(blocks).reshape(members, clusters, members, half_rows, LANES)
        every = every.transpose(2, 0, 1, 3, 4).reshape(members, groups, LANES // 16, 16, LANES)
        every = every.transpose(1, 2, 0, 3, 4).reshape(groups, members * LANES, LANES)
        blocks = list(every)
        units, state = take_in(0, blocks[0], [], ())
        units, state = take_in(1, blocks[1], units, state)
    for block in range(2, groups - 1):
        units, state = take_in(block, blocks[block], units, state)
    nearest, *_ = pl.pallas_call(
        functools.partial(last_kernel, (capacity, clusters, members)),
        out_shape=(jax.ShapeDtypeStruct((tiles, LANES), f32), *state_shape),
        in_specs=[smem] + [vmem] * (groups + 7),
        out_specs=(vmem,) * 5,
        scratch_shapes=[pltpu.VMEM((width, members * COLS), bf16)] + code_scratch(1),
        input_output_aliases={groups + 4 + which: 1 + which for which in range(4)},
        compiler_params=PARAMS,
        cost_estimate=cost(scores_flops),
        name="last_rows",
    )(place, blocks[groups - 1], *table, *units, *state)
    return nearest.reshape(1, 1, slots)


def solution(mesh):
    in_specs = (P("cluster", "blk", None, None), P("cluster", "blk", None, None), P(), P())
    out_specs = P("cluster", "blk", None)
    return jax.shard_map(
        on_device, mesh=mesh, in_specs=in_specs, out_specs=out_specs, check_vma=False
    )
```

```python
import functools

import jax
import jax.numpy as jnp
from jax import lax
from jax.experimental import pallas as pl
from jax.experimental.pallas import tpu as pltpu
from jax.sharding import PartitionSpec as P

LANES = 128
COLS = 256
ROWS = 16
HELD = 6
LOW = -4.0
VMEM_LIMIT = 40 * 1024 * 1024
PARAMS = pltpu.CompilerParams(vmem_limit_bytes=VMEM_LIMIT)
PACK_PARAMS = pltpu.CompilerParams(vmem_limit_bytes=60 * 1024 * 1024)


LANE_LOOKUP = lax.GatherDimensionNumbers(
    offset_dims=(),
    collapsed_slice_dims=(1,),
    start_index_map=(1,),
    operand_batching_dims=(0,),
    start_indices_batching_dims=(0,),
)


def take_lanes(table, index):
    return lax.gather(
        table, index[:, :, None], LANE_LOOKUP, (1, 1),
        mode=lax.GatherScatterMode.PROMISE_IN_BOUNDS,
    )


def pack_kernel(
    devices, capacity, codes_any, routes_any, out_any, codes_ref, routes_ref, out_ref, semaphores
):
    routes_in = pltpu.make_async_copy(routes_any, routes_ref, semaphores.at[0])
    codes_in = pltpu.make_async_copy(codes_any, codes_ref, semaphores.at[1])
    routes_in.start()
    codes_in.start()
    in_rows = codes_ref.shape[1]
    half_rows = capacity // 2
    earlier = (
        lax.broadcasted_iota(jnp.int32, (in_rows, in_rows), 0)
        < lax.broadcasted_iota(jnp.int32, (in_rows, in_rows), 1)
    )
    earlier = jnp.where(earlier, 1.0, 0.0).astype(jnp.bfloat16)
    routes_in.wait()
    targets = routes_ref[...]
    hot = lax.broadcasted_iota(jnp.int32, (devices, in_rows), 0) == targets
    hot32 = jnp.where(hot, 1.0, 0.0)
    running = jnp.dot(
        hot32.astype(jnp.bfloat16), earlier, preferred_element_type=jnp.float32
    )
    position = jnp.sum(hot32 * running, axis=0, keepdims=True).astype(jnp.int32)
    second = position >= half_rows
    key = targets * half_rows + jnp.where(second, position - half_rows, position)
    codes_in.wait()
    values = (codes_ref[...] + 1).astype(jnp.bfloat16)
    out_rows = out_ref.shape[0] // 2
    copies = []
    for part in range(2):
        rows = slice(part * out_rows, (part + 1) * out_rows)
        row_ids = lax.broadcasted_iota(jnp.int32, (out_rows, in_rows), 0) + part * out_rows
        halves = []
        for wanted in (jnp.where(second, -1, key), jnp.where(second, key, -1)):
            move = jnp.where(row_ids == wanted, 1.0, 0.0).astype(jnp.bfloat16)
            halves.append(
                lax.dot_general(
                    move, values, (((1,), (1,)), ((), ())), preferred_element_type=jnp.float32
                )
            )
        out_ref[rows, :] = jnp.concatenate(halves, axis=1).astype(jnp.bfloat16)
        copies.append(
            pltpu.make_async_copy(out_ref.at[rows], out_any.at[rows], semaphores.at[2 + part])
        )
        copies[part].start()
    for copy in copies:
        copy.wait()


def table_kernel(group_ref, book_ref, words_ref, centre_ref, norms_ref):
    width, words = words_ref.shape
    subspaces = norms_ref.shape[0]
    sub_width = width // subspaces
    block = ROWS * sub_width
    new = lax.broadcasted_iota(jnp.int32, (block, block), 0)
    old = lax.broadcasted_iota(jnp.int32, (block, block), 1)
    order = jnp.where(old == (new % ROWS) * sub_width + new // ROWS, 1.0, 0.0).astype(jnp.bfloat16)
    clusters = book_ref.shape[0] - words
    pick = lax.broadcasted_iota(jnp.int32, (1, clusters), 1) == group_ref[0, 0]
    for part in range(width // block):
        rows = slice(part * block, (part + 1) * block)
        turned = lax.dot_general(
            order, book_ref[:, rows], (((1,), (1,)), ((), ())), preferred_element_type=jnp.float32
        )
        centre = jnp.sum(jnp.where(pick, turned[:, words:], 0.0), axis=1, keepdims=True)
        words_ref[rows, :] = turned[:, :words].astype(jnp.bfloat16)
        centre_ref[rows, :] = jnp.broadcast_to(centre, (block, LANES))
        table = turned[:, :words] + centre
        norms_ref[part * ROWS : (part + 1) * ROWS, :] = jnp.sum(
            (table * table).reshape(sub_width, ROWS, words), axis=0
        )


def owner_block(codes_ref, owner, owners):
    parts = [
        codes_ref[pl.ds(pl.multiple_of((part * owners + owner) * 16, 16), 16), :]
        for part in range(LANES // 16)
    ]
    return jnp.concatenate(parts, axis=0)


def unpack_codes(block, norms_ref, code_ref, scale_ref, mark_ref, group, place):
    turned = jnp.transpose(block.astype(jnp.float32)).astype(jnp.int32)
    subspaces = turned.shape[0] // 2
    for half in range(2):
        part = turned[half * subspaces : (half + 1) * subspaces]
        code = jnp.maximum(part - 1, 0)
        code_ref[2 * group + half] = code
        mark_ref[2 * place + half] = jnp.where(part[0:8] > 0, 1.0, 0.0)
        low = code & (LANES - 1)
        squares = jnp.where(
            code >= LANES,
            take_lanes(norms_ref[:, LANES:], low),
            take_lanes(norms_ref[:, :LANES], low),
        )
        scale = lax.rsqrt(jnp.sum(squares, axis=0, keepdims=True) + 1e-06)
        scale_ref[2 * group + half] = jnp.broadcast_to(scale, (8, LANES))


def unpack_block(
    place, first, which, codes_ref, norms_ref, code_ref, scale_ref, mark_ref, owners, groups
):
    for turn in range(owners):
        owner = lax.rem(place + turn, owners)
        unpack_codes(
            owner_block(codes_ref, owner, owners), norms_ref, code_ref, scale_ref, mark_ref,
            which * owners + turn, turn * groups + first + which,
        )


def decode_steps(code_ref, scale_ref, tile, words_ref, centre_ref, units_ref, start):
    subspaces = code_ref.shape[1]
    sub_width = words_ref.shape[0] // subspaces

    def step(part):
        code = code_ref[tile, part * ROWS : (part + 1) * ROWS, :].astype(jnp.int16)
        scale = jnp.concatenate([scale_ref[tile]] * (ROWS // 8), axis=0)
        low = code & (LANES - 1)
        high = code > LANES - 1
        values = []
        for entry in range(sub_width):
            row = (part * sub_width + entry) * ROWS
            rows = slice(row, row + ROWS)
            word = jnp.where(
                high,
                take_lanes(words_ref[rows, LANES:], low),
                take_lanes(words_ref[rows, :LANES], low),
            )
            unit = (word.astype(jnp.float32) + centre_ref[rows, :]) * scale
            values.append((rows, unit.astype(jnp.bfloat16)))
        return values

    def put(values):
        for rows, value in values:
            units_ref[rows, pl.ds(start, LANES)] = value

    return [(functools.partial(step, part), put) for part in range(subspaces // ROWS)]


def run(decoding):
    for step, put in decoding:
        put(step())


def mix(scoring, decoding):
    whole = sum(weight for weight, _ in scoring)
    done, behind = 0, 0
    for weight, score_rows in scoring:
        behind += weight
        upto = behind * len(decoding) // whole
        beside = decoding[done : min(upto, done + HELD)]
        held = [(step(), put) for step, put in beside]
        score_rows()
        for values, put in held:
            put(values)
        run(decoding[done + len(beside) : upto])
        done = upto


def turn_own(units_ref, left_ref, block):
    for half in range(2):
        start = block * COLS + half * LANES
        left_ref[start : start + LANES, :] = jnp.transpose(
            units_ref[:, half * LANES : (half + 1) * LANES]
        )


def score(left_ref, rows, units_ref, start, marks, best_ref):
    scores = jnp.dot(
        left_ref[rows, :], units_ref[:, pl.ds(start, COLS)], preferred_element_type=jnp.float32
    )
    best = best_ref[rows, :]
    for part in range(COLS // LANES):
        best = jnp.maximum(
            best, jnp.where(marks[part], scores[:, part * LANES : (part + 1) * LANES], LOW)
        )
    best_ref[rows, :] = best


def own_score(left_ref, units_ref, block, mark_ref, best_ref, mirror_ref):
    above, count = block * COLS, (block + 1) * COLS
    scores = jnp.dot(
        left_ref[:count, :], units_ref[:, :COLS], preferred_element_type=jnp.float32
    )
    row_ids = lax.broadcasted_iota(jnp.int32, (COLS, LANES), 0)
    lane_ids = lax.broadcasted_iota(jnp.int32, (COLS, LANES), 1)
    for part in range(COLS // LANES):
        tile = block * (COLS // LANES) + part
        lanes = slice(part * LANES, (part + 1) * LANES)
        filled = mark_ref[tile][0:1, :] > 0
        keep = filled & (row_ids != lane_ids + part * LANES)
        best_ref[above:count, :] = jnp.maximum(
            best_ref[above:count, :], jnp.where(keep, scores[above:count, lanes], LOW)
        )
        mirror = jnp.full((1, LANES), LOW, jnp.float32)
        for other in range(above // LANES):
            rows = slice(other * LANES, (other + 1) * LANES)
            piece = scores[rows, lanes]
            best_ref[rows, :] = jnp.maximum(best_ref[rows, :], jnp.where(filled, piece, LOW))
            row_filled = jnp.transpose(
                jnp.broadcast_to(mark_ref[other][0:1, :], (LANES, LANES))
            )
            mirror = jnp.maximum(
                mirror,
                jnp.max(jnp.where(row_filled > 0, piece, LOW), axis=0, keepdims=True),
            )
        mirror_ref[tile] = jnp.broadcast_to(mirror, (8, LANES))


def marks_of(mark_ref, group):
    return [mark_ref[2 * group + part][0:1, :] > 0 for part in range(COLS // LANES)]


def block_kernel(block, place, codes_ref, table_refs, units_refs, state):
    left_ref, mark_ref, best_ref, mirror_ref, code_ref, scale_ref = state
    words_ref, centre_ref, norms_ref = table_refs
    units_ref = units_refs[block]
    owners = units_ref.shape[1] // COLS
    groups = left_ref.shape[0] // COLS
    unpack_block(
        place, block, 0, codes_ref, norms_ref, code_ref, scale_ref, mark_ref, owners, groups
    )

    def column_of(turn, offset=0):
        column = turn * COLS + offset
        return column if isinstance(turn, int) else pl.multiple_of(column, LANES)

    def decoding(turn):
        steps = []
        for half in range(2):
            steps += decode_steps(
                code_ref, scale_ref, 2 * turn + half, words_ref, centre_ref, units_ref,
                column_of(turn, half * LANES),
            )
        return steps

    def scoring(which, turn, first, last):
        rows = slice(first * COLS, last * COLS)
        return last - first, functools.partial(
            score, left_ref, rows, units_refs[which], column_of(turn),
            marks_of(mark_ref, turn * groups + which), best_ref,
        )

    if block == 0:
        best_ref[...] = jnp.full(best_ref.shape, LOW, jnp.float32)
        run(decoding(0))
    else:
        mix([scoring(block - 1, owners - 1, 0, block)], decoding(0))
    turn_own(units_ref, left_ref, block)

    steps = [
        (
            block + 1,
            functools.partial(
                own_score, left_ref, units_ref, block, mark_ref, best_ref, mirror_ref
            ),
        )
    ]
    for which in range(block):
        steps.append(scoring(which, 1, block, block + 1))
    mix(steps, decoding(1))

    def both(turn, _):
        steps = [scoring(block, turn - 1, 0, block + 1)]
        for which in range(block):
            steps.append(scoring(which, turn, block, block + 1))
        mix(steps, decoding(turn))
        return 0

    lax.fori_loop(2, owners, both, 0)


def next_kernel(block, place_ref, codes_ref, *refs):
    table_refs, refs = refs[:3], refs[3:]
    units_refs, refs = refs[:block], refs[block:]
    units_ref, left_ref, mark_ref, best_ref, mirror_ref, code_ref, scale_ref = refs[-7:]
    block_kernel(
        block, place_ref[0, 0], codes_ref, table_refs, [*units_refs, units_ref],
        (left_ref, mark_ref, best_ref, mirror_ref, code_ref, scale_ref),
    )


def last_kernel(sizes, place_ref, codes_ref, *refs):
    capacity, clusters, members = sizes
    place = place_ref[0, 0]
    table_refs, refs = refs[:3], refs[3:]
    units_refs, refs = refs[:-12], refs[-8:]
    out_ref, left_ref, mark_ref, best_ref, mirror_ref, units_ref, code_ref, scale_ref = refs
    slots = left_ref.shape[0]
    groups = slots // COLS
    owners = units_ref.shape[1] // COLS
    block_kernel(
        groups - 1, place, codes_ref, table_refs, [*units_refs, units_ref],
        (left_ref, mark_ref, best_ref, mirror_ref, code_ref, scale_ref),
    )

    final = (owners - 1) * groups + groups - 1
    score(
        left_ref, slice(0, slots), units_ref, (owners - 1) * COLS, marks_of(mark_ref, final),
        best_ref,
    )

    half_rows = capacity // 2
    tiles = slots // LANES
    lane = lax.broadcasted_iota(jnp.int32, (tiles, LANES), 1)
    slot = lax.broadcasted_iota(jnp.int32, (tiles, LANES), 0) * LANES + lane
    source, within = slot // capacity, slot % capacity
    turn = place ^ (source % members)
    own_row = (turn * clusters + source // members) * half_rows + within % half_rows
    tile_of = 2 * (own_row // LANES) + within // half_rows
    result = jnp.zeros((tiles, LANES), jnp.float32)
    for tile in range(tiles):
        best = jnp.max(
            jnp.transpose(best_ref[tile * LANES : (tile + 1) * LANES, :]), axis=0, keepdims=True
        )
        best = jnp.maximum(best, mirror_ref[tile][0:1, :])
        mark = mark_ref[tile]
        best = jnp.where(mark[0:1, :] > 0, best, 0.0)
        result = jnp.where(
            tile_of == tile,
            take_lanes(jnp.broadcast_to(best, (tiles, LANES)), own_row % LANES),
            result,
        )
    out_ref[...] = result


def on_device(codes, routes, codebook, centroids):
    clusters = lax.axis_size("cluster")
    members = lax.axis_size("blk")
    devices = clusters * members
    subspaces, in_rows = codes.shape[2:]
    capacity = 2 * in_rows // devices
    half_rows = capacity // 2
    slots = devices * capacity
    tiles = slots // LANES
    groups = slots // COLS
    words, width = codebook.shape
    bf16, f32, i32 = jnp.bfloat16, jnp.float32, jnp.int32
    smem = pl.BlockSpec(memory_space=pltpu.SMEM)
    vmem = pl.BlockSpec(memory_space=pltpu.VMEM)

    anywhere = pl.BlockSpec(memory_space=pl.ANY)
    packed = pl.pallas_call(
        functools.partial(pack_kernel, devices, capacity),
        out_shape=jax.ShapeDtypeStruct((in_rows, 2 * subspaces), bf16),
        in_specs=[anywhere] * 2,
        out_specs=anywhere,
        scratch_shapes=[
            pltpu.VMEM((subspaces, in_rows), i32),
            pltpu.VMEM((1, in_rows), i32),
            pltpu.VMEM((in_rows, 2 * subspaces), bf16),
            pltpu.SemaphoreType.DMA((4,)),
        ],
        compiler_params=PACK_PARAMS,
        name="pack_rows",
    )(codes[0, 0], routes.reshape(1, in_rows))
    here = lax.all_to_all(packed, "cluster", split_axis=0, concat_axis=0, tiled=True)
    def from_member(block, mask):
        return lax.ppermute(block, "blk", [(i, i ^ mask) for i in range(members)])

    masks = range(1, members)
    blocks = {0: here}
    for mask in masks:
        if mask & (mask - 1) == 0:
            blocks[mask] = from_member(here, mask)

    place = lax.axis_index("blk").astype(i32).reshape(1, 1)
    group = lax.axis_index("cluster").astype(i32).reshape(1, 1)
    table = pl.pallas_call(
        table_kernel,
        out_shape=(
            jax.ShapeDtypeStruct((width, words), bf16),
            jax.ShapeDtypeStruct((width, LANES), f32),
            jax.ShapeDtypeStruct((subspaces, words), f32),
        ),
        in_specs=[smem, vmem],
        compiler_params=PARAMS,
        cost_estimate=pl.CostEstimate(
            flops=4 * words * width, bytes_accessed=6 * words * width, transcendentals=0
        ),
        name="word_table",
    )(group, jnp.concatenate([codebook, centroids], axis=0))

    units_shape = jax.ShapeDtypeStruct((width, members * COLS), bf16)
    state_shape = (
        jax.ShapeDtypeStruct((slots, width), bf16),
        jax.ShapeDtypeStruct((2 * members * groups, 8, LANES), f32),
        jax.ShapeDtypeStruct((slots, LANES), f32),
        jax.ShapeDtypeStruct((tiles, 8, LANES), f32),
    )

    def code_scratch(count):
        return [
            pltpu.VMEM((2 * members * count, subspaces, LANES), i32),
            pltpu.VMEM((2 * members * count, 8, LANES), f32),
        ]

    def cost(flops):
        return pl.CostEstimate(
            flops=flops, bytes_accessed=16 * slots * width, transcendentals=0
        )

    scores_flops = 2 * slots * members * slots * width
    def take_in(block, codes_in, units, state):
        kept = len(state)
        outs = pl.pallas_call(
            functools.partial(next_kernel, block),
            out_shape=(units_shape, *state_shape),
            in_specs=[smem] + [vmem] * (4 + block + kept),
            out_specs=(vmem,) * 5,
            scratch_shapes=code_scratch(1),
            input_output_aliases={5 + block + which: 1 + which for which in range(kept)},
            compiler_params=PARAMS,
            cost_estimate=cost(scores_flops // 4),
            name=f"rows_{block}",
        )(place, codes_in, *table, *units, *state)
        return [*units, outs[0]], outs[1:]

    whole_groups = half_rows == 16 and clusters * half_rows == LANES
    if whole_groups:
        units, state = take_in(0, here, [], ())
        units, state = take_in(1, blocks[1], units, state)
    for mask in masks:
        if mask not in blocks:
            low = mask & -mask
            block = blocks[mask - low]
            if whole_groups:
                left, marks, best, mirror = state
                block, marks = lax.optimization_barrier((block, marks))
                state = (left, marks, best, mirror)
            blocks[mask] = from_member(block, low)
    blocks = [here] + [blocks[mask] for mask in masks]
    if not whole_groups:
        every = jnp.stack(blocks).reshape(members, clusters, members, half_rows, LANES)
        every = every.transpose(2, 0, 1, 3, 4).reshape(members, groups, LANES // 16, 16, LANES)
        every = every.transpose(1, 2, 0, 3, 4).reshape(groups, members * LANES, LANES)
        blocks = list(every)
        units, state = take_in(0, blocks[0], [], ())
        units, state = take_in(1, blocks[1], units, state)
    for block in range(2, groups - 1):
        units, state = take_in(block, blocks[block], units, state)
    nearest, *_ = pl.pallas_call(
        functools.partial(last_kernel, (capacity, clusters, members)),
        out_shape=(jax.ShapeDtypeStruct((tiles, LANES), f32), *state_shape),
        in_specs=[smem] + [vmem] * (groups + 7),
        out_specs=(vmem,) * 5,
        scratch_shapes=[pltpu.VMEM((width, members * COLS), bf16)] + code_scratch(1),
        input_output_aliases={groups + 4 + which: 1 + which for which in range(4)},
        compiler_params=PARAMS,
        cost_estimate=cost(scores_flops),
        name="last_rows",
    )(place, blocks[groups - 1], *table, *units, *state)
    return nearest.reshape(1, 1, slots)


def solution(mesh):
    in_specs = (P("cluster", "blk", None, None), P("cluster", "blk", None, None), P(), P())
    out_specs = P("cluster", "blk", None)
    return jax.shard_map(
        on_device, mesh=mesh, in_specs=in_specs, out_specs=out_specs, check_vma=False
    )
```

```python
import functools

import jax
import jax.numpy as jnp
from jax import lax
from jax.experimental import pallas as pl
from jax.experimental.pallas import tpu as pltpu
from jax.sharding import PartitionSpec as P

LANES = 128
COLS = 256
ROWS = 16
HELD = 12
LOW = -4.0
VMEM_LIMIT = 40 * 1024 * 1024
PARAMS = pltpu.CompilerParams(vmem_limit_bytes=VMEM_LIMIT)
PACK_PARAMS = pltpu.CompilerParams(vmem_limit_bytes=60 * 1024 * 1024)


LANE_LOOKUP = lax.GatherDimensionNumbers(
    offset_dims=(),
    collapsed_slice_dims=(1,),
    start_index_map=(1,),
    operand_batching_dims=(0,),
    start_indices_batching_dims=(0,),
)


def take_lanes(table, index):
    return lax.gather(
        table, index[:, :, None], LANE_LOOKUP, (1, 1),
        mode=lax.GatherScatterMode.PROMISE_IN_BOUNDS,
    )


def pack_kernel(
    devices, capacity, codes_any, routes_any, out_any, codes_ref, routes_ref, out_ref, semaphores
):
    routes_in = pltpu.make_async_copy(routes_any, routes_ref, semaphores.at[0])
    codes_in = pltpu.make_async_copy(codes_any, codes_ref, semaphores.at[1])
    routes_in.start()
    codes_in.start()
    in_rows = codes_ref.shape[1]
    half_rows = capacity // 2
    earlier = (
        lax.broadcasted_iota(jnp.int32, (in_rows, in_rows), 0)
        < lax.broadcasted_iota(jnp.int32, (in_rows, in_rows), 1)
    )
    earlier = jnp.where(earlier, 1.0, 0.0).astype(jnp.bfloat16)
    routes_in.wait()
    targets = routes_ref[...]
    hot = lax.broadcasted_iota(jnp.int32, (devices, in_rows), 0) == targets
    hot32 = jnp.where(hot, 1.0, 0.0)
    running = jnp.dot(
        hot32.astype(jnp.bfloat16), earlier, preferred_element_type=jnp.float32
    )
    position = jnp.sum(hot32 * running, axis=0, keepdims=True).astype(jnp.int32)
    second = position >= half_rows
    key = targets * half_rows + jnp.where(second, position - half_rows, position)
    codes_in.wait()
    values = (codes_ref[...] + 1).astype(jnp.bfloat16)
    out_rows = out_ref.shape[0] // 2
    copies = []
    for part in range(2):
        rows = slice(part * out_rows, (part + 1) * out_rows)
        row_ids = lax.broadcasted_iota(jnp.int32, (out_rows, in_rows), 0) + part * out_rows
        halves = []
        for wanted in (jnp.where(second, -1, key), jnp.where(second, key, -1)):
            move = jnp.where(row_ids == wanted, 1.0, 0.0).astype(jnp.bfloat16)
            halves.append(
                lax.dot_general(
                    move, values, (((1,), (1,)), ((), ())), preferred_element_type=jnp.float32
                )
            )
        out_ref[rows, :] = jnp.concatenate(halves, axis=1).astype(jnp.bfloat16)
        copies.append(
            pltpu.make_async_copy(out_ref.at[rows], out_any.at[rows], semaphores.at[2 + part])
        )
        copies[part].start()
    for copy in copies:
        copy.wait()


def table_kernel(group_ref, book_ref, words_ref, centre_ref, norms_ref):
    width, words = words_ref.shape
    subspaces = norms_ref.shape[0]
    sub_width = width // subspaces
    block = ROWS * sub_width
    new = lax.broadcasted_iota(jnp.int32, (block, block), 0)
    old = lax.broadcasted_iota(jnp.int32, (block, block), 1)
    order = jnp.where(old == (new % ROWS) * sub_width + new // ROWS, 1.0, 0.0).astype(jnp.bfloat16)
    clusters = book_ref.shape[0] - words
    pick = lax.broadcasted_iota(jnp.int32, (1, clusters), 1) == group_ref[0, 0]
    for part in range(width // block):
        rows = slice(part * block, (part + 1) * block)
        turned = lax.dot_general(
            order, book_ref[:, rows], (((1,), (1,)), ((), ())), preferred_element_type=jnp.float32
        )
        centre = jnp.sum(jnp.where(pick, turned[:, words:], 0.0), axis=1, keepdims=True)
        words_ref[rows, :] = turned[:, :words].astype(jnp.bfloat16)
        centre_ref[rows, :] = jnp.broadcast_to(centre, (block, LANES))
        table = turned[:, :words] + centre
        norms_ref[part * ROWS : (part + 1) * ROWS, :] = jnp.sum(
            (table * table).reshape(sub_width, ROWS, words), axis=0
        )


def owner_block(codes_ref, owner, owners):
    parts = [
        codes_ref[pl.ds(pl.multiple_of((part * owners + owner) * 16, 16), 16), :]
        for part in range(LANES // 16)
    ]
    return jnp.concatenate(parts, axis=0)


def unpack_step(
    place, block, turn, codes_ref, norms_ref, code_ref, scale_ref, mark_ref, owners, groups
):
    def step():
        owner = lax.rem(place + turn, owners)
        rows = owner_block(codes_ref, owner, owners)
        turned = jnp.transpose(rows.astype(jnp.float32)).astype(jnp.int32)
        subspaces = turned.shape[0] // 2
        values = []
        for half in range(2):
            part = turned[half * subspaces : (half + 1) * subspaces]
            code = jnp.maximum(part - 1, 0)
            low = code & (LANES - 1)
            squares = jnp.where(
                code >= LANES,
                take_lanes(norms_ref[:, LANES:], low),
                take_lanes(norms_ref[:, :LANES], low),
            )
            scale = lax.rsqrt(jnp.sum(squares, axis=0, keepdims=True) + 1e-06)
            marks = jnp.where(part[0:8] > 0, 1.0, 0.0)
            values.append((code, jnp.broadcast_to(scale, (8, LANES)), marks))
        return values

    def put(values):
        for half, (code, scale, marks) in enumerate(values):
            code_ref[2 * turn + half] = code
            scale_ref[2 * turn + half] = scale
            mark_ref[2 * (turn * groups + block) + half] = marks

    return step, put


def decode_steps(code_ref, scale_ref, tile, words_ref, centre_ref, units_ref, start):
    subspaces = code_ref.shape[1]
    sub_width = words_ref.shape[0] // subspaces

    def step(part):
        code = code_ref[tile, part * ROWS : (part + 1) * ROWS, :].astype(jnp.int16)
        scale = jnp.concatenate([scale_ref[tile]] * (ROWS // 8), axis=0)
        low = code & (LANES - 1)
        high = code > LANES - 1
        values = []
        for entry in range(sub_width):
            row = (part * sub_width + entry) * ROWS
            rows = slice(row, row + ROWS)
            word = jnp.where(
                high,
                take_lanes(words_ref[rows, LANES:], low),
                take_lanes(words_ref[rows, :LANES], low),
            )
            unit = (word.astype(jnp.float32) + centre_ref[rows, :]) * scale
            values.append((rows, unit.astype(jnp.bfloat16)))
        return values

    def put(values):
        for rows, value in values:
            units_ref[rows, pl.ds(start, LANES)] = value

    return [(functools.partial(step, part), put) for part in range(subspaces // ROWS)]


def run(decoding):
    for step, put in decoding:
        put(step())


def mix(scoring, decoding):
    whole = sum(weight for weight, _ in scoring)
    done, behind = 0, 0
    for weight, score_rows in scoring:
        behind += weight
        upto = behind * len(decoding) // whole
        beside = decoding[done : min(upto, done + HELD)]
        held = [(step(), put) for step, put in beside]
        score_rows()
        for values, put in held:
            put(values)
        run(decoding[done + len(beside) : upto])
        done = upto


def turn_own(units_ref, left_ref, block):
    for half in range(2):
        start = block * COLS + half * LANES
        left_ref[start : start + LANES, :] = jnp.transpose(
            units_ref[:, half * LANES : (half + 1) * LANES]
        )


def score(left_ref, rows, units_ref, start, marks, best_ref):
    scores = jnp.dot(
        left_ref[rows, :], units_ref[:, pl.ds(start, COLS)], preferred_element_type=jnp.float32
    )
    best = best_ref[rows, :]
    for part in range(COLS // LANES):
        best = jnp.maximum(
            best, jnp.where(marks[part], scores[:, part * LANES : (part + 1) * LANES], LOW)
        )
    best_ref[rows, :] = best


def own_score(left_ref, units_ref, block, mark_ref, best_ref, mirror_ref):
    above, count = block * COLS, (block + 1) * COLS
    scores = jnp.dot(
        left_ref[:count, :], units_ref[:, :COLS], preferred_element_type=jnp.float32
    )
    row_ids = lax.broadcasted_iota(jnp.int32, (COLS, LANES), 0)
    lane_ids = lax.broadcasted_iota(jnp.int32, (COLS, LANES), 1)
    for part in range(COLS // LANES):
        tile = block * (COLS // LANES) + part
        lanes = slice(part * LANES, (part + 1) * LANES)
        filled = mark_ref[tile][0:1, :] > 0
        keep = filled & (row_ids != lane_ids + part * LANES)
        best_ref[above:count, :] = jnp.maximum(
            best_ref[above:count, :], jnp.where(keep, scores[above:count, lanes], LOW)
        )
        mirror = jnp.full((1, LANES), LOW, jnp.float32)
        for other in range(above // LANES):
            rows = slice(other * LANES, (other + 1) * LANES)
            piece = scores[rows, lanes]
            best_ref[rows, :] = jnp.maximum(best_ref[rows, :], jnp.where(filled, piece, LOW))
            row_filled = jnp.transpose(
                jnp.broadcast_to(mark_ref[other][0:1, :], (LANES, LANES))
            )
            mirror = jnp.maximum(
                mirror,
                jnp.max(jnp.where(row_filled > 0, piece, LOW), axis=0, keepdims=True),
            )
        mirror_ref[tile] = jnp.broadcast_to(mirror, (8, LANES))


def marks_of(mark_ref, group):
    return [mark_ref[2 * group + part][0:1, :] > 0 for part in range(COLS // LANES)]


def block_kernel(block, place, codes_ref, table_refs, units_refs, state):
    left_ref, mark_ref, best_ref, mirror_ref, code_ref, scale_ref = state
    words_ref, centre_ref, norms_ref = table_refs
    units_ref = units_refs[block]
    owners = units_ref.shape[1] // COLS
    groups = left_ref.shape[0] // COLS
    unpacking = [
        unpack_step(
            place, block, turn, codes_ref, norms_ref, code_ref, scale_ref, mark_ref,
            owners, groups,
        )
        for turn in range(owners)
    ]
    run(unpacking[:1])

    def column_of(turn, offset=0):
        column = turn * COLS + offset
        return column if isinstance(turn, int) else pl.multiple_of(column, LANES)

    def decoding(turn):
        steps = []
        for half in range(2):
            steps += decode_steps(
                code_ref, scale_ref, 2 * turn + half, words_ref, centre_ref, units_ref,
                column_of(turn, half * LANES),
            )
        return steps

    def scoring(which, turn, first, last):
        rows = slice(first * COLS, last * COLS)
        return last - first, functools.partial(
            score, left_ref, rows, units_refs[which], column_of(turn),
            marks_of(mark_ref, turn * groups + which), best_ref,
        )

    if block == 0:
        best_ref[...] = jnp.full(best_ref.shape, LOW, jnp.float32)
        run(unpacking[1:] + decoding(0))
    else:
        mix([scoring(block - 1, owners - 1, 0, block)], unpacking[1:] + decoding(0))
    turn_own(units_ref, left_ref, block)

    steps = [
        (
            block + 1,
            functools.partial(
                own_score, left_ref, units_ref, block, mark_ref, best_ref, mirror_ref
            ),
        )
    ]
    for which in range(block):
        steps.append(scoring(which, 1, block, block + 1))
    mix(steps, decoding(1))

    def both(turn, _):
        steps = [scoring(block, turn - 1, 0, block + 1)]
        for which in range(block):
            steps.append(scoring(which, turn, block, block + 1))
        mix(steps, decoding(turn))
        return 0

    lax.fori_loop(2, owners, both, 0)


def next_kernel(block, place_ref, codes_ref, *refs):
    table_refs, refs = refs[:3], refs[3:]
    units_refs, refs = refs[:block], refs[block:]
    units_ref, left_ref, mark_ref, best_ref, mirror_ref, code_ref, scale_ref = refs[-7:]
    block_kernel(
        block, place_ref[0, 0], codes_ref, table_refs, [*units_refs, units_ref],
        (left_ref, mark_ref, best_ref, mirror_ref, code_ref, scale_ref),
    )


def last_kernel(sizes, place_ref, codes_ref, *refs):
    capacity, clusters, members = sizes
    place = place_ref[0, 0]
    table_refs, refs = refs[:3], refs[3:]
    units_refs, refs = refs[:-12], refs[-8:]
    out_ref, left_ref, mark_ref, best_ref, mirror_ref, units_ref, code_ref, scale_ref = refs
    slots = left_ref.shape[0]
    groups = slots // COLS
    owners = units_ref.shape[1] // COLS
    block_kernel(
        groups - 1, place, codes_ref, table_refs, [*units_refs, units_ref],
        (left_ref, mark_ref, best_ref, mirror_ref, code_ref, scale_ref),
    )

    final = (owners - 1) * groups + groups - 1
    score(
        left_ref, slice(0, slots), units_ref, (owners - 1) * COLS, marks_of(mark_ref, final),
        best_ref,
    )

    half_rows = capacity // 2
    tiles = slots // LANES
    lane = lax.broadcasted_iota(jnp.int32, (tiles, LANES), 1)
    slot = lax.broadcasted_iota(jnp.int32, (tiles, LANES), 0) * LANES + lane
    source, within = slot // capacity, slot % capacity
    turn = place ^ (source % members)
    own_row = (turn * clusters + source // members) * half_rows + within % half_rows
    tile_of = 2 * (own_row // LANES) + within // half_rows
    result = jnp.zeros((tiles, LANES), jnp.float32)
    for tile in range(tiles):
        best = jnp.max(
            jnp.transpose(best_ref[tile * LANES : (tile + 1) * LANES, :]), axis=0, keepdims=True
        )
        best = jnp.maximum(best, mirror_ref[tile][0:1, :])
        mark = mark_ref[tile]
        best = jnp.where(mark[0:1, :] > 0, best, 0.0)
        result = jnp.where(
            tile_of == tile,
            take_lanes(jnp.broadcast_to(best, (tiles, LANES)), own_row % LANES),
            result,
        )
    out_ref[...] = result


def on_device(codes, routes, codebook, centroids):
    clusters = lax.axis_size("cluster")
    members = lax.axis_size("blk")
    devices = clusters * members
    subspaces, in_rows = codes.shape[2:]
    capacity = 2 * in_rows // devices
    half_rows = capacity // 2
    slots = devices * capacity
    tiles = slots // LANES
    groups = slots // COLS
    words, width = codebook.shape
    bf16, f32, i32 = jnp.bfloat16, jnp.float32, jnp.int32
    smem = pl.BlockSpec(memory_space=pltpu.SMEM)
    vmem = pl.BlockSpec(memory_space=pltpu.VMEM)

    anywhere = pl.BlockSpec(memory_space=pl.ANY)
    packed = pl.pallas_call(
        functools.partial(pack_kernel, devices, capacity),
        out_shape=jax.ShapeDtypeStruct((in_rows, 2 * subspaces), bf16),
        in_specs=[anywhere] * 2,
        out_specs=anywhere,
        scratch_shapes=[
            pltpu.VMEM((subspaces, in_rows), i32),
            pltpu.VMEM((1, in_rows), i32),
            pltpu.VMEM((in_rows, 2 * subspaces), bf16),
            pltpu.SemaphoreType.DMA((4,)),
        ],
        compiler_params=PACK_PARAMS,
        name="pack_rows",
    )(codes[0, 0], routes.reshape(1, in_rows))
    here = lax.all_to_all(packed, "cluster", split_axis=0, concat_axis=0, tiled=True)
    def from_member(block, mask):
        return lax.ppermute(block, "blk", [(i, i ^ mask) for i in range(members)])

    masks = range(1, members)
    blocks = {0: here}
    for mask in masks:
        if mask & (mask - 1) == 0:
            blocks[mask] = from_member(here, mask)

    place = lax.axis_index("blk").astype(i32).reshape(1, 1)
    group = lax.axis_index("cluster").astype(i32).reshape(1, 1)
    table = pl.pallas_call(
        table_kernel,
        out_shape=(
            jax.ShapeDtypeStruct((width, words), bf16),
            jax.ShapeDtypeStruct((width, LANES), f32),
            jax.ShapeDtypeStruct((subspaces, words), f32),
        ),
        in_specs=[smem, vmem],
        compiler_params=PARAMS,
        cost_estimate=pl.CostEstimate(
            flops=4 * words * width, bytes_accessed=6 * words * width, transcendentals=0
        ),
        name="word_table",
    )(group, jnp.concatenate([codebook, centroids], axis=0))

    units_shape = jax.ShapeDtypeStruct((width, members * COLS), bf16)
    state_shape = (
        jax.ShapeDtypeStruct((slots, width), bf16),
        jax.ShapeDtypeStruct((2 * members * groups, 8, LANES), f32),
        jax.ShapeDtypeStruct((slots, LANES), f32),
        jax.ShapeDtypeStruct((tiles, 8, LANES), f32),
    )

    def code_scratch(count):
        return [
            pltpu.VMEM((2 * members * count, subspaces, LANES), i32),
            pltpu.VMEM((2 * members * count, 8, LANES), f32),
        ]

    def cost(flops):
        return pl.CostEstimate(
            flops=flops, bytes_accessed=16 * slots * width, transcendentals=0
        )

    scores_flops = 2 * slots * members * slots * width
    def take_in(block, codes_in, units, state):
        kept = len(state)
        outs = pl.pallas_call(
            functools.partial(next_kernel, block),
            out_shape=(units_shape, *state_shape),
            in_specs=[smem] + [vmem] * (4 + block + kept),
            out_specs=(vmem,) * 5,
            scratch_shapes=code_scratch(1),
            input_output_aliases={5 + block + which: 1 + which for which in range(kept)},
            compiler_params=PARAMS,
            cost_estimate=cost(scores_flops // 4),
            name=f"rows_{block}",
        )(place, codes_in, *table, *units, *state)
        return [*units, outs[0]], outs[1:]

    whole_groups = half_rows == 16 and clusters * half_rows == LANES
    if whole_groups:
        units, state = take_in(0, here, [], ())
        units, state = take_in(1, blocks[1], units, state)
    for mask in masks:
        if mask not in blocks:
            low = mask & -mask
            block = blocks[mask - low]
            if whole_groups:
                left, marks, best, mirror = state
                block, marks = lax.optimization_barrier((block, marks))
                state = (left, marks, best, mirror)
            blocks[mask] = from_member(block, low)
    blocks = [here] + [blocks[mask] for mask in masks]
    if not whole_groups:
        every = jnp.stack(blocks).reshape(members, clusters, members, half_rows, LANES)
        every = every.transpose(2, 0, 1, 3, 4).reshape(members, groups, LANES // 16, 16, LANES)
        every = every.transpose(1, 2, 0, 3, 4).reshape(groups, members * LANES, LANES)
        blocks = list(every)
        units, state = take_in(0, blocks[0], [], ())
        units, state = take_in(1, blocks[1], units, state)
    for block in range(2, groups - 1):
        units, state = take_in(block, blocks[block], units, state)
    nearest, *_ = pl.pallas_call(
        functools.partial(last_kernel, (capacity, clusters, members)),
        out_shape=(jax.ShapeDtypeStruct((tiles, LANES), f32), *state_shape),
        in_specs=[smem] + [vmem] * (groups + 7),
        out_specs=(vmem,) * 5,
        scratch_shapes=[pltpu.VMEM((width, members * COLS), bf16)] + code_scratch(1),
        input_output_aliases={groups + 4 + which: 1 + which for which in range(4)},
        compiler_params=PARAMS,
        cost_estimate=cost(scores_flops),
        name="last_rows",
    )(place, blocks[groups - 1], *table, *units, *state)
    return nearest.reshape(1, 1, slots)


def solution(mesh):
    in_specs = (P("cluster", "blk", None, None), P("cluster", "blk", None, None), P(), P())
    out_specs = P("cluster", "blk", None)
    return jax.shard_map(
        on_device, mesh=mesh, in_specs=in_specs, out_specs=out_specs, check_vma=False
    )
```

```python
import functools

import jax
import jax.numpy as jnp
from jax import lax
from jax.experimental import pallas as pl
from jax.experimental.pallas import tpu as pltpu
from jax.sharding import PartitionSpec as P

LANES = 128
COLS = 256
ROWS = 16
HELD = 12
LOW = -4.0
VMEM_LIMIT = 40 * 1024 * 1024
PARAMS = pltpu.CompilerParams(vmem_limit_bytes=VMEM_LIMIT)
PACK_PARAMS = pltpu.CompilerParams(vmem_limit_bytes=60 * 1024 * 1024)


LANE_LOOKUP = lax.GatherDimensionNumbers(
    offset_dims=(),
    collapsed_slice_dims=(1,),
    start_index_map=(1,),
    operand_batching_dims=(0,),
    start_indices_batching_dims=(0,),
)


def take_lanes(table, index):
    return lax.gather(
        table, index[:, :, None], LANE_LOOKUP, (1, 1),
        mode=lax.GatherScatterMode.PROMISE_IN_BOUNDS,
    )


def pack_kernel(
    devices, capacity, codes_any, routes_any, out_any, codes_ref, routes_ref, out_ref, semaphores
):
    routes_in = pltpu.make_async_copy(routes_any, routes_ref, semaphores.at[0])
    codes_in = pltpu.make_async_copy(codes_any, codes_ref, semaphores.at[1])
    routes_in.start()
    codes_in.start()
    in_rows = codes_ref.shape[1]
    half_rows = capacity // 2
    earlier = (
        lax.broadcasted_iota(jnp.int32, (in_rows, in_rows), 0)
        < lax.broadcasted_iota(jnp.int32, (in_rows, in_rows), 1)
    )
    earlier = jnp.where(earlier, 1.0, 0.0).astype(jnp.bfloat16)
    routes_in.wait()
    targets = routes_ref[...]
    hot = lax.broadcasted_iota(jnp.int32, (devices, in_rows), 0) == targets
    hot32 = jnp.where(hot, 1.0, 0.0)
    running = jnp.dot(
        hot32.astype(jnp.bfloat16), earlier, preferred_element_type=jnp.float32
    )
    position = jnp.sum(hot32 * running, axis=0, keepdims=True).astype(jnp.int32)
    second = position >= half_rows
    key = targets * half_rows + jnp.where(second, position - half_rows, position)
    codes_in.wait()
    values = (codes_ref[...] + 1).astype(jnp.bfloat16)
    out_rows = out_ref.shape[0] // 2
    copies = []
    for part in range(2):
        rows = slice(part * out_rows, (part + 1) * out_rows)
        row_ids = lax.broadcasted_iota(jnp.int32, (out_rows, in_rows), 0) + part * out_rows
        halves = []
        for wanted in (jnp.where(second, -1, key), jnp.where(second, key, -1)):
            move = jnp.where(row_ids == wanted, 1.0, 0.0).astype(jnp.bfloat16)
            halves.append(
                lax.dot_general(
                    move, values, (((1,), (1,)), ((), ())), preferred_element_type=jnp.float32
                )
            )
        out_ref[rows, :] = jnp.concatenate(halves, axis=1).astype(jnp.bfloat16)
        copies.append(
            pltpu.make_async_copy(out_ref.at[rows], out_any.at[rows], semaphores.at[2 + part])
        )
        copies[part].start()
    for copy in copies:
        copy.wait()


def table_kernel(group_ref, book_ref, words_ref, centre_ref, norms_ref):
    width, words = words_ref.shape
    subspaces = norms_ref.shape[0]
    sub_width = width // subspaces
    block = ROWS * sub_width
    new = lax.broadcasted_iota(jnp.int32, (block, block), 0)
    old = lax.broadcasted_iota(jnp.int32, (block, block), 1)
    order = jnp.where(old == (new % ROWS) * sub_width + new // ROWS, 1.0, 0.0).astype(jnp.bfloat16)
    clusters = book_ref.shape[0] - words
    pick = lax.broadcasted_iota(jnp.int32, (1, clusters), 1) == group_ref[0, 0]
    for part in range(width // block):
        rows = slice(part * block, (part + 1) * block)
        turned = lax.dot_general(
            order, book_ref[:, rows], (((1,), (1,)), ((), ())), preferred_element_type=jnp.float32
        )
        centre = jnp.sum(jnp.where(pick, turned[:, words:], 0.0), axis=1, keepdims=True)
        words_ref[rows, :] = turned[:, :words].astype(jnp.bfloat16)
        centre_ref[rows, :] = jnp.broadcast_to(centre, (block, LANES))
        table = turned[:, :words] + centre
        norms_ref[part * ROWS : (part + 1) * ROWS, :] = jnp.sum(
            (table * table).reshape(sub_width, ROWS, words), axis=0
        )


def owner_block(codes_ref, owner, owners):
    parts = [
        codes_ref[pl.ds(pl.multiple_of((part * owners + owner) * 16, 16), 16), :]
        for part in range(LANES // 16)
    ]
    return jnp.concatenate(parts, axis=0)


def unpack_step(
    place, block, turn, codes_ref, norms_ref, code_ref, scale_ref, mark_ref, owners, groups
):
    def step():
        owner = lax.rem(place + turn, owners)
        rows = owner_block(codes_ref, owner, owners)
        turned = jnp.transpose(rows.astype(jnp.float32)).astype(jnp.int32)
        subspaces = turned.shape[0] // 2
        values = []
        for half in range(2):
            part = turned[half * subspaces : (half + 1) * subspaces]
            code = jnp.maximum(part - 1, 0)
            low = code & (LANES - 1)
            squares = jnp.where(
                code >= LANES,
                take_lanes(norms_ref[:, LANES:], low),
                take_lanes(norms_ref[:, :LANES], low),
            )
            scale = lax.rsqrt(jnp.sum(squares, axis=0, keepdims=True) + 1e-06)
            marks = jnp.where(part[0:8] > 0, 1.0, 0.0)
            values.append((code, jnp.broadcast_to(scale, (8, LANES)), marks))
        return values

    def put(values):
        for half, (code, scale, marks) in enumerate(values):
            code_ref[2 * turn + half] = code
            scale_ref[2 * turn + half] = scale
            mark_ref[2 * (turn * groups + block) + half] = marks

    return step, put


def decode_steps(code_ref, scale_ref, tile, words_ref, centre_ref, units_ref, start):
    subspaces = code_ref.shape[1]
    sub_width = words_ref.shape[0] // subspaces

    def step(part):
        code = code_ref[tile, part * ROWS : (part + 1) * ROWS, :].astype(jnp.int16)
        scale = jnp.concatenate([scale_ref[tile]] * (ROWS // 8), axis=0)
        low = code & (LANES - 1)
        high = code > LANES - 1
        values = []
        for entry in range(sub_width):
            row = (part * sub_width + entry) * ROWS
            rows = slice(row, row + ROWS)
            word = jnp.where(
                high,
                take_lanes(words_ref[rows, LANES:], low),
                take_lanes(words_ref[rows, :LANES], low),
            )
            unit = (word.astype(jnp.float32) + centre_ref[rows, :]) * scale
            values.append((rows, unit.astype(jnp.bfloat16)))
        return values

    def put(values):
        for rows, value in values:
            units_ref[rows, pl.ds(start, LANES)] = value

    return [(functools.partial(step, part), put) for part in range(subspaces // ROWS)]


def run(decoding):
    for step, put in decoding:
        put(step())


def mix(scoring, decoding):
    whole = sum(weight for weight, _ in scoring)
    done, behind = 0, 0
    for weight, score_rows in scoring:
        behind += weight
        upto = behind * len(decoding) // whole
        beside = decoding[done : min(upto, done + HELD)]
        held = [(step(), put) for step, put in beside]
        score_rows()
        for values, put in held:
            put(values)
        run(decoding[done + len(beside) : upto])
        done = upto


def turn_own(units_ref, left_ref, block):
    for half in range(2):
        start = block * COLS + half * LANES
        left_ref[start : start + LANES, :] = jnp.transpose(
            units_ref[:, half * LANES : (half + 1) * LANES]
        )


def score(left_ref, rows, units_ref, start, marks, best_ref):
    scores = jnp.dot(
        left_ref[rows, :], units_ref[:, pl.ds(start, COLS)], preferred_element_type=jnp.float32
    )
    best = best_ref[rows, :]
    for part in range(COLS // LANES):
        best = jnp.maximum(
            best, jnp.where(marks[part], scores[:, part * LANES : (part + 1) * LANES], LOW)
        )
    best_ref[rows, :] = best


def own_score(left_ref, units_ref, block, mark_ref, best_ref, mirror_ref):
    above, count = block * COLS, (block + 1) * COLS
    scores = jnp.dot(
        left_ref[:count, :], units_ref[:, :COLS], preferred_element_type=jnp.float32
    )
    row_ids = lax.broadcasted_iota(jnp.int32, (COLS, LANES), 0)
    lane_ids = lax.broadcasted_iota(jnp.int32, (COLS, LANES), 1)
    for part in range(COLS // LANES):
        tile = block * (COLS // LANES) + part
        lanes = slice(part * LANES, (part + 1) * LANES)
        filled = mark_ref[tile][0:1, :] > 0
        keep = filled & (row_ids != lane_ids + part * LANES)
        best_ref[above:count, :] = jnp.maximum(
            best_ref[above:count, :], jnp.where(keep, scores[above:count, lanes], LOW)
        )
        mirror = jnp.full((1, LANES), LOW, jnp.float32)
        for other in range(above // LANES):
            rows = slice(other * LANES, (other + 1) * LANES)
            piece = scores[rows, lanes]
            best_ref[rows, :] = jnp.maximum(best_ref[rows, :], jnp.where(filled, piece, LOW))
            row_filled = jnp.transpose(
                jnp.broadcast_to(mark_ref[other][0:1, :], (LANES, LANES))
            )
            mirror = jnp.maximum(
                mirror,
                jnp.max(jnp.where(row_filled > 0, piece, LOW), axis=0, keepdims=True),
            )
        mirror_ref[tile] = jnp.broadcast_to(mirror, (8, LANES))


def marks_of(mark_ref, group):
    return [mark_ref[2 * group + part][0:1, :] > 0 for part in range(COLS // LANES)]


def block_kernel(block, place, codes_ref, table_refs, units_refs, state):
    left_ref, mark_ref, best_ref, mirror_ref, code_ref, scale_ref = state
    words_ref, centre_ref, norms_ref = table_refs
    units_ref = units_refs[block]
    owners = units_ref.shape[1] // COLS
    groups = left_ref.shape[0] // COLS
    unpacking = [
        unpack_step(
            place, block, turn, codes_ref, norms_ref, code_ref, scale_ref, mark_ref,
            owners, groups,
        )
        for turn in range(owners)
    ]
    run(unpacking[:1])

    def column_of(turn, offset=0):
        column = turn * COLS + offset
        return column if isinstance(turn, int) else pl.multiple_of(column, LANES)

    def decoding(turn):
        steps = []
        for half in range(2):
            steps += decode_steps(
                code_ref, scale_ref, 2 * turn + half, words_ref, centre_ref, units_ref,
                column_of(turn, half * LANES),
            )
        return steps

    def scoring(which, turn, first, last):
        rows = slice(first * COLS, last * COLS)
        return last - first, functools.partial(
            score, left_ref, rows, units_refs[which], column_of(turn),
            marks_of(mark_ref, turn * groups + which), best_ref,
        )

    if block == 0:
        best_ref[...] = jnp.full(best_ref.shape, LOW, jnp.float32)
        run(unpacking[1:2] + decoding(0))
    else:
        mix([scoring(block - 1, owners - 1, 0, block)], unpacking[1:2] + decoding(0))
    turn_own(units_ref, left_ref, block)

    steps = [
        (
            block + 1,
            functools.partial(
                own_score, left_ref, units_ref, block, mark_ref, best_ref, mirror_ref
            ),
        )
    ]
    for which in range(block):
        steps.append(scoring(which, 1, block, block + 1))
    mix(steps, unpacking[2:] + decoding(1))

    def both(turn, _):
        steps = [scoring(block, turn - 1, 0, block + 1)]
        for which in range(block):
            steps.append(scoring(which, turn, block, block + 1))
        mix(steps, decoding(turn))
        return 0

    lax.fori_loop(2, owners, both, 0)


def next_kernel(block, place_ref, codes_ref, *refs):
    table_refs, refs = refs[:3], refs[3:]
    units_refs, refs = refs[:block], refs[block:]
    units_ref, left_ref, mark_ref, best_ref, mirror_ref, code_ref, scale_ref = refs[-7:]
    block_kernel(
        block, place_ref[0, 0], codes_ref, table_refs, [*units_refs, units_ref],
        (left_ref, mark_ref, best_ref, mirror_ref, code_ref, scale_ref),
    )


def last_kernel(sizes, place_ref, codes_ref, *refs):
    capacity, clusters, members = sizes
    place = place_ref[0, 0]
    table_refs, refs = refs[:3], refs[3:]
    units_refs, refs = refs[:-12], refs[-8:]
    out_ref, left_ref, mark_ref, best_ref, mirror_ref, units_ref, code_ref, scale_ref = refs
    slots = left_ref.shape[0]
    groups = slots // COLS
    owners = units_ref.shape[1] // COLS
    block_kernel(
        groups - 1, place, codes_ref, table_refs, [*units_refs, units_ref],
        (left_ref, mark_ref, best_ref, mirror_ref, code_ref, scale_ref),
    )

    final = (owners - 1) * groups + groups - 1
    score(
        left_ref, slice(0, slots), units_ref, (owners - 1) * COLS, marks_of(mark_ref, final),
        best_ref,
    )

    half_rows = capacity // 2
    tiles = slots // LANES
    lane = lax.broadcasted_iota(jnp.int32, (tiles, LANES), 1)
    slot = lax.broadcasted_iota(jnp.int32, (tiles, LANES), 0) * LANES + lane
    source, within = slot // capacity, slot % capacity
    turn = place ^ (source % members)
    own_row = (turn * clusters + source // members) * half_rows + within % half_rows
    tile_of = 2 * (own_row // LANES) + within // half_rows
    result = jnp.zeros((tiles, LANES), jnp.float32)
    for tile in range(tiles):
        best = jnp.max(
            jnp.transpose(best_ref[tile * LANES : (tile + 1) * LANES, :]), axis=0, keepdims=True
        )
        best = jnp.maximum(best, mirror_ref[tile][0:1, :])
        mark = mark_ref[tile]
        best = jnp.where(mark[0:1, :] > 0, best, 0.0)
        result = jnp.where(
            tile_of == tile,
            take_lanes(jnp.broadcast_to(best, (tiles, LANES)), own_row % LANES),
            result,
        )
    out_ref[...] = result


def on_device(codes, routes, codebook, centroids):
    clusters = lax.axis_size("cluster")
    members = lax.axis_size("blk")
    devices = clusters * members
    subspaces, in_rows = codes.shape[2:]
    capacity = 2 * in_rows // devices
    half_rows = capacity // 2
    slots = devices * capacity
    tiles = slots // LANES
    groups = slots // COLS
    words, width = codebook.shape
    bf16, f32, i32 = jnp.bfloat16, jnp.float32, jnp.int32
    smem = pl.BlockSpec(memory_space=pltpu.SMEM)
    vmem = pl.BlockSpec(memory_space=pltpu.VMEM)

    anywhere = pl.BlockSpec(memory_space=pl.ANY)
    packed = pl.pallas_call(
        functools.partial(pack_kernel, devices, capacity),
        out_shape=jax.ShapeDtypeStruct((in_rows, 2 * subspaces), bf16),
        in_specs=[anywhere] * 2,
        out_specs=anywhere,
        scratch_shapes=[
            pltpu.VMEM((subspaces, in_rows), i32),
            pltpu.VMEM((1, in_rows), i32),
            pltpu.VMEM((in_rows, 2 * subspaces), bf16),
            pltpu.SemaphoreType.DMA((4,)),
        ],
        compiler_params=PACK_PARAMS,
        name="pack_rows",
    )(codes[0, 0], routes.reshape(1, in_rows))
    here = lax.all_to_all(packed, "cluster", split_axis=0, concat_axis=0, tiled=True)
    def from_member(block, mask):
        return lax.ppermute(block, "blk", [(i, i ^ mask) for i in range(members)])

    masks = range(1, members)
    blocks = {0: here}
    for mask in masks:
        if mask & (mask - 1) == 0:
            blocks[mask] = from_member(here, mask)

    place = lax.axis_index("blk").astype(i32).reshape(1, 1)
    group = lax.axis_index("cluster").astype(i32).reshape(1, 1)
    table = pl.pallas_call(
        table_kernel,
        out_shape=(
            jax.ShapeDtypeStruct((width, words), bf16),
            jax.ShapeDtypeStruct((width, LANES), f32),
            jax.ShapeDtypeStruct((subspaces, words), f32),
        ),
        in_specs=[smem, vmem],
        compiler_params=PARAMS,
        cost_estimate=pl.CostEstimate(
            flops=4 * words * width, bytes_accessed=6 * words * width, transcendentals=0
        ),
        name="word_table",
    )(group, jnp.concatenate([codebook, centroids], axis=0))

    units_shape = jax.ShapeDtypeStruct((width, members * COLS), bf16)
    state_shape = (
        jax.ShapeDtypeStruct((slots, width), bf16),
        jax.ShapeDtypeStruct((2 * members * groups, 8, LANES), f32),
        jax.ShapeDtypeStruct((slots, LANES), f32),
        jax.ShapeDtypeStruct((tiles, 8, LANES), f32),
    )

    def code_scratch(count):
        return [
            pltpu.VMEM((2 * members * count, subspaces, LANES), i32),
            pltpu.VMEM((2 * members * count, 8, LANES), f32),
        ]

    def cost(flops):
        return pl.CostEstimate(
            flops=flops, bytes_accessed=16 * slots * width, transcendentals=0
        )

    scores_flops = 2 * slots * members * slots * width
    def take_in(block, codes_in, units, state):
        kept = len(state)
        outs = pl.pallas_call(
            functools.partial(next_kernel, block),
            out_shape=(units_shape, *state_shape),
            in_specs=[smem] + [vmem] * (4 + block + kept),
            out_specs=(vmem,) * 5,
            scratch_shapes=code_scratch(1),
            input_output_aliases={5 + block + which: 1 + which for which in range(kept)},
            compiler_params=PARAMS,
            cost_estimate=cost(scores_flops // 4),
            name=f"rows_{block}",
        )(place, codes_in, *table, *units, *state)
        return [*units, outs[0]], outs[1:]

    whole_groups = half_rows == 16 and clusters * half_rows == LANES
    if whole_groups:
        units, state = take_in(0, here, [], ())
        units, state = take_in(1, blocks[1], units, state)
    for mask in masks:
        if mask not in blocks:
            low = mask & -mask
            block = blocks[mask - low]
            if whole_groups:
                left, marks, best, mirror = state
                block, marks = lax.optimization_barrier((block, marks))
                state = (left, marks, best, mirror)
            blocks[mask] = from_member(block, low)
    blocks = [here] + [blocks[mask] for mask in masks]
    if not whole_groups:
        every = jnp.stack(blocks).reshape(members, clusters, members, half_rows, LANES)
        every = every.transpose(2, 0, 1, 3, 4).reshape(members, groups, LANES // 16, 16, LANES)
        every = every.transpose(1, 2, 0, 3, 4).reshape(groups, members * LANES, LANES)
        blocks = list(every)
        units, state = take_in(0, blocks[0], [], ())
        units, state = take_in(1, blocks[1], units, state)
    for block in range(2, groups - 1):
        units, state = take_in(block, blocks[block], units, state)
    nearest, *_ = pl.pallas_call(
        functools.partial(last_kernel, (capacity, clusters, members)),
        out_shape=(jax.ShapeDtypeStruct((tiles, LANES), f32), *state_shape),
        in_specs=[smem] + [vmem] * (groups + 7),
        out_specs=(vmem,) * 5,
        scratch_shapes=[pltpu.VMEM((width, members * COLS), bf16)] + code_scratch(1),
        input_output_aliases={groups + 4 + which: 1 + which for which in range(4)},
        compiler_params=PARAMS,
        cost_estimate=cost(scores_flops),
        name="last_rows",
    )(place, blocks[groups - 1], *table, *units, *state)
    return nearest.reshape(1, 1, slots)


def solution(mesh):
    in_specs = (P("cluster", "blk", None, None), P("cluster", "blk", None, None), P(), P())
    out_specs = P("cluster", "blk", None)
    return jax.shard_map(
        on_device, mesh=mesh, in_specs=in_specs, out_specs=out_specs, check_vma=False
    )
```

```python
import functools

import jax
import jax.numpy as jnp
from jax import lax
from jax.experimental import pallas as pl
from jax.experimental.pallas import tpu as pltpu
from jax.sharding import PartitionSpec as P

LANES = 128
COLS = 256
ROWS = 16
HELD = 12
LOW = -4.0
VMEM_LIMIT = 40 * 1024 * 1024
PARAMS = pltpu.CompilerParams(vmem_limit_bytes=VMEM_LIMIT)
PACK_PARAMS = pltpu.CompilerParams(vmem_limit_bytes=60 * 1024 * 1024)


LANE_LOOKUP = lax.GatherDimensionNumbers(
    offset_dims=(),
    collapsed_slice_dims=(1,),
    start_index_map=(1,),
    operand_batching_dims=(0,),
    start_indices_batching_dims=(0,),
)


def take_lanes(table, index):
    return lax.gather(
        table, index[:, :, None], LANE_LOOKUP, (1, 1),
        mode=lax.GatherScatterMode.PROMISE_IN_BOUNDS,
    )


def pack_kernel(
    devices, capacity, codes_any, routes_any, out_any, codes_ref, routes_ref, out_ref, semaphores
):
    routes_in = pltpu.make_async_copy(routes_any, routes_ref, semaphores.at[0])
    codes_in = pltpu.make_async_copy(codes_any, codes_ref, semaphores.at[1])
    routes_in.start()
    codes_in.start()
    in_rows = codes_ref.shape[1]
    half_rows = capacity // 2
    earlier = (
        lax.broadcasted_iota(jnp.int32, (in_rows, in_rows), 0)
        < lax.broadcasted_iota(jnp.int32, (in_rows, in_rows), 1)
    )
    earlier = jnp.where(earlier, 1.0, 0.0).astype(jnp.bfloat16)
    routes_in.wait()
    targets = routes_ref[...]
    hot = lax.broadcasted_iota(jnp.int32, (devices, in_rows), 0) == targets
    hot32 = jnp.where(hot, 1.0, 0.0)
    running = jnp.dot(
        hot32.astype(jnp.bfloat16), earlier, preferred_element_type=jnp.float32
    )
    position = jnp.sum(hot32 * running, axis=0, keepdims=True).astype(jnp.int32)
    second = position >= half_rows
    key = targets * half_rows + jnp.where(second, position - half_rows, position)
    codes_in.wait()
    values = (codes_ref[...] + 1).astype(jnp.bfloat16)
    out_rows = out_ref.shape[0] // 2
    copies = []
    for part in range(2):
        rows = slice(part * out_rows, (part + 1) * out_rows)
        row_ids = lax.broadcasted_iota(jnp.int32, (out_rows, in_rows), 0) + part * out_rows
        halves = []
        for wanted in (jnp.where(second, -1, key), jnp.where(second, key, -1)):
            move = jnp.where(row_ids == wanted, 1.0, 0.0).astype(jnp.bfloat16)
            halves.append(
                lax.dot_general(
                    move, values, (((1,), (1,)), ((), ())), preferred_element_type=jnp.float32
                )
            )
        out_ref[rows, :] = jnp.concatenate(halves, axis=1).astype(jnp.bfloat16)
        copies.append(
            pltpu.make_async_copy(out_ref.at[rows], out_any.at[rows], semaphores.at[2 + part])
        )
        copies[part].start()
    for copy in copies:
        copy.wait()


def table_kernel(group_ref, book_ref, words_ref, centre_ref, norms_ref):
    width, words = words_ref.shape
    subspaces = norms_ref.shape[0]
    sub_width = width // subspaces
    block = ROWS * sub_width
    new = lax.broadcasted_iota(jnp.int32, (block, block), 0)
    old = lax.broadcasted_iota(jnp.int32, (block, block), 1)
    order = jnp.where(old == (new % ROWS) * sub_width + new // ROWS, 1.0, 0.0).astype(jnp.bfloat16)
    clusters = book_ref.shape[0] - words
    pick = lax.broadcasted_iota(jnp.int32, (1, clusters), 1) == group_ref[0, 0]
    for part in range(width // block):
        rows = slice(part * block, (part + 1) * block)
        turned = lax.dot_general(
            order, book_ref[:, rows], (((1,), (1,)), ((), ())), preferred_element_type=jnp.float32
        )
        centre = jnp.sum(jnp.where(pick, turned[:, words:], 0.0), axis=1, keepdims=True)
        words_ref[rows, :] = turned[:, :words].astype(jnp.bfloat16)
        centre_ref[rows, :] = jnp.broadcast_to(centre, (block, LANES))
        table = turned[:, :words] + centre
        norms_ref[part * ROWS : (part + 1) * ROWS, :] = jnp.sum(
            (table * table).reshape(sub_width, ROWS, words), axis=0
        )


def owner_block(codes_ref, owner, owners):
    parts = [
        codes_ref[pl.ds(pl.multiple_of((part * owners + owner) * 16, 16), 16), :]
        for part in range(LANES // 16)
    ]
    return jnp.concatenate(parts, axis=0)


def unpack_step(
    place, block, turn, codes_ref, norms_ref, code_ref, scale_ref, mark_ref, owners, groups
):
    def step():
        owner = lax.rem(place + turn, owners)
        rows = owner_block(codes_ref, owner, owners)
        turned = jnp.transpose(rows.astype(jnp.float32)).astype(jnp.int32)
        subspaces = turned.shape[0] // 2
        values = []
        for half in range(2):
            part = turned[half * subspaces : (half + 1) * subspaces]
            code = jnp.maximum(part - 1, 0)
            low = code & (LANES - 1)
            squares = jnp.where(
                code >= LANES,
                take_lanes(norms_ref[:, LANES:], low),
                take_lanes(norms_ref[:, :LANES], low),
            )
            scale = lax.rsqrt(jnp.sum(squares, axis=0, keepdims=True) + 1e-06)
            marks = jnp.where(part[0:8] > 0, 1.0, 0.0)
            values.append((code, jnp.broadcast_to(scale, (8, LANES)), marks))
        return values

    def put(values):
        for half, (code, scale, marks) in enumerate(values):
            code_ref[2 * turn + half] = code
            scale_ref[2 * turn + half] = scale
            mark_ref[2 * (turn * groups + block) + half] = marks

    return step, put


def decode_steps(code_ref, scale_ref, tile, words_ref, centre_ref, units_ref, start):
    subspaces = code_ref.shape[1]
    sub_width = words_ref.shape[0] // subspaces

    def step(part):
        code = code_ref[tile, part * ROWS : (part + 1) * ROWS, :].astype(jnp.int16)
        scale = jnp.concatenate([scale_ref[tile]] * (ROWS // 8), axis=0)
        low = code & (LANES - 1)
        high = code > LANES - 1
        values = []
        for entry in range(sub_width):
            row = (part * sub_width + entry) * ROWS
            rows = slice(row, row + ROWS)
            word = jnp.where(
                high,
                take_lanes(words_ref[rows, LANES:], low),
                take_lanes(words_ref[rows, :LANES], low),
            )
            unit = (word.astype(jnp.float32) + centre_ref[rows, :]) * scale
            values.append((rows, unit.astype(jnp.bfloat16)))
        return values

    def put(values):
        for rows, value in values:
            units_ref[rows, pl.ds(start, LANES)] = value

    return [(functools.partial(step, part), put) for part in range(subspaces // ROWS)]


def run(decoding):
    for step, put in decoding:
        put(step())


def mix(scoring, decoding):
    whole = sum(weight for weight, _ in scoring)
    done, behind = 0, 0
    for weight, score_rows in scoring:
        behind += weight
        upto = behind * len(decoding) // whole
        beside = decoding[done : min(upto, done + HELD)]
        held = [(step(), put) for step, put in beside]
        score_rows()
        for values, put in held:
            put(values)
        run(decoding[done + len(beside) : upto])
        done = upto


def turn_own(units_ref, left_ref, block):
    for half in range(2):
        start = block * COLS + half * LANES
        left_ref[start : start + LANES, :] = jnp.transpose(
            units_ref[:, half * LANES : (half + 1) * LANES]
        )


def score(left_ref, rows, units_ref, start, marks, best_ref):
    scores = jnp.dot(
        left_ref[rows, :], units_ref[:, pl.ds(start, COLS)], preferred_element_type=jnp.float32
    )
    best = best_ref[rows, :]
    for part in range(COLS // LANES):
        best = jnp.maximum(
            best, jnp.where(marks[part], scores[:, part * LANES : (part + 1) * LANES], LOW)
        )
    best_ref[rows, :] = best


def own_score(left_ref, units_ref, block, mark_ref, best_ref, mirror_ref):
    above, count = block * COLS, (block + 1) * COLS
    scores = jnp.dot(
        left_ref[:count, :], units_ref[:, :COLS], preferred_element_type=jnp.float32
    )
    row_ids = lax.broadcasted_iota(jnp.int32, (COLS, LANES), 0)
    lane_ids = lax.broadcasted_iota(jnp.int32, (COLS, LANES), 1)
    row_filled = [
        jnp.transpose(jnp.broadcast_to(mark_ref[other][0:1, :], (LANES, LANES))) > 0
        for other in range(above // LANES)
    ]
    for part in range(COLS // LANES):
        tile = block * (COLS // LANES) + part
        lanes = slice(part * LANES, (part + 1) * LANES)
        filled = mark_ref[tile][0:1, :] > 0
        keep = filled & (row_ids != lane_ids + part * LANES)
        best_ref[above:count, :] = jnp.maximum(
            best_ref[above:count, :], jnp.where(keep, scores[above:count, lanes], LOW)
        )
        mirror = jnp.full((1, LANES), LOW, jnp.float32)
        for other in range(above // LANES):
            rows = slice(other * LANES, (other + 1) * LANES)
            piece = scores[rows, lanes]
            best_ref[rows, :] = jnp.maximum(best_ref[rows, :], jnp.where(filled, piece, LOW))
            mirror = jnp.maximum(
                mirror,
                jnp.max(jnp.where(row_filled[other], piece, LOW), axis=0, keepdims=True),
            )
        mirror_ref[tile] = jnp.broadcast_to(mirror, (8, LANES))


def marks_of(mark_ref, group):
    return [mark_ref[2 * group + part][0:1, :] > 0 for part in range(COLS // LANES)]


def block_kernel(block, place, codes_ref, table_refs, units_refs, state):
    left_ref, mark_ref, best_ref, mirror_ref, code_ref, scale_ref = state
    words_ref, centre_ref, norms_ref = table_refs
    units_ref = units_refs[block]
    owners = units_ref.shape[1] // COLS
    groups = left_ref.shape[0] // COLS
    unpacking = [
        unpack_step(
            place, block, turn, codes_ref, norms_ref, code_ref, scale_ref, mark_ref,
            owners, groups,
        )
        for turn in range(owners)
    ]
    run(unpacking[:1])

    def column_of(turn, offset=0):
        column = turn * COLS + offset
        return column if isinstance(turn, int) else pl.multiple_of(column, LANES)

    def decoding(turn):
        steps = []
        for half in range(2):
            steps += decode_steps(
                code_ref, scale_ref, 2 * turn + half, words_ref, centre_ref, units_ref,
                column_of(turn, half * LANES),
            )
        return steps

    def scoring(which, turn, first, last):
        rows = slice(first * COLS, last * COLS)
        return last - first, functools.partial(
            score, left_ref, rows, units_refs[which], column_of(turn),
            marks_of(mark_ref, turn * groups + which), best_ref,
        )

    if block == 0:
        best_ref[...] = jnp.full(best_ref.shape, LOW, jnp.float32)
        run(unpacking[1:2] + decoding(0))
    else:
        mix([scoring(block - 1, owners - 1, 0, block)], unpacking[1:2] + decoding(0))
    turn_own(units_ref, left_ref, block)

    steps = [
        (
            block + 1,
            functools.partial(
                own_score, left_ref, units_ref, block, mark_ref, best_ref, mirror_ref
            ),
        )
    ]
    for which in range(block):
        steps.append(scoring(which, 1, block, block + 1))
    mix(steps, unpacking[2:] + decoding(1))

    def both(turn, _):
        steps = [scoring(block, turn - 1, 0, block + 1)]
        for which in range(block):
            steps.append(scoring(which, turn, block, block + 1))
        mix(steps, decoding(turn))
        return 0

    lax.fori_loop(2, owners, both, 0)


def next_kernel(block, place_ref, codes_ref, *refs):
    table_refs, refs = refs[:3], refs[3:]
    units_refs, refs = refs[:block], refs[block:]
    units_ref, left_ref, mark_ref, best_ref, mirror_ref, code_ref, scale_ref = refs[-7:]
    block_kernel(
        block, place_ref[0, 0], codes_ref, table_refs, [*units_refs, units_ref],
        (left_ref, mark_ref, best_ref, mirror_ref, code_ref, scale_ref),
    )


def last_kernel(sizes, place_ref, codes_ref, *refs):
    capacity, clusters, members = sizes
    place = place_ref[0, 0]
    table_refs, refs = refs[:3], refs[3:]
    units_refs, refs = refs[:-12], refs[-8:]
    out_ref, left_ref, mark_ref, best_ref, mirror_ref, units_ref, code_ref, scale_ref = refs
    slots = left_ref.shape[0]
    groups = slots // COLS
    owners = units_ref.shape[1] // COLS
    block_kernel(
        groups - 1, place, codes_ref, table_refs, [*units_refs, units_ref],
        (left_ref, mark_ref, best_ref, mirror_ref, code_ref, scale_ref),
    )

    final = (owners - 1) * groups + groups - 1
    score(
        left_ref, slice(0, slots), units_ref, (owners - 1) * COLS, marks_of(mark_ref, final),
        best_ref,
    )

    half_rows = capacity // 2
    tiles = slots // LANES
    lane = lax.broadcasted_iota(jnp.int32, (tiles, LANES), 1)
    slot = lax.broadcasted_iota(jnp.int32, (tiles, LANES), 0) * LANES + lane
    source, within = slot // capacity, slot % capacity
    turn = place ^ (source % members)
    own_row = (turn * clusters + source // members) * half_rows + within % half_rows
    tile_of = 2 * (own_row // LANES) + within // half_rows
    result = jnp.zeros((tiles, LANES), jnp.float32)
    for tile in range(tiles):
        best = jnp.max(
            jnp.transpose(best_ref[tile * LANES : (tile + 1) * LANES, :]), axis=0, keepdims=True
        )
        best = jnp.maximum(best, mirror_ref[tile][0:1, :])
        mark = mark_ref[tile]
        best = jnp.where(mark[0:1, :] > 0, best, 0.0)
        result = jnp.where(
            tile_of == tile,
            take_lanes(jnp.broadcast_to(best, (tiles, LANES)), own_row % LANES),
            result,
        )
    out_ref[...] = result


def on_device(codes, routes, codebook, centroids):
    clusters = lax.axis_size("cluster")
    members = lax.axis_size("blk")
    devices = clusters * members
    subspaces, in_rows = codes.shape[2:]
    capacity = 2 * in_rows // devices
    half_rows = capacity // 2
    slots = devices * capacity
    tiles = slots // LANES
    groups = slots // COLS
    words, width = codebook.shape
    bf16, f32, i32 = jnp.bfloat16, jnp.float32, jnp.int32
    smem = pl.BlockSpec(memory_space=pltpu.SMEM)
    vmem = pl.BlockSpec(memory_space=pltpu.VMEM)

    anywhere = pl.BlockSpec(memory_space=pl.ANY)
    packed = pl.pallas_call(
        functools.partial(pack_kernel, devices, capacity),
        out_shape=jax.ShapeDtypeStruct((in_rows, 2 * subspaces), bf16),
        in_specs=[anywhere] * 2,
        out_specs=anywhere,
        scratch_shapes=[
            pltpu.VMEM((subspaces, in_rows), i32),
            pltpu.VMEM((1, in_rows), i32),
            pltpu.VMEM((in_rows, 2 * subspaces), bf16),
            pltpu.SemaphoreType.DMA((4,)),
        ],
        compiler_params=PACK_PARAMS,
        name="pack_rows",
    )(codes[0, 0], routes.reshape(1, in_rows))
    here = lax.all_to_all(packed, "cluster", split_axis=0, concat_axis=0, tiled=True)
    def from_member(block, mask):
        return lax.ppermute(block, "blk", [(i, i ^ mask) for i in range(members)])

    masks = range(1, members)
    blocks = {0: here}
    for mask in masks:
        if mask & (mask - 1) == 0:
            blocks[mask] = from_member(here, mask)

    place = lax.axis_index("blk").astype(i32).reshape(1, 1)
    group = lax.axis_index("cluster").astype(i32).reshape(1, 1)
    table = pl.pallas_call(
        table_kernel,
        out_shape=(
            jax.ShapeDtypeStruct((width, words), bf16),
            jax.ShapeDtypeStruct((width, LANES), f32),
            jax.ShapeDtypeStruct((subspaces, words), f32),
        ),
        in_specs=[smem, vmem],
        compiler_params=PARAMS,
        cost_estimate=pl.CostEstimate(
            flops=4 * words * width, bytes_accessed=6 * words * width, transcendentals=0
        ),
        name="word_table",
    )(group, jnp.concatenate([codebook, centroids], axis=0))

    units_shape = jax.ShapeDtypeStruct((width, members * COLS), bf16)
    state_shape = (
        jax.ShapeDtypeStruct((slots, width), bf16),
        jax.ShapeDtypeStruct((2 * members * groups, 8, LANES), f32),
        jax.ShapeDtypeStruct((slots, LANES), f32),
        jax.ShapeDtypeStruct((tiles, 8, LANES), f32),
    )

    def code_scratch(count):
        return [
            pltpu.VMEM((2 * members * count, subspaces, LANES), i32),
            pltpu.VMEM((2 * members * count, 8, LANES), f32),
        ]

    def cost(flops):
        return pl.CostEstimate(
            flops=flops, bytes_accessed=16 * slots * width, transcendentals=0
        )

    scores_flops = 2 * slots * members * slots * width
    def take_in(block, codes_in, units, state):
        kept = len(state)
        outs = pl.pallas_call(
            functools.partial(next_kernel, block),
            out_shape=(units_shape, *state_shape),
            in_specs=[smem] + [vmem] * (4 + block + kept),
            out_specs=(vmem,) * 5,
            scratch_shapes=code_scratch(1),
            input_output_aliases={5 + block + which: 1 + which for which in range(kept)},
            compiler_params=PARAMS,
            cost_estimate=cost(scores_flops // 4),
            name=f"rows_{block}",
        )(place, codes_in, *table, *units, *state)
        return [*units, outs[0]], outs[1:]

    whole_groups = half_rows == 16 and clusters * half_rows == LANES
    if whole_groups:
        units, state = take_in(0, here, [], ())
        units, state = take_in(1, blocks[1], units, state)
    for mask in masks:
        if mask not in blocks:
            low = mask & -mask
            block = blocks[mask - low]
            if whole_groups:
                left, marks, best, mirror = state
                block, marks = lax.optimization_barrier((block, marks))
                state = (left, marks, best, mirror)
            blocks[mask] = from_member(block, low)
    blocks = [here] + [blocks[mask] for mask in masks]
    if not whole_groups:
        every = jnp.stack(blocks).reshape(members, clusters, members, half_rows, LANES)
        every = every.transpose(2, 0, 1, 3, 4).reshape(members, groups, LANES // 16, 16, LANES)
        every = every.transpose(1, 2, 0, 3, 4).reshape(groups, members * LANES, LANES)
        blocks = list(every)
        units, state = take_in(0, blocks[0], [], ())
        units, state = take_in(1, blocks[1], units, state)
    for block in range(2, groups - 1):
        units, state = take_in(block, blocks[block], units, state)
    nearest, *_ = pl.pallas_call(
        functools.partial(last_kernel, (capacity, clusters, members)),
        out_shape=(jax.ShapeDtypeStruct((tiles, LANES), f32), *state_shape),
        in_specs=[smem] + [vmem] * (groups + 7),
        out_specs=(vmem,) * 5,
        scratch_shapes=[pltpu.VMEM((width, members * COLS), bf16)] + code_scratch(1),
        input_output_aliases={groups + 4 + which: 1 + which for which in range(4)},
        compiler_params=PARAMS,
        cost_estimate=cost(scores_flops),
        name="last_rows",
    )(place, blocks[groups - 1], *table, *units, *state)
    return nearest.reshape(1, 1, slots)


def solution(mesh):
    in_specs = (P("cluster", "blk", None, None), P("cluster", "blk", None, None), P(), P())
    out_specs = P("cluster", "blk", None)
    return jax.shard_map(
        on_device, mesh=mesh, in_specs=in_specs, out_specs=out_specs, check_vma=False
    )
```
